32 devices in a mesh: grp: 2 (over y), seq: 4 (over z), head: 4 (over x, core).
Axes of the slice: x: 2, y: 2, z: 4, core: 2. Of those that a mesh axis runs over, the one named last changes fastest.
Arguments:
- tokens: bfloat16 [1024, 2048], P(('grp', 'seq')), parts along dimension 0, may hold values from -6 to 6
- attn_weight: bfloat16 [4, 2048, 2048], P(None, 'seq', 'head'), may hold values from -0.125 to 0.125
- attn_gain: float32 [2048], replicated, may hold values from 0.25 to 1.75
- moe_gain: float32 [2048], replicated, may hold values from 0.25 to 1.75
- routes: int32 [1024, 8], P(('grp', 'seq')), parts along dimension 0, may hold values from 0 to 63, all different within a row; in each aligned block of 128 rows (0 to 127, 128 to 255, ...) at most 18 rows name the same one
- gates: float32 [1024, 8], P(('grp', 'seq')), parts along dimension 0, may hold values from 0.05 to 0.4
- expert_gate: bfloat16 [64, 2048, 1024], P('seq', None, 'head'), may hold values from -0.125 to 0.125
- expert_up: bfloat16 [64, 2048, 1024], P('seq', None, 'head'), may hold values from -0.125 to 0.125
- expert_down: bfloat16 [64, 1024, 2048], P('seq', 'head'), may hold values from -0.1875 to 0.1875
Outputs:
- mixed: bfloat16 [1024, 2048], P(('grp', 'seq')), parts along dimension 0
The draws below stay inside these ranges and needn't reach their ends.
There are 2 independent parts, one for each index of `grp`. The reference program is written for one: setup_inputs(seed, part) draws one part's arguments, and reference() takes and returns one part's arrays. A program takes and returns all parts, laid end to end along the dimension named above; an argument that names none is the same for every part. Nothing has to cross between parts.
Inputs may be any that keep to these rules, and one draw needn't show every extreme that they name: `routes`: in each aligned block of 128 tokens, no expert is named by more than 18 pairs of a token and a choice, a bound that some block reaches; a token's 8 experts differ.
All inputs are finite; a program needn't handle non-finite values.
Results may differ from the reference program's by a relative error of at most 0.015.
Values may be sent and summed in bfloat16 or wider, within the bound.
No kernel may reach another device: no remote copies, remote signals or barrier semaphores. Data moves between devices by JAX's collectives and lax.ppermute only.
A program may use at most 128 MiB of HBM per device.

```python
import math
import jax
import jax.numpy as jnp
import numpy as np
from jax import lax

D = 2048
HEADS = 16
HEAD_DIM = 128
EXPERTS = 64
FFE = 1024
TOPK = 8
TOK_DEV = 128
CAP = 18
TOKENS = 512
N_SEQ = 4
N_HEAD = 4


def levels(key, shape, cuts, smallest, top_value):
    def one(dim, blocks):
        heights = jax.random.uniform(jax.random.fold_in(jax.random.fold_in(key, 6), dim), (blocks,), jnp.float32, smallest / len(cuts), top_value / len(cuts))
        return jnp.repeat(jnp.exp(heights), shape[dim] // blocks).reshape((-1,) + (1,) * (len(shape) - dim - 1))

    level = one(*cuts[0])
    for cut in cuts[1:]:
        level = level * one(*cut)
    return level


def shared_out(stream_key, own, number, rows, amount, top, most, skew):
    ranking = jax.random.permutation(stream_key, amount)
    heavy_load, ordinary = shares(amount, rows * top, most, skew, True), shares(amount, rows * top, most, skew, False)
    places = jnp.arange(amount)

    def named(sizes, offset_by):
        used = int((sizes > 0).sum())
        fixed = max(1, used // 4)
        shifted = fixed + (places - fixed + offset_by * (used - fixed)) % max(1, amount - fixed)
        return jnp.zeros((amount,), jnp.int32).at[ranking[jnp.where(places < fixed, places, shifted)]].set(jnp.asarray(sizes, jnp.int32))

    sizes = jnp.where(number % 4 == 0, named(heavy_load, number // 4), named(ordinary, number - number // 4 - 1))
    mixed = jax.random.permutation(jax.random.fold_in(own, 3), amount)
    source_of, receiver = mixed[0:amount // 2 * 2:2], mixed[1:amount // 2 * 2:2]
    slack = jnp.minimum(sizes[source_of] - 1, most - sizes[receiver]) // 2
    slack = jnp.where((source_of == ranking[0]) | (receiver == ranking[0]) | (sizes[receiver] == 0), 0, jnp.maximum(slack, 0))
    shifted = jax.random.randint(jax.random.fold_in(own, 4), (amount // 2,), 0, 1 << 20) % (slack + 1)
    sizes = sizes.at[source_of].add(-shifted).at[receiver].add(shifted)
    members = jnp.searchsorted(jnp.cumsum(sizes), jnp.arange(rows * top), side="right").astype(jnp.int32)
    table = members.reshape(top, rows).T
    table = table[jax.random.permutation(jax.random.fold_in(own, 1), rows)]
    offset_by = jax.random.randint(jax.random.fold_in(own, 2), (rows, 1), 0, top)
    return jnp.take_along_axis(table, (jnp.arange(top)[None, :] + offset_by) % top, axis=1)


def shares(count, total, limit, slope, full):
    portions = [(1 << 20) // math.isqrt(rank ** slope) + 1 for rank in range(1, count + 1)]
    largest = limit if full else min(limit, max(-(-total // count), total * portions[0] // sum(portions)))
    least = 1 if total - largest >= count - 1 else 0
    counts, spare = [largest] + [least] * (count - 1), total - largest - least * (count - 1)
    while spare > 0:
        movable = [i for i in range(1, count) if counts[i] < largest] or [i for i in range(1, count) if counts[i] < limit]
        whole, budget = sum([portions[i] for i in movable]), spare
        for i in movable:
            extra = min(limit - counts[i], max(1, budget * portions[i] // whole), spare)
            counts[i] = counts[i] + extra
            spare = spare - extra
    return np.array(counts)


def bell_draw(stream_key, shape, spread, bound, split=(), kind=jnp.bfloat16):
    drawn = jax.random.normal(stream_key, shape, jnp.float32) * spread
    if len(split) > 0:
        drawn = levels(stream_key, shape, split, -0.22, 0.18) * drawn
    return jnp.clip(drawn, min=-bound, max=bound).astype(kind)


def setup_inputs(seed: int = 0, part: int = 0) -> dict:
    keys = jax.random.split(jax.random.key(seed), 10)
    part_splits = jax.random.split(jax.random.fold_in(keys[9], part), 10)
    tokens = bell_draw(part_splits[0], (TOKENS, D), 1.0, 6.0, ((0, 4),))
    attn_weight = bell_draw(keys[1], (4, D, HEADS * HEAD_DIM), D ** -0.5, 0.125, ((1, 4), (2, 4)))
    attn_gain = jnp.clip(1.0 + 0.15 * jax.random.normal(keys[2], (D,), jnp.float32), 0.25, 1.75)
    moe_gain = jnp.clip(1.0 + 0.15 * jax.random.normal(keys[3], (D,), jnp.float32), 0.25, 1.75)
    routes_keys = jax.random.split(jax.random.fold_in(part_splits[4], 1), TOKENS // TOK_DEV)
    routes_turns = jax.random.permutation(jax.random.fold_in(part_splits[4], 3), TOKENS // TOK_DEV)
    routes = jax.vmap(lambda own, number: shared_out(jax.random.fold_in(part_splits[4], 2), own, number, TOK_DEV, EXPERTS, TOPK, CAP, 2))(routes_keys, routes_turns).reshape((TOKENS, TOPK))
    gates = jnp.clip(0.05 + 0.35 * jax.random.uniform(part_splits[5], (TOKENS, TOPK), jnp.float32) ** levels(part_splits[5], (TOKENS, TOPK), ((0, 4),), -0.2, 0.2), 0.05, 0.4)
    expert_gate = bell_draw(keys[6], (EXPERTS, D, FFE), D ** -0.5, 0.125, ((0, 4), (2, 4)))
    expert_up = bell_draw(keys[7], (EXPERTS, D, FFE), D ** -0.5, 0.125, ((0, 4), (2, 4)))
    expert_down = bell_draw(keys[8], (EXPERTS, FFE, D), FFE ** -0.5, 0.1875, ((0, 4), (1, 4)))
    return dict(tokens=tokens, attn_weight=attn_weight, attn_gain=attn_gain, moe_gain=moe_gain, routes=routes, gates=gates, expert_gate=expert_gate, expert_up=expert_up, expert_down=expert_down)


PRECISE = lax.Precision.HIGHEST

def rms_scale(row_block, gain_vec):
    widened = row_block.astype(jnp.float32)
    factor = lax.rsqrt(lax.optimization_barrier(jnp.mean(widened * widened, axis=-1, keepdims=True)) + 1e-06)
    return widened * factor * gain_vec

def head_norm(outputs):
    return outputs * lax.rsqrt(lax.optimization_barrier(jnp.mean(outputs * outputs, axis=-1, keepdims=True)) + 1e-06)

def causal_linear(query_rows, key_rows, value_rows):
    block_count = query_rows.shape[0] // TOK_DEV
    shaped = [matrix.reshape(block_count, TOK_DEV, HEADS, HEAD_DIM).astype(jnp.float32) for matrix in (query_rows, key_rows, value_rows)]
    lower_mask = jnp.arange(TOK_DEV)[:, None] >= jnp.arange(TOK_DEV)[None, :]

    def advance(carry_state, block):
        query_blk, key_blk, value_blk = block
        inter_part = jnp.einsum('thd,hde->the', query_blk, carry_state, precision=PRECISE)
        scores = jnp.einsum('thd,shd->hts', query_blk, key_blk, precision=PRECISE)
        scores = jnp.where(lower_mask[None], scores, 0.0)
        intra_part = jnp.einsum('hts,she->the', scores, value_blk, precision=PRECISE)
        carry_state = carry_state + jnp.einsum('thd,the->hde', key_blk, value_blk, precision=PRECISE)
        return (carry_state, inter_part + intra_part)
    start_state = jnp.zeros((HEADS, HEAD_DIM, HEAD_DIM), jnp.float32)
    final_state, outputs = lax.scan(advance, start_state, tuple(shaped))
    return outputs.reshape(block_count * TOK_DEV, HEADS, HEAD_DIM)

def slot_numbers(route_rows):
    one_hot = (route_rows[..., None] == jnp.arange(EXPERTS, dtype=jnp.int32)).astype(jnp.int32)
    earlier = jnp.cumsum(one_hot, axis=-2) - one_hot
    return route_rows * CAP + lax.optimization_barrier(jnp.sum(earlier * one_hot, axis=-1))

def expert_apply(slot_rows, gate_mat, up_mat, down_mat):
    gate_val = jnp.dot(slot_rows, gate_mat, preferred_element_type=jnp.float32)
    up_val = jnp.dot(slot_rows, up_mat, preferred_element_type=jnp.float32)
    hidden = (jax.nn.silu(gate_val) * up_val).astype(jnp.bfloat16)
    grouped = hidden.reshape(-1, N_HEAD, FFE // N_HEAD).astype(jnp.float32)
    down_groups = down_mat.reshape(N_HEAD, FFE // N_HEAD, D).astype(jnp.float32)
    partial_value = jnp.einsum('rgf,gfd->rgd', grouped, down_groups, precision=PRECISE).astype(jnp.bfloat16)
    return lax.optimization_barrier(jnp.sum(partial_value.astype(jnp.float32), axis=1))

def reference(tokens, attn_weight, attn_gain, moe_gain, routes, gates, expert_gate, expert_up, expert_down):
    total_rows = tokens.shape[0]
    normed = rms_scale(tokens, attn_gain).astype(jnp.bfloat16)
    projected = [jnp.dot(normed, attn_weight[which], preferred_element_type=jnp.float32).astype(jnp.bfloat16) for which in range(3)]
    outputs = causal_linear(projected[0], projected[1], projected[2])
    attended = head_norm(outputs).reshape(total_rows, HEADS * HEAD_DIM).astype(jnp.bfloat16)
    out_proj = lax.dot_general(attended, attn_weight[3], (((1,), (1,)), ((), ())), preferred_element_type=jnp.float32)
    residual = (tokens.astype(jnp.float32) + out_proj).astype(jnp.bfloat16)
    moe_in = rms_scale(residual, moe_gain).astype(jnp.bfloat16)
    route_rows = routes.reshape(N_SEQ, TOK_DEV * TOPK)
    slots = slot_numbers(route_rows)
    token_ids = jnp.repeat(jnp.arange(total_rows, dtype=jnp.int32).reshape(N_SEQ, TOK_DEV), TOPK, axis=1)
    block_ids = jnp.broadcast_to(jnp.arange(N_SEQ, dtype=jnp.int32)[:, None], slots.shape)
    owner_table = jnp.full((N_SEQ, EXPERTS * CAP), total_rows, jnp.int32).at[block_ids, slots].set(token_ids)
    weight_table = jnp.zeros((N_SEQ, EXPERTS * CAP), jnp.float32).at[block_ids, slots].set(gates.reshape(N_SEQ, TOK_DEV * TOPK))
    padded_in = jnp.concatenate([moe_in, jnp.zeros((1, D), jnp.bfloat16)], axis=0)

    def one_expert(moe_sum, expert_id):
        picked = lax.dynamic_slice_in_dim(owner_table, expert_id * CAP, CAP, 1).reshape(-1)
        slot_gate = lax.dynamic_slice_in_dim(weight_table, expert_id * CAP, CAP, 1).reshape(-1)
        produced = expert_apply(padded_in[picked], expert_gate[expert_id], expert_up[expert_id], expert_down[expert_id])
        return (moe_sum.at[picked].add(slot_gate[:, None] * produced), None)
    start_sum = jnp.zeros((total_rows + 1, D), jnp.float32)
    moe_sum, unused = lax.scan(one_expert, start_sum, jnp.arange(EXPERTS, dtype=jnp.int32))
    return (residual.astype(jnp.float32) + moe_sum[:total_rows]).astype(jnp.bfloat16)
```

```python
import functools

import jax
import jax.numpy as jnp
from jax import lax
from jax.experimental import pallas as pl
from jax.experimental.pallas import tpu as pltpu
from jax.sharding import PartitionSpec as P

HEAD_DIM = 128
EXPERTS = 64
TOPK = 8
CAP = 18
EPS = 1e-06

PRECISE = lax.Precision.HIGHEST
BF16 = jnp.bfloat16
F32 = jnp.float32
ANY = pl.BlockSpec(memory_space=pl.ANY)
SMEM = pl.BlockSpec(memory_space=pltpu.SMEM)
VMEM = pl.BlockSpec(memory_space=pltpu.VMEM)
MIB = 1024 * 1024


def prefix_2(array, axis, combine, identity):
    peers, position = (lax.axis_size(axis), lax.axis_index(axis))
    everything = lax.all_gather(array.astype(jnp.bfloat16), axis)
    start = jnp.broadcast_to(jnp.asarray(identity, array.dtype), array.shape)

    def hop(k, before):
        reached = k < position
        new = combine(before, everything[k].astype(array.dtype))
        return jnp.where(reached, new, before)

    return lax.fori_loop(0, peers, hop, start)


def rms_scale(row_block, gain_vec):
    widened = row_block.astype(jnp.float32)
    factor = lax.rsqrt(jnp.mean(widened * widened, axis=-1, keepdims=True) + 1e-06)
    return widened * factor * gain_vec


def head_norm(outputs):
    return outputs * lax.rsqrt(jnp.mean(outputs * outputs, axis=-1, keepdims=True) + 1e-06)


def add_states(earlier, later):
    return earlier + later


def slot_numbers(route_flat):
    one_hot = (route_flat[:, None] == jnp.arange(EXPERTS, dtype=jnp.int32)[None, :]).astype(
        jnp.int32
    )
    earlier = jnp.cumsum(one_hot, axis=0) - one_hot
    return route_flat * CAP + jnp.sum(earlier * one_hot, axis=1)


def make_runner(expert_gate, expert_up, expert_down):

    def run_experts(received):
        gate_val = jnp.einsum(
            "necd,edf->necf", received, expert_gate, preferred_element_type=jnp.float32
        )
        up_val = jnp.einsum(
            "necd,edf->necf", received, expert_up, preferred_element_type=jnp.float32
        )
        hidden = (jax.nn.silu(gate_val) * up_val).astype(jnp.bfloat16)
        partial_value = jnp.einsum(
            "necf,efd->necd", hidden, expert_down, preferred_element_type=jnp.float32
        ).astype(jnp.bfloat16)
        groups = lax.axis_size("head")
        shape_now = partial_value.shape
        split = partial_value.reshape(
            shape_now[0], shape_now[1], shape_now[2], groups, shape_now[3] // groups
        )
        by_group = lax.all_to_all(split, "head", split_axis=3, concat_axis=3, tiled=True)
        summed = jnp.sum(by_group.astype(jnp.float32), axis=3)
        return lax.all_to_all(
            summed.astype(jnp.bfloat16), "seq", split_axis=0, concat_axis=0, tiled=True
        ).astype(summed.dtype)

    return run_experts


def general_body(
    tokens, attn_weight, attn_gain, moe_gain, routes, gates, expert_gate, expert_up, expert_down
):
    local_rows = tokens.shape[0]
    normed = rms_scale(tokens, attn_gain).astype(jnp.bfloat16)
    weights = lax.all_gather(attn_weight, "seq", axis=1, tiled=True)
    head_count = weights.shape[2] // HEAD_DIM
    projected = [
        jnp.dot(normed, weights[which], preferred_element_type=jnp.float32)
        .astype(jnp.bfloat16)
        .reshape(local_rows, head_count, HEAD_DIM)
        for which in range(3)
    ]
    query_rows, key_rows, value_rows = projected
    own_state = jnp.einsum("thd,the->hde", key_rows, value_rows, preferred_element_type=jnp.float32)
    prefix = prefix_2(own_state, "seq", add_states, jnp.zeros_like(own_state))
    inter_part = jnp.einsum(
        "thd,hde->the", query_rows.astype(jnp.float32), prefix, precision=PRECISE
    )
    scores = jnp.einsum("thd,shd->hts", query_rows, key_rows, preferred_element_type=jnp.float32)
    lower_mask = jnp.arange(local_rows)[:, None] >= jnp.arange(local_rows)[None, :]
    scores = jnp.where(lower_mask[None], scores, 0.0)
    intra_part = jnp.einsum(
        "hts,she->the", scores, value_rows.astype(jnp.float32), precision=PRECISE
    )
    attended = (
        head_norm(inter_part + intra_part)
        .reshape(local_rows, head_count * HEAD_DIM)
        .astype(jnp.bfloat16)
    )
    out_part = lax.dot_general(
        attended, weights[3], (((1,), (1,)), ((), ())), preferred_element_type=jnp.float32
    )
    residual = (
        tokens.astype(jnp.float32)
        + lax.psum(out_part.astype(jnp.bfloat16), "head").astype(jnp.float32)
    ).astype(jnp.bfloat16)
    moe_in = rms_scale(residual, moe_gain).astype(jnp.bfloat16)
    route_flat = routes.reshape(-1)
    slots = slot_numbers(route_flat)
    owners = lax.axis_size("seq")
    local_experts = expert_gate.shape[0]
    source_row = jnp.arange(route_flat.shape[0], dtype=jnp.int32) // TOPK
    run_experts = make_runner(expert_gate, expert_up, expert_down)
    outbound = (
        jnp.zeros((EXPERTS * CAP, moe_in.shape[1]), jnp.bfloat16).at[slots].set(moe_in[source_row])
    )
    outbound = outbound.reshape(owners, local_experts, CAP, moe_in.shape[1])
    returned = run_experts(lax.all_to_all(outbound, "seq", split_axis=0, concat_axis=0, tiled=True))
    arrived = returned.reshape(EXPERTS * CAP, -1)[slots].reshape(local_rows, TOPK, -1)
    moe_partial = jnp.einsum("tkd,tk->td", arrived, gates, precision=PRECISE)
    column_span = moe_partial.shape[1]
    residual_share = lax.dynamic_slice_in_dim(
        residual, lax.axis_index("head") * column_span, column_span, 1
    )
    mixed_share = (residual_share.astype(jnp.float32) + moe_partial).astype(jnp.bfloat16)
    return lax.all_gather(mixed_share, "head", axis=1, tiled=True)


def swap(array, axis, distance):
    size = lax.axis_size(axis)
    return lax.ppermute(array, axis, [(i, i ^ distance) for i in range(size)])


def run_copies(copies):
    for copy in copies:
        copy.start()
    for copy in copies:
        copy.wait()


def prep_kernel(n, pos, tokens, weight, x_send, w_own, *rest):
    w_sends, sems = rest[:-1], rest[-1]
    g, s, h = pos[0], pos[1], pos[2]
    rows, cols = x_send.shape
    depth, half = w_own.shape[0], w_sends[0].shape[0]
    copies = [
        (tokens.at[:, pl.ds(pl.multiple_of(h * cols, cols), cols)], x_send),
    ]
    for which in range(3):
        span = pl.ds(which * HEAD_DIM, HEAD_DIM)
        for distance, out in enumerate(w_sends, 1):
            column = pl.multiple_of((s ^ distance) * HEAD_DIM, HEAD_DIM)
            copies.append(
                (
                    weight.at[
                        which, pl.ds(pl.multiple_of(g * half, half), half), pl.ds(column, HEAD_DIM)
                    ],
                    out.at[:, span],
                )
            )
        column = pl.multiple_of(s * HEAD_DIM, HEAD_DIM)
        copies.append((weight.at[which, :, pl.ds(column, HEAD_DIM)], w_own.at[:, span]))
    run_copies([pltpu.make_async_copy(a, b, sems.at[i]) for i, (a, b) in enumerate(copies)])


def attend_kernel(n, pos, gain, tokens, w_own, *rest):
    x_pieces, rest = rest[:n], rest[n:]
    w_near, rest = rest[: n - 1], rest[n - 1 :]
    w_far, rest = rest[: n - 1], rest[n - 1 :]
    attended, x_share, x_all, w_all, sems = rest
    g, s, h = pos[0], pos[1], pos[2]
    rows, width = tokens.shape
    cols = width // n
    depth, half = w_own.shape[0], w_near[0].shape[0]
    total = n * rows

    def at_rows(block, size):
        return pl.ds(pl.multiple_of(block * size, size), size)

    copies = [(tokens, x_all.at[at_rows(s, rows)]), (w_own, w_all.at[at_rows(s, depth)])]
    for e in range(n):
        for d in range(1, n):
            copies.append(
                (x_pieces[e].at[d - 1], x_all.at[at_rows(s ^ d, rows), at_rows(h ^ e, cols)])
            )
    for d in range(1, n):
        copies.append((w_near[d - 1], w_all.at[at_rows((s ^ d) * 2 + g, half)]))
        copies.append((w_far[d - 1], w_all.at[at_rows((s ^ d) * 2 + (1 - g), half)]))
    run_copies([pltpu.make_async_copy(a, b, sems.at[i]) for i, (a, b) in enumerate(copies)])

    projected = []
    for block in range(n):
        wide = x_all[block * rows : (block + 1) * rows, :].astype(F32)
        factor = lax.rsqrt(jnp.mean(wide * wide, axis=-1, keepdims=True) + EPS)
        normed = (wide * factor * gain[...]).astype(BF16)
        projected.append(
            jnp.dot(normed, w_all[...], preferred_element_type=F32).astype(BF16)
        )
    whole = jnp.concatenate(projected, axis=0)
    query, key, value = (whole[:, i * HEAD_DIM : (i + 1) * HEAD_DIM] for i in range(3))
    for block in range(n):
        upto = (block + 1) * rows
        scores = lax.dot_general(
            query[block * rows : upto],
            key[:upto],
            (((1,), (1,)), ((), ())),
            preferred_element_type=F32,
        )
        ahead = lax.broadcasted_iota(jnp.int32, scores.shape, 0) + block * rows
        scores = jnp.where(ahead >= lax.broadcasted_iota(jnp.int32, scores.shape, 1), scores, 0.0)
        high = scores.astype(BF16)
        low = (scores - high.astype(F32)).astype(BF16)
        out = jnp.dot(high, value[:upto], preferred_element_type=F32) + jnp.dot(
            low, value[:upto], preferred_element_type=F32
        )
        out = out * lax.rsqrt(jnp.mean(out * out, axis=-1, keepdims=True) + EPS)
        attended[block] = out.astype(BF16)
    x_share[...] = x_all[at_rows(h, rows), at_rows(s, cols)]


def project_kernel(n, pos, x_share, w_own, w_others, *rest):
    pieces, (out, a_all, w_all, sems) = rest[:n], rest[n:]
    s, h = pos[1], pos[2]
    cols = w_own.shape[1]
    copies = []
    for e in range(n):
        source = w_own if e == 0 else w_others.at[e - 1]
        copies.append((source, w_all.at[:, pl.ds(pl.multiple_of((h ^ e) * cols, cols), cols)]))
        for d in range(n):
            head = (h ^ e) * n + (s ^ d)
            span = pl.ds(pl.multiple_of(head * HEAD_DIM, HEAD_DIM), HEAD_DIM)
            copies.append((pieces[d].at[e], a_all.at[:, span]))
    run_copies([pltpu.make_async_copy(a, b, sems.at[i]) for i, (a, b) in enumerate(copies)])
    product = lax.dot_general(
        a_all[...], w_all[...], (((1,), (1,)), ((), ())), preferred_element_type=F32
    )
    out[...] = (x_share[...].astype(F32) + product).astype(BF16)


def route_kernel(n, experts, slots, pos, own, *rest):
    others, (pick, place, weight, table, sems) = rest[: n - 1], rest[n - 1 :]
    s = pos[1]
    rows = own.shape[1]
    total = n * rows
    copies = []
    for d, piece in enumerate((own,) + tuple(others)):
        copies.append((piece, table.at[:, pl.ds(pl.multiple_of((s ^ d) * rows, rows), rows)]))
    run_copies([pltpu.make_async_copy(a, b, sems.at[i]) for i, (a, b) in enumerate(copies)])
    first = (s * experts).astype(F32)
    names = lax.broadcasted_iota(jnp.int32, (experts, total), 0).astype(F32) + first
    member = jnp.zeros((experts, total), F32)
    gate = jnp.zeros((experts, total), F32)
    for k in range(TOPK):
        hit = table[k : k + 1, :] == names
        member = jnp.where(hit, 1.0, member)
        gate = jnp.where(hit, table[TOPK + k : TOPK + k + 1, :], gate)
    earlier = (
        lax.broadcasted_iota(jnp.int32, (total, total), 0)
        < lax.broadcasted_iota(jnp.int32, (total, total), 1)
    ).astype(F32).astype(BF16)
    rank = jnp.dot(member.astype(BF16), earlier, preferred_element_type=F32)
    slot = jnp.where(member > 0.0, rank, -1.0).astype(BF16)
    pairs = experts * slots
    expand = (
        lax.broadcasted_iota(jnp.int32, (experts, pairs), 1) // slots
        == lax.broadcasted_iota(jnp.int32, (experts, pairs), 0)
    ).astype(F32).astype(BF16)
    across = lax.dot_general(
        slot, expand, (((0,), (0,)), ((), ())), preferred_element_type=F32
    )
    number = (lax.broadcasted_iota(jnp.int32, (total, pairs), 1) % slots).astype(F32)
    place[...] = jnp.where(across == number, 1.0, 0.0).astype(BF16)
    for e in range(experts):
        span = pl.ds(e * slots, slots)
        number = lax.broadcasted_iota(jnp.int32, (slots, total), 0).astype(F32)
        hit = number == slot[e : e + 1, :].astype(F32)
        pick[span, :] = jnp.where(hit, 1.0, 0.0).astype(BF16)
        chosen = jnp.sum(jnp.where(hit, gate[e : e + 1, :], 0.0), axis=1, keepdims=True)
        weight[span, :] = jnp.broadcast_to(chosen, (slots, weight.shape[1]))


def experts_kernel(
    n, pos, gain, r0, r1, r2, r3, pick, place, weight, w_gate, w_up, w_down,
    out, share, r_all, x_slots, y_slots, sems,
):
    s, h = pos[1], pos[2]
    step = pl.program_id(0)
    rows, cols = r0.shape[1:]
    slots = x_slots.shape[0] // pl.num_programs(0)

    def span(block, size):
        return pl.ds(pl.multiple_of(block * size, size), size)

    @pl.when(step == 0)
    def _():
        copies = []
        for e, piece in enumerate((r0, r1, r2, r3)):
            for d in range(n):
                copies.append((piece.at[d], r_all.at[span(h ^ e, rows), span(s ^ d, cols)]))
        run_copies([pltpu.make_async_copy(a, b, sems.at[i]) for i, (a, b) in enumerate(copies)])
        share[...] = r_all[span(s, rows), span(h, cols)]
        for block in range(n):
            where = slice(block * rows, (block + 1) * rows)
            wide = r_all[where, :].astype(F32)
            factor = lax.rsqrt(jnp.mean(wide * wide, axis=-1, keepdims=True) + EPS)
            r_all[where, :] = (wide * factor * gain[...]).astype(BF16)
        for block in range(n):
            where = slice(block * cols, (block + 1) * cols)
            x_slots[:, where] = jnp.dot(
                pick[...], r_all[:, where], preferred_element_type=F32
            ).astype(BF16)

    mine = span(step, slots)
    taken = x_slots[mine, :]
    gate_val = jnp.dot(taken, w_gate[0], preferred_element_type=F32)
    up_val = jnp.dot(taken, w_up[0], preferred_element_type=F32)
    scale = weight[mine, :1]
    hidden = (gate_val * jax.nn.sigmoid(gate_val) * up_val * scale).astype(BF16)
    y_slots[mine, :] = jnp.dot(hidden, w_down[0], preferred_element_type=F32).astype(BF16)

    @pl.when(step == pl.num_programs(0) - 1)
    def _():
        for e in range(n):
            out[e] = jnp.dot(
                place[...], y_slots[:, span(h ^ e, cols)], preferred_element_type=F32
            ).astype(BF16)


def square_body(
    n, tokens, attn_weight, attn_gain, moe_gain, routes, gates, expert_gate, expert_up, expert_down
):
    g, s, h = (lax.axis_index(axis) for axis in ("grp", "seq", "head"))
    pos = jnp.stack([g, s, h]).astype(jnp.int32)
    rows, width = tokens.shape
    cols = width // n
    depth = attn_weight.shape[1]
    half = depth // 2
    experts, _, hidden = expert_gate.shape
    total = n * rows
    slots = -(-n * CAP // 16) * 16
    sds = jax.ShapeDtypeStruct
    dma = pltpu.SemaphoreType.DMA

    with jax.named_scope("route_tables"):
        table = jnp.concatenate([routes.T.astype(F32), gates.T], axis=0)
        table_others = [swap(table, "seq", d) for d in range(1, n)]

    with jax.named_scope("cut_pieces"):
        x_send, w_own, *w_sends = pl.pallas_call(
            functools.partial(prep_kernel, n),
            out_shape=[sds((rows, cols), BF16), sds((depth, 3 * HEAD_DIM), BF16)]
            + [sds((half, 3 * HEAD_DIM), BF16)] * (n - 1),
            in_specs=[SMEM, ANY, ANY],
            out_specs=[ANY] * (n + 1),
            scratch_shapes=[dma((1 + 3 * n,))],
        )(pos, tokens, attn_weight)
    with jax.named_scope("gather_tokens"):
        x_near = jnp.stack([swap(x_send, "seq", d) for d in range(1, n)])
        x_pieces = {0: x_near}
        for stride in (2, 1):
            for e in list(x_pieces):
                x_pieces[e ^ stride] = swap(x_pieces[e], "head", stride)
    with jax.named_scope("gather_head_weights"):
        w_near = [swap(w_sends[d - 1], "seq", d) for d in range(1, n)]
        w_far = [swap(w, "grp", 1) for w in w_near]
    with jax.named_scope("gather_out_weights"):
        o_own = attn_weight[3]
        o_pieces = {0: o_own}
        for stride in (2, 1):
            for e in list(o_pieces):
                o_pieces[e ^ stride] = swap(o_pieces[e], "head", stride)
        o_others = jnp.stack([o_pieces[e] for e in range(1, n)])

    with jax.named_scope("routing"):
        pick, place, weight = pl.pallas_call(
            functools.partial(route_kernel, n, experts, slots),
            out_shape=[
                sds((experts * slots, total), BF16),
                sds((total, experts * slots), BF16),
                sds((experts * slots, 128), F32),
            ],
            in_specs=[SMEM] + [ANY] * n,
            out_specs=[VMEM] * 3,
            scratch_shapes=[pltpu.VMEM((2 * TOPK, total), F32), dma((n,))],
            compiler_params=pltpu.CompilerParams(vmem_limit_bytes=32 * MIB),
        )(pos, table, *table_others)

    with jax.named_scope("attention"):
        attended, x_share = pl.pallas_call(
            functools.partial(attend_kernel, n),
            out_shape=[sds((n, rows, HEAD_DIM), BF16), sds((rows, cols), BF16)],
            in_specs=[SMEM, VMEM] + [ANY] * (2 + n + 2 * (n - 1)),
            out_specs=[VMEM] * 2,
            scratch_shapes=[
                pltpu.VMEM((total, width), BF16),
                pltpu.VMEM((width, 3 * HEAD_DIM), BF16),
                dma((2 + n * (n - 1) + 2 * (n - 1),)),
            ],
            compiler_params=pltpu.CompilerParams(vmem_limit_bytes=32 * MIB),
        )(
            pos, attn_gain.reshape(1, width), tokens, w_own,
            *[x_pieces[e] for e in range(n)], *w_near, *w_far,
        )

    with jax.named_scope("heads_to_tokens"):
        by_block = [
            lax.dynamic_index_in_dim(attended, h ^ e, 0, keepdims=False) for e in range(n)
        ]
        arrived = jnp.stack(
            [by_block[0]] + [swap(by_block[e], "head", e) for e in range(1, n)]
        )
        a_pieces = [arrived] + [swap(arrived, "seq", d) for d in range(1, n)]

    with jax.named_scope("output_projection"):
        residual = pl.pallas_call(
            functools.partial(project_kernel, n),
            out_shape=sds((rows, cols), BF16),
            in_specs=[SMEM, VMEM] + [ANY] * (2 + n),
            out_specs=VMEM,
            scratch_shapes=[
                pltpu.VMEM((rows, width), BF16),
                pltpu.VMEM((depth, width), BF16),
                dma((n + n * n,)),
            ],
            compiler_params=pltpu.CompilerParams(vmem_limit_bytes=32 * MIB),
        )(pos, x_share, o_own, o_others, *a_pieces)

    with jax.named_scope("gather_residual"):
        r_near = jnp.stack([residual] + [swap(residual, "seq", d) for d in range(1, n)])
        r_pieces = {0: r_near}
        for stride in (2, 1):
            for e in list(r_pieces):
                r_pieces[e ^ stride] = swap(r_pieces[e], "head", stride)

    with jax.named_scope("experts"):
        full = lambda *shape: pl.BlockSpec(shape, lambda e: (0,) * len(shape))
        out, r_share = pl.pallas_call(
            functools.partial(experts_kernel, n),
            grid=(experts,),
            out_shape=[sds((n, total, cols), BF16), sds((rows, cols), BF16)],
            in_specs=[SMEM, full(1, width)]
            + [ANY] * n
            + [
                full(experts * slots, total),
                full(total, experts * slots),
                full(experts * slots, 128),
                pl.BlockSpec((1, width, hidden), lambda e: (e, 0, 0)),
                pl.BlockSpec((1, width, hidden), lambda e: (e, 0, 0)),
                pl.BlockSpec((1, hidden, width), lambda e: (e, 0, 0)),
            ],
            out_specs=[full(n, total, cols), full(rows, cols)],
            scratch_shapes=[
                pltpu.VMEM((total, width), BF16),
                pltpu.VMEM((experts * slots, width), BF16),
                pltpu.VMEM((experts * slots, width), BF16),
                dma((n * n,)),
            ],
            compiler_params=pltpu.CompilerParams(vmem_limit_bytes=52 * MIB),
        )(
            pos, moe_gain.reshape(1, width), *[r_pieces[e] for e in range(n)],
            pick, place, weight, expert_gate, expert_up, expert_down,
        )

    def plus(a, b):
        return (a.astype(F32) + b.astype(F32)).astype(BF16)

    with jax.named_scope("sum_over_head"):
        parts = {e: out[e] for e in range(n)}
        for stride in (1, 2):
            parts = {
                e: plus(parts[e], swap(parts[e ^ stride], "head", stride))
                for e in parts
                if not e & stride
            }
        summed = parts[0].reshape(n, rows, cols)
    with jax.named_scope("sum_over_seq"):
        blocks = [lax.dynamic_index_in_dim(summed, s ^ d, 0, keepdims=False) for d in range(n)]
        mixed = r_share.astype(F32) + blocks[0].astype(F32)
        for d in range(1, n):
            mixed = mixed + swap(blocks[d], "seq", d).astype(F32)
        mixed = mixed.astype(BF16)
    with jax.named_scope("gather_columns"):
        return lax.all_gather(mixed, "head", axis=1, tiled=True)


def solution(mesh):
    sizes = dict(mesh.shape)
    n = sizes["seq"]

    def body(tokens, attn_weight, *rest):
        width = tokens.shape[1]
        square = (
            n == sizes["head"]
            and n == 4
            and sizes["grp"] == 2
            and width == n * attn_weight.shape[1] == n * attn_weight.shape[2]
            and width == n * n * HEAD_DIM
        )
        if square:
            return square_body(n, tokens, attn_weight, *rest)
        return general_body(tokens, attn_weight, *rest)

    return jax.shard_map(
        body,
        mesh=mesh,
        in_specs=(
            P(("grp", "seq"), None),
            P(None, "seq", "head"),
            P(),
            P(),
            P(("grp", "seq"), None),
            P(("grp", "seq"), None),
            P("seq", None, "head"),
            P("seq", None, "head"),
            P("seq", "head", None),
        ),
        out_specs=P(("grp", "seq"), None),
        check_vma=False,
    )
```

```python
import functools

import jax
import jax.numpy as jnp
from jax import lax
from jax.experimental import pallas as pl
from jax.experimental.pallas import tpu as pltpu
from jax.sharding import PartitionSpec as P

HEAD_DIM = 128
EXPERTS = 64
TOPK = 8
CAP = 18
EPS = 1e-06

PRECISE = lax.Precision.HIGHEST
BF16 = jnp.bfloat16
F32 = jnp.float32
ANY = pl.BlockSpec(memory_space=pl.ANY)
SMEM = pl.BlockSpec(memory_space=pltpu.SMEM)
VMEM = pl.BlockSpec(memory_space=pltpu.VMEM)
MIB = 1024 * 1024


def prefix_2(array, axis, combine, identity):
    peers, position = (lax.axis_size(axis), lax.axis_index(axis))
    everything = lax.all_gather(array.astype(jnp.bfloat16), axis)
    start = jnp.broadcast_to(jnp.asarray(identity, array.dtype), array.shape)

    def hop(k, before):
        reached = k < position
        new = combine(before, everything[k].astype(array.dtype))
        return jnp.where(reached, new, before)

    return lax.fori_loop(0, peers, hop, start)


def rms_scale(row_block, gain_vec):
    widened = row_block.astype(jnp.float32)
    factor = lax.rsqrt(jnp.mean(widened * widened, axis=-1, keepdims=True) + 1e-06)
    return widened * factor * gain_vec


def head_norm(outputs):
    return outputs * lax.rsqrt(jnp.mean(outputs * outputs, axis=-1, keepdims=True) + 1e-06)


def add_states(earlier, later):
    return earlier + later


def slot_numbers(route_flat):
    one_hot = (route_flat[:, None] == jnp.arange(EXPERTS, dtype=jnp.int32)[None, :]).astype(
        jnp.int32
    )
    earlier = jnp.cumsum(one_hot, axis=0) - one_hot
    return route_flat * CAP + jnp.sum(earlier * one_hot, axis=1)


def make_runner(expert_gate, expert_up, expert_down):

    def run_experts(received):
        gate_val = jnp.einsum(
            "necd,edf->necf", received, expert_gate, preferred_element_type=jnp.float32
        )
        up_val = jnp.einsum(
            "necd,edf->necf", received, expert_up, preferred_element_type=jnp.float32
        )
        hidden = (jax.nn.silu(gate_val) * up_val).astype(jnp.bfloat16)
        partial_value = jnp.einsum(
            "necf,efd->necd", hidden, expert_down, preferred_element_type=jnp.float32
        ).astype(jnp.bfloat16)
        groups = lax.axis_size("head")
        shape_now = partial_value.shape
        split = partial_value.reshape(
            shape_now[0], shape_now[1], shape_now[2], groups, shape_now[3] // groups
        )
        by_group = lax.all_to_all(split, "head", split_axis=3, concat_axis=3, tiled=True)
        summed = jnp.sum(by_group.astype(jnp.float32), axis=3)
        return lax.all_to_all(
            summed.astype(jnp.bfloat16), "seq", split_axis=0, concat_axis=0, tiled=True
        ).astype(summed.dtype)

    return run_experts


def general_body(
    tokens, attn_weight, attn_gain, moe_gain, routes, gates, expert_gate, expert_up, expert_down
):
    local_rows = tokens.shape[0]
    normed = rms_scale(tokens, attn_gain).astype(jnp.bfloat16)
    weights = lax.all_gather(attn_weight, "seq", axis=1, tiled=True)
    head_count = weights.shape[2] // HEAD_DIM
    projected = [
        jnp.dot(normed, weights[which], preferred_element_type=jnp.float32)
        .astype(jnp.bfloat16)
        .reshape(local_rows, head_count, HEAD_DIM)
        for which in range(3)
    ]
    query_rows, key_rows, value_rows = projected
    own_state = jnp.einsum("thd,the->hde", key_rows, value_rows, preferred_element_type=jnp.float32)
    prefix = prefix_2(own_state, "seq", add_states, jnp.zeros_like(own_state))
    inter_part = jnp.einsum(
        "thd,hde->the", query_rows.astype(jnp.float32), prefix, precision=PRECISE
    )
    scores = jnp.einsum("thd,shd->hts", query_rows, key_rows, preferred_element_type=jnp.float32)
    lower_mask = jnp.arange(local_rows)[:, None] >= jnp.arange(local_rows)[None, :]
    scores = jnp.where(lower_mask[None], scores, 0.0)
    intra_part = jnp.einsum(
        "hts,she->the", scores, value_rows.astype(jnp.float32), precision=PRECISE
    )
    attended = (
        head_norm(inter_part + intra_part)
        .reshape(local_rows, head_count * HEAD_DIM)
        .astype(jnp.bfloat16)
    )
    out_part = lax.dot_general(
        attended, weights[3], (((1,), (1,)), ((), ())), preferred_element_type=jnp.float32
    )
    residual = (
        tokens.astype(jnp.float32)
        + lax.psum(out_part.astype(jnp.bfloat16), "head").astype(jnp.float32)
    ).astype(jnp.bfloat16)
    moe_in = rms_scale(residual, moe_gain).astype(jnp.bfloat16)
    route_flat = routes.reshape(-1)
    slots = slot_numbers(route_flat)
    owners = lax.axis_size("seq")
    local_experts = expert_gate.shape[0]
    source_row = jnp.arange(route_flat.shape[0], dtype=jnp.int32) // TOPK
    run_experts = make_runner(expert_gate, expert_up, expert_down)
    outbound = (
        jnp.zeros((EXPERTS * CAP, moe_in.shape[1]), jnp.bfloat16).at[slots].set(moe_in[source_row])
    )
    outbound = outbound.reshape(owners, local_experts, CAP, moe_in.shape[1])
    returned = run_experts(lax.all_to_all(outbound, "seq", split_axis=0, concat_axis=0, tiled=True))
    arrived = returned.reshape(EXPERTS * CAP, -1)[slots].reshape(local_rows, TOPK, -1)
    moe_partial = jnp.einsum("tkd,tk->td", arrived, gates, precision=PRECISE)
    column_span = moe_partial.shape[1]
    residual_share = lax.dynamic_slice_in_dim(
        residual, lax.axis_index("head") * column_span, column_span, 1
    )
    mixed_share = (residual_share.astype(jnp.float32) + moe_partial).astype(jnp.bfloat16)
    return lax.all_gather(mixed_share, "head", axis=1, tiled=True)


def swap(array, axis, distance):
    size = lax.axis_size(axis)
    return lax.ppermute(array, axis, [(i, i ^ distance) for i in range(size)])


def run_copies(copies):
    for copy in copies:
        copy.start()
    for copy in copies:
        copy.wait()


def after(array, *earlier):
    return lax.optimization_barrier((array,) + earlier)[0]


def cut_kernel(pos, tokens, weight, x_send, w_own, *rest):
    w_sends, sems = rest[:-1], rest[-1]
    g, s, h = pos[0], pos[1], pos[2]
    cols, half = x_send.shape[1], w_sends[0].shape[0]
    copies = [
        (tokens.at[:, pl.ds(pl.multiple_of(h * cols, cols), cols)], x_send),
    ]
    for which in range(3):
        span = pl.ds(which * HEAD_DIM, HEAD_DIM)
        for distance, out in enumerate(w_sends, 1):
            column = pl.multiple_of((s ^ distance) * HEAD_DIM, HEAD_DIM)
            own_half = pl.ds(pl.multiple_of(g * half, half), half)
            copies.append(
                (weight.at[which, own_half, pl.ds(column, HEAD_DIM)], out.at[:, span])
            )
        column = pl.multiple_of(s * HEAD_DIM, HEAD_DIM)
        copies.append((weight.at[which, :, pl.ds(column, HEAD_DIM)], w_own.at[:, span]))
    run_copies([pltpu.make_async_copy(a, b, sems.at[i]) for i, (a, b) in enumerate(copies)])


def attend_kernel(n, pos, gain, tokens, w_own, *rest):
    x_pieces, rest = rest[:n], rest[n:]
    w_near, rest = rest[: n - 1], rest[n - 1 :]
    w_far, rest = rest[: n - 1], rest[n - 1 :]
    attended, x_share, x_all, w_all, sems = rest
    g, s, h = pos[0], pos[1], pos[2]
    rows, width = tokens.shape
    cols = width // n
    depth, half = w_own.shape[0], w_near[0].shape[0]
    total = n * rows

    def at_rows(block, size):
        return pl.ds(pl.multiple_of(block * size, size), size)

    copies = [(tokens, x_all.at[at_rows(s, rows)]), (w_own, w_all.at[at_rows(s, depth)])]
    for e in range(n):
        for d in range(1, n):
            copies.append(
                (x_pieces[e].at[d - 1], x_all.at[at_rows(s ^ d, rows), at_rows(h ^ e, cols)])
            )
    for d in range(1, n):
        copies.append((w_near[d - 1], w_all.at[at_rows((s ^ d) * 2 + g, half)]))
        copies.append((w_far[d - 1], w_all.at[at_rows((s ^ d) * 2 + (1 - g), half)]))
    run_copies([pltpu.make_async_copy(a, b, sems.at[i]) for i, (a, b) in enumerate(copies)])

    projected = []
    for block in range(n):
        wide = x_all[block * rows : (block + 1) * rows, :].astype(F32)
        factor = lax.rsqrt(jnp.mean(wide * wide, axis=-1, keepdims=True) + EPS)
        normed = (wide * factor * gain[...]).astype(BF16)
        projected.append(
            jnp.dot(normed, w_all[...], preferred_element_type=F32).astype(BF16)
        )
    whole = jnp.concatenate(projected, axis=0)
    query, key, value = (whole[:, i * HEAD_DIM : (i + 1) * HEAD_DIM] for i in range(3))
    for block in range(n):
        upto = (block + 1) * rows
        scores = lax.dot_general(
            query[block * rows : upto],
            key[:upto],
            (((1,), (1,)), ((), ())),
            preferred_element_type=F32,
        )
        ahead = lax.broadcasted_iota(jnp.int32, scores.shape, 0) + block * rows
        scores = jnp.where(ahead >= lax.broadcasted_iota(jnp.int32, scores.shape, 1), scores, 0.0)
        high = scores.astype(BF16)
        low = (scores - high.astype(F32)).astype(BF16)
        out = jnp.dot(high, value[:upto], preferred_element_type=F32) + jnp.dot(
            low, value[:upto], preferred_element_type=F32
        )
        out = out * lax.rsqrt(jnp.mean(out * out, axis=-1, keepdims=True) + EPS)
        attended[block] = out.astype(BF16)
    x_share[...] = x_all[at_rows(h, rows), at_rows(s, cols)]


def project_kernel(n, pos, x_share, *rest):
    weights, pieces, (out, a_all, w_all, sems) = rest[:n], rest[n : 2 * n], rest[2 * n :]
    s, h = pos[1], pos[2]
    cols = weights[0].shape[1]
    copies = []
    for e in range(n):
        copies.append((weights[e], w_all.at[:, pl.ds(pl.multiple_of((h ^ e) * cols, cols), cols)]))
        for d in range(n):
            head = (h ^ e) * n + (s ^ d)
            span = pl.ds(pl.multiple_of(head * HEAD_DIM, HEAD_DIM), HEAD_DIM)
            copies.append((pieces[d].at[e], a_all.at[:, span]))
    run_copies([pltpu.make_async_copy(a, b, sems.at[i]) for i, (a, b) in enumerate(copies)])
    product = lax.dot_general(
        a_all[...], w_all[...], (((1,), (1,)), ((), ())), preferred_element_type=F32
    )
    out[...] = (x_share[...].astype(F32) + product).astype(BF16)


def route_kernel(n, experts, slots, pos, own, *rest):
    others, (pick, place, weight, table, sems) = rest[: n - 1], rest[n - 1 :]
    s = pos[1]
    rows = own.shape[1]
    total = n * rows
    copies = []
    for d, piece in enumerate((own,) + tuple(others)):
        copies.append((piece, table.at[:, pl.ds(pl.multiple_of((s ^ d) * rows, rows), rows)]))
    run_copies([pltpu.make_async_copy(a, b, sems.at[i]) for i, (a, b) in enumerate(copies)])
    first = (s * experts).astype(F32)
    names = lax.broadcasted_iota(jnp.int32, (experts, total), 0).astype(F32) + first
    member = jnp.zeros((experts, total), F32)
    gate = jnp.zeros((experts, total), F32)
    for k in range(TOPK):
        hit = table[k : k + 1, :] == names
        member = jnp.where(hit, 1.0, member)
        gate = jnp.where(hit, table[TOPK + k : TOPK + k + 1, :], gate)
    earlier = (
        lax.broadcasted_iota(jnp.int32, (total, total), 0)
        < lax.broadcasted_iota(jnp.int32, (total, total), 1)
    ).astype(F32).astype(BF16)
    rank = jnp.dot(member.astype(BF16), earlier, preferred_element_type=F32)
    slot = jnp.where(member > 0.0, rank, -1.0).astype(BF16)
    pairs = experts * slots
    expand = (
        lax.broadcasted_iota(jnp.int32, (experts, pairs), 1) // slots
        == lax.broadcasted_iota(jnp.int32, (experts, pairs), 0)
    ).astype(F32).astype(BF16)
    across = lax.dot_general(
        slot, expand, (((0,), (0,)), ((), ())), preferred_element_type=F32
    )
    number = (lax.broadcasted_iota(jnp.int32, (total, pairs), 1) % slots).astype(F32)
    place[...] = jnp.where(across == number, 1.0, 0.0).astype(BF16)
    for e in range(experts):
        span = pl.ds(e * slots, slots)
        number = lax.broadcasted_iota(jnp.int32, (slots, total), 0).astype(F32)
        hit = number == slot[e : e + 1, :].astype(F32)
        pick[span, :] = jnp.where(hit, 1.0, 0.0).astype(BF16)
        chosen = jnp.sum(jnp.where(hit, gate[e : e + 1, :], 0.0), axis=1, keepdims=True)
        weight[span, :] = jnp.broadcast_to(chosen, (slots, weight.shape[1]))


def hidden_kernel(n, slots, group, first, last, pos, *refs):
    refs = list(refs)
    gain = refs.pop(0)
    pieces = [refs.pop(0) for _ in range(n)]
    pick, w_gate, w_up = (refs.pop(0) for _ in range(3))
    if not first:
        total_in, square_in = refs.pop(0), refs.pop(0)
    if last:
        weight, hidden_out, r_all = refs
    else:
        total_out, square_out, r_all = refs
    h = pos[2]
    rows = pieces[0].shape[0]
    hidden = w_gate.shape[2]

    @pl.when(pl.program_id(0) == 0)
    def _():
        for e in range(n):
            r_all[pl.ds(pl.multiple_of((h ^ e) * rows, rows), rows), :] = pieces[e][...]

    taken = jnp.dot(pick[...], r_all[...], preferred_element_type=F32)
    square = jnp.sum(taken * taken, axis=1, keepdims=True)
    if not first:
        square = square + square_in[:, :1]
    scaled = (taken * gain[...]).astype(BF16)
    for e in range(group):
        span = slice(e * slots, (e + 1) * slots)
        gate_val = jnp.dot(scaled[span], w_gate[e], preferred_element_type=F32)
        up_val = jnp.dot(scaled[span], w_up[e], preferred_element_type=F32)
        if not first:
            gate_val = gate_val + total_in[span, :hidden]
            up_val = up_val + total_in[span, hidden:]
        if last:
            width = n * r_all.shape[1]
            factor = lax.rsqrt(square[span] / width + EPS)
            gate_val, up_val = gate_val * factor, up_val * factor
            value = gate_val * jax.nn.sigmoid(gate_val) * (up_val * weight[span, :1])
            hidden_out[span, :] = value.astype(BF16)
        else:
            total_out[span, :hidden] = gate_val
            total_out[span, hidden:] = up_val
    if not last:
        square_out[...] = jnp.broadcast_to(square, square_out.shape)


def down_kernel(n, slots, group, pos, hidden, place, w_down, out, y_slots):
    step = pl.program_id(0)
    for e in range(group):
        product = jnp.dot(
            hidden[e * slots : (e + 1) * slots, :], w_down[e], preferred_element_type=F32
        )
        row = pl.multiple_of(step * group * slots, group * slots) + e * slots
        y_slots[pl.ds(pl.multiple_of(row, slots), slots), :] = product.astype(BF16)

    @pl.when(step == pl.num_programs(0) - 1)
    def _():
        out[...] = jnp.dot(place[...], y_slots[...], preferred_element_type=F32).astype(BF16)


def square_body(
    n, tokens, attn_weight, attn_gain, moe_gain, routes, gates, expert_gate, expert_up, expert_down
):
    g, s, h = (lax.axis_index(axis) for axis in ("grp", "seq", "head"))
    pos = jnp.stack([g, s, h]).astype(jnp.int32)
    rows, width = tokens.shape
    cols = width // n
    depth = attn_weight.shape[1]
    half = depth // 2
    experts, _, hidden = expert_gate.shape
    total = n * rows
    slots = -(-n * CAP // 16) * 16
    pairs = experts * slots
    sds = jax.ShapeDtypeStruct
    dma = pltpu.SemaphoreType.DMA
    grid_spec = functools.partial(pltpu.PrefetchScalarGridSpec, num_scalar_prefetch=1)

    def room(mib):
        return pltpu.CompilerParams(vmem_limit_bytes=mib * MIB)

    def whole(*shape):
        return pl.BlockSpec(shape, lambda step, pos: (0,) * len(shape))

    def plus(*terms):
        total_value = terms[0].astype(F32)
        for term in terms[1:]:
            total_value = total_value + term.astype(F32)
        return total_value

    with jax.named_scope("cut_pieces"):
        x_send, w_own, *w_sends = pl.pallas_call(
            cut_kernel,
            out_shape=[sds((rows, cols), BF16), sds((depth, 3 * HEAD_DIM), BF16)]
            + [sds((half, 3 * HEAD_DIM), BF16)] * (n - 1),
            in_specs=[SMEM, ANY, ANY],
            out_specs=[VMEM] * (n + 1),
            scratch_shapes=[dma((1 + 3 * n,))],
            compiler_params=room(8),
        )(pos, tokens, attn_weight)
    with jax.named_scope("gather_tokens"):
        x_far = [swap(x_send, "seq", d) for d in range(1, n)]
        x_pieces = {0: jnp.stack(x_far)}
        x_pieces[2] = swap(x_pieces[0], "head", 2)
        for e in (0, 2):
            x_pieces[e ^ 1] = swap(x_pieces[e], "head", 1)
    with jax.named_scope("gather_head_weights"):
        w_near = [swap(w_sends[0], "seq", 1)]
        w_near += [swap(after(w_sends[d - 1], *x_far), "seq", d) for d in range(2, n)]
        w_far = [swap(w, "grp", 1) for w in w_near]
    with jax.named_scope("route_tables"):
        table = jnp.concatenate([routes.T.astype(F32), gates.T], axis=0)
        table_others = [swap(table, "seq", d) for d in range(1, n)]
    with jax.named_scope("routing"):
        pick, place, weight = pl.pallas_call(
            functools.partial(route_kernel, n, experts, slots),
            out_shape=[sds((pairs, total), BF16), sds((total, pairs), BF16), sds((pairs, 128), F32)],
            in_specs=[SMEM] + [ANY] * n,
            out_specs=[VMEM] * 3,
            scratch_shapes=[pltpu.VMEM((2 * TOPK, total), F32), dma((n,))],
            compiler_params=room(16),
        )(pos, table, *table_others)
        w_near[0] = after(w_near[0], pick)
    with jax.named_scope("gather_out_weights"):
        o_pieces = {0: after(attn_weight, x_far[0])[3]}
        o_pieces[2] = swap(after(o_pieces[0], x_pieces[2]), "head", 2)
        for e in (0, 2):
            o_pieces[e ^ 1] = swap(o_pieces[e], "head", 1)

    with jax.named_scope("attention"):
        attended, x_share = pl.pallas_call(
            functools.partial(attend_kernel, n),
            out_shape=[sds((n, rows, HEAD_DIM), BF16), sds((rows, cols), BF16)],
            in_specs=[SMEM, VMEM] + [ANY] * (2 + n + 2 * (n - 1)),
            out_specs=[VMEM] * 2,
            scratch_shapes=[
                pltpu.VMEM((total, width), BF16),
                pltpu.VMEM((width, 3 * HEAD_DIM), BF16),
                dma((2 + n * (n - 1) + 2 * (n - 1),)),
            ],
            compiler_params=room(20),
        )(
            pos, attn_gain.reshape(1, width), tokens, w_own,
            *[x_pieces[e] for e in range(n)], *w_near, *w_far,
        )

    with jax.named_scope("heads_to_tokens"):
        by_block = [
            lax.dynamic_index_in_dim(attended, h ^ e, 0, keepdims=False) for e in range(n)
        ]
        arrived = jnp.stack([by_block[0]] + [swap(by_block[e], "head", e) for e in range(1, n)])
        a_pieces = [arrived] + [swap(arrived, "seq", d) for d in range(1, n)]

    with jax.named_scope("output_projection"):
        residual = pl.pallas_call(
            functools.partial(project_kernel, n),
            out_shape=sds((rows, cols), BF16),
            in_specs=[SMEM, VMEM] + [ANY] * (2 * n),
            out_specs=VMEM,
            scratch_shapes=[
                pltpu.VMEM((rows, width), BF16),
                pltpu.VMEM((depth, width), BF16),
                dma((n + n * n,)),
            ],
            compiler_params=room(12),
        )(pos, x_share, *[o_pieces[e] for e in range(n)], *a_pieces)

    with jax.named_scope("gather_residual"):
        r_pieces = []
        for d in range(n):
            r = {0: residual if d == 0 else swap(residual, "seq", d)}
            r[2] = swap(r[0], "head", 2)
            for e in (0, 2):
                r[e ^ 1] = swap(r[e], "head", 1)
            r_pieces.append(r)

    group = 4
    block = group * slots
    state = ()
    for d in range(n):
        first, last = d == 0, d == n - 1
        by_step = lambda size: pl.BlockSpec((block, size), lambda step, pos: (step, 0))

        def columns(step, pos, d=d):
            return (step, pos[1] ^ d, 0)

        totals = [by_step(2 * hidden), by_step(128)]
        with jax.named_scope(f"hidden_units_{d}"):
            state = pl.pallas_call(
                functools.partial(hidden_kernel, n, slots, group, first, last),
                out_shape=[sds((pairs, hidden), BF16)]
                if last
                else [sds((pairs, 2 * hidden), F32), sds((pairs, 128), F32)],
                grid_spec=grid_spec(
                    grid=(experts // group,),
                    in_specs=[pl.BlockSpec((1, cols), lambda step, pos, d=d: (0, pos[1] ^ d))]
                    + [whole(rows, cols)] * n
                    + [by_step(total)]
                    + [pl.BlockSpec((group, cols, hidden), columns)] * 2
                    + ([] if first else totals)
                    + ([by_step(128)] if last else []),
                    out_specs=[by_step(hidden)] if last else totals,
                    scratch_shapes=[pltpu.VMEM((total, cols), BF16)],
                ),
                compiler_params=room(16),
            )(
                pos, moe_gain.reshape(1, width), *[r_pieces[d][e] for e in range(n)],
                pick, expert_gate, expert_up, *state, *([weight] if last else []),
            )
    (units,) = state

    group_down = 8
    out = {}
    for e in (3, 2, 1, 0):
        with jax.named_scope(f"down_quarter_{e}"):
            out[e] = pl.pallas_call(
                functools.partial(down_kernel, n, slots, group_down),
                out_shape=sds((total, cols), BF16),
                grid_spec=grid_spec(
                    grid=(experts // group_down,),
                    in_specs=[
                        pl.BlockSpec((group_down * slots, hidden), lambda step, pos: (step, 0)),
                        whole(total, pairs),
                        pl.BlockSpec(
                            (group_down, hidden, cols),
                            lambda step, pos, e=e: (step, 0, pos[2] ^ e),
                        ),
                    ],
                    out_specs=whole(total, cols),
                    scratch_shapes=[pltpu.VMEM((pairs, cols), BF16)],
                ),
                compiler_params=room(16),
            )(pos, units, place, expert_down)

    def rows_of(array, d):
        return lax.dynamic_slice_in_dim(array, (s ^ d) * rows, rows, 0)

    with jax.named_scope("sum_over_devices"):
        from_core = {e: swap(out[e ^ 1], "head", 1) for e in (2, 0)}
        mixed = lax.select_n(s ^ h, *[r_pieces[d][d] for d in range(n)]).astype(F32)
        for d in (3, 2, 1, 0):
            near = plus(rows_of(out[2], d), rows_of(from_core[2], d)).astype(BF16)
            summed = plus(
                rows_of(out[0], d), rows_of(from_core[0], d), swap(near, "head", 2)
            )
            if d:
                summed = swap(summed.astype(BF16), "seq", d)
            mixed = mixed + summed
        mixed = mixed.astype(BF16)
    with jax.named_scope("gather_columns"):
        return lax.all_gather(mixed, "head", axis=1, tiled=True)


def solution(mesh):
    sizes = dict(mesh.shape)
    n = sizes["seq"]

    def body(tokens, attn_weight, *rest):
        width = tokens.shape[1]
        square = (
            n == sizes["head"]
            and n == 4
            and sizes["grp"] == 2
            and width == n * attn_weight.shape[1] == n * attn_weight.shape[2]
            and width == n * n * HEAD_DIM
        )
        if square:
            return square_body(n, tokens, attn_weight, *rest)
        return general_body(tokens, attn_weight, *rest)

    return jax.shard_map(
        body,
        mesh=mesh,
        in_specs=(
            P(("grp", "seq"), None),
            P(None, "seq", "head"),
            P(),
            P(),
            P(("grp", "seq"), None),
            P(("grp", "seq"), None),
            P("seq", None, "head"),
            P("seq", None, "head"),
            P("seq", "head", None),
        ),
        out_specs=P(("grp", "seq"), None),
        check_vma=False,
    )
```

```python
import functools

import jax
import jax.numpy as jnp
from jax import lax
from jax.experimental import pallas as pl
from jax.experimental.pallas import tpu as pltpu
from jax.sharding import PartitionSpec as P

HEAD_DIM = 128
EXPERTS = 64
TOPK = 8
CAP = 18
EPS = 1e-06

PRECISE = lax.Precision.HIGHEST
BF16 = jnp.bfloat16
F32 = jnp.float32
ANY = pl.BlockSpec(memory_space=pl.ANY)
SMEM = pl.BlockSpec(memory_space=pltpu.SMEM)
VMEM = pl.BlockSpec(memory_space=pltpu.VMEM)
MIB = 1024 * 1024


def prefix_2(array, axis, combine, identity):
    peers, position = (lax.axis_size(axis), lax.axis_index(axis))
    everything = lax.all_gather(array.astype(jnp.bfloat16), axis)
    start = jnp.broadcast_to(jnp.asarray(identity, array.dtype), array.shape)

    def hop(k, before):
        reached = k < position
        new = combine(before, everything[k].astype(array.dtype))
        return jnp.where(reached, new, before)

    return lax.fori_loop(0, peers, hop, start)


def rms_scale(row_block, gain_vec):
    widened = row_block.astype(jnp.float32)
    factor = lax.rsqrt(jnp.mean(widened * widened, axis=-1, keepdims=True) + 1e-06)
    return widened * factor * gain_vec


def head_norm(outputs):
    return outputs * lax.rsqrt(jnp.mean(outputs * outputs, axis=-1, keepdims=True) + 1e-06)


def add_states(earlier, later):
    return earlier + later


def slot_numbers(route_flat):
    one_hot = (route_flat[:, None] == jnp.arange(EXPERTS, dtype=jnp.int32)[None, :]).astype(
        jnp.int32
    )
    earlier = jnp.cumsum(one_hot, axis=0) - one_hot
    return route_flat * CAP + jnp.sum(earlier * one_hot, axis=1)


def make_runner(expert_gate, expert_up, expert_down):

    def run_experts(received):
        gate_val = jnp.einsum(
            "necd,edf->necf", received, expert_gate, preferred_element_type=jnp.float32
        )
        up_val = jnp.einsum(
            "necd,edf->necf", received, expert_up, preferred_element_type=jnp.float32
        )
        hidden = (jax.nn.silu(gate_val) * up_val).astype(jnp.bfloat16)
        partial_value = jnp.einsum(
            "necf,efd->necd", hidden, expert_down, preferred_element_type=jnp.float32
        ).astype(jnp.bfloat16)
        groups = lax.axis_size("head")
        shape_now = partial_value.shape
        split = partial_value.reshape(
            shape_now[0], shape_now[1], shape_now[2], groups, shape_now[3] // groups
        )
        by_group = lax.all_to_all(split, "head", split_axis=3, concat_axis=3, tiled=True)
        summed = jnp.sum(by_group.astype(jnp.float32), axis=3)
        return lax.all_to_all(
            summed.astype(jnp.bfloat16), "seq", split_axis=0, concat_axis=0, tiled=True
        ).astype(summed.dtype)

    return run_experts


def general_body(
    tokens, attn_weight, attn_gain, moe_gain, routes, gates, expert_gate, expert_up, expert_down
):
    local_rows = tokens.shape[0]
    normed = rms_scale(tokens, attn_gain).astype(jnp.bfloat16)
    weights = lax.all_gather(attn_weight, "seq", axis=1, tiled=True)
    head_count = weights.shape[2] // HEAD_DIM
    projected = [
        jnp.dot(normed, weights[which], preferred_element_type=jnp.float32)
        .astype(jnp.bfloat16)
        .reshape(local_rows, head_count, HEAD_DIM)
        for which in range(3)
    ]
    query_rows, key_rows, value_rows = projected
    own_state = jnp.einsum("thd,the->hde", key_rows, value_rows, preferred_element_type=jnp.float32)
    prefix = prefix_2(own_state, "seq", add_states, jnp.zeros_like(own_state))
    inter_part = jnp.einsum(
        "thd,hde->the", query_rows.astype(jnp.float32), prefix, precision=PRECISE
    )
    scores = jnp.einsum("thd,shd->hts", query_rows, key_rows, preferred_element_type=jnp.float32)
    lower_mask = jnp.arange(local_rows)[:, None] >= jnp.arange(local_rows)[None, :]
    scores = jnp.where(lower_mask[None], scores, 0.0)
    intra_part = jnp.einsum(
        "hts,she->the", scores, value_rows.astype(jnp.float32), precision=PRECISE
    )
    attended = (
        head_norm(inter_part + intra_part)
        .reshape(local_rows, head_count * HEAD_DIM)
        .astype(jnp.bfloat16)
    )
    out_part = lax.dot_general(
        attended, weights[3], (((1,), (1,)), ((), ())), preferred_element_type=jnp.float32
    )
    residual = (
        tokens.astype(jnp.float32)
        + lax.psum(out_part.astype(jnp.bfloat16), "head").astype(jnp.float32)
    ).astype(jnp.bfloat16)
    moe_in = rms_scale(residual, moe_gain).astype(jnp.bfloat16)
    route_flat = routes.reshape(-1)
    slots = slot_numbers(route_flat)
    owners = lax.axis_size("seq")
    local_experts = expert_gate.shape[0]
    source_row = jnp.arange(route_flat.shape[0], dtype=jnp.int32) // TOPK
    run_experts = make_runner(expert_gate, expert_up, expert_down)
    outbound = (
        jnp.zeros((EXPERTS * CAP, moe_in.shape[1]), jnp.bfloat16).at[slots].set(moe_in[source_row])
    )
    outbound = outbound.reshape(owners, local_experts, CAP, moe_in.shape[1])
    returned = run_experts(lax.all_to_all(outbound, "seq", split_axis=0, concat_axis=0, tiled=True))
    arrived = returned.reshape(EXPERTS * CAP, -1)[slots].reshape(local_rows, TOPK, -1)
    moe_partial = jnp.einsum("tkd,tk->td", arrived, gates, precision=PRECISE)
    column_span = moe_partial.shape[1]
    residual_share = lax.dynamic_slice_in_dim(
        residual, lax.axis_index("head") * column_span, column_span, 1
    )
    mixed_share = (residual_share.astype(jnp.float32) + moe_partial).astype(jnp.bfloat16)
    return lax.all_gather(mixed_share, "head", axis=1, tiled=True)


def swap(array, axis, distance):
    size = lax.axis_size(axis)
    return lax.ppermute(array, axis, [(i, i ^ distance) for i in range(size)])


def run_copies(copies):
    for copy in copies:
        copy.start()
    for copy in copies:
        copy.wait()


def after(array, *earlier):
    return lax.optimization_barrier((array,) + earlier)[0]


def held(array):
    return pltpu.with_memory_space_constraint(array, pltpu.HBM)


def cut_kernel(pos, routes, gates, tokens, weight, x_send, w_own, o_own, *rest):
    w_sends, sems = rest[:-1], rest[-1]
    g, s, h = pos[0], pos[1], pos[2]
    rows, cols, half = tokens.shape[0], x_send.shape[1], w_sends[0].shape[0]
    copies = [
        (
            tokens.at[:, pl.ds(pl.multiple_of(h * cols, cols), cols)],
            x_send.at[pl.ds(0, rows)],
        ),
        (weight.at[3], o_own),
    ]
    for which in range(3):
        span = pl.ds(which * HEAD_DIM, HEAD_DIM)
        for distance, out in enumerate(w_sends, 1):
            column = pl.multiple_of((s ^ distance) * HEAD_DIM, HEAD_DIM)
            own_half = pl.ds(pl.multiple_of(g * half, half), half)
            copies.append(
                (weight.at[which, own_half, pl.ds(column, HEAD_DIM)], out.at[:, span])
            )
        column = pl.multiple_of(s * HEAD_DIM, HEAD_DIM)
        copies.append((weight.at[which, :, pl.ds(column, HEAD_DIM)], w_own.at[:, span]))
    copies = [pltpu.make_async_copy(a, b, sems.at[i]) for i, (a, b) in enumerate(copies)]
    for copy in copies:
        copy.start()
    parts, left = [routes[...].astype(F32)], gates[...]
    for _ in range(3):
        parts.append(left.astype(BF16).astype(F32))
        left = left - parts[-1]
    lines = jnp.concatenate(parts, axis=1)
    lines = jnp.concatenate([lines, jnp.zeros_like(lines)], axis=0)
    blank = jnp.zeros((lines.shape[0], cols - lines.shape[1]), F32)
    if blank.shape[1]:
        lines = jnp.concatenate([lines, blank], axis=1)
    x_send[rows:, :] = lines.astype(BF16)
    for copy in copies:
        copy.wait()


def attend_kernel(n, pos, gain, tokens, w_own, *rest):
    x_pieces, rest = rest[:n], rest[n:]
    w_near, rest = rest[: n - 1], rest[n - 1 :]
    w_far, rest = rest[: n - 1], rest[n - 1 :]
    attended, x_share, x_all, w_all, sems = rest
    g, s, h = pos[0], pos[1], pos[2]
    rows, width = tokens.shape
    cols = width // n
    depth, half = w_own.shape[0], w_near[0].shape[0]
    total = n * rows

    def at_rows(block, size):
        return pl.ds(pl.multiple_of(block * size, size), size)

    copies = [(tokens, x_all.at[at_rows(s, rows)]), (w_own, w_all.at[at_rows(s, depth)])]
    for e in range(n):
        for d in range(1, n):
            copies.append(
                (x_pieces[e].at[d - 1], x_all.at[at_rows(s ^ d, rows), at_rows(h ^ e, cols)])
            )
    for d in range(1, n):
        copies.append((w_near[d - 1], w_all.at[at_rows((s ^ d) * 2 + g, half)]))
        copies.append((w_far[d - 1], w_all.at[at_rows((s ^ d) * 2 + (1 - g), half)]))
    run_copies([pltpu.make_async_copy(a, b, sems.at[i]) for i, (a, b) in enumerate(copies)])

    projected = []
    for block in range(n):
        wide = x_all[block * rows : (block + 1) * rows, :].astype(F32)
        factor = lax.rsqrt(jnp.mean(wide * wide, axis=-1, keepdims=True) + EPS)
        normed = (wide * factor * gain[...]).astype(BF16)
        projected.append(
            jnp.dot(normed, w_all[...], preferred_element_type=F32).astype(BF16)
        )
    whole = jnp.concatenate(projected, axis=0)
    query, key, value = (whole[:, i * HEAD_DIM : (i + 1) * HEAD_DIM] for i in range(3))
    for block in range(n):
        upto = (block + 1) * rows
        scores = lax.dot_general(
            query[block * rows : upto],
            key[:upto],
            (((1,), (1,)), ((), ())),
            preferred_element_type=F32,
        )
        ahead = lax.broadcasted_iota(jnp.int32, scores.shape, 0) + block * rows
        scores = jnp.where(ahead >= lax.broadcasted_iota(jnp.int32, scores.shape, 1), scores, 0.0)
        high = scores.astype(BF16)
        low = (scores - high.astype(F32)).astype(BF16)
        out = jnp.dot(high, value[:upto], preferred_element_type=F32) + jnp.dot(
            low, value[:upto], preferred_element_type=F32
        )
        out = out * lax.rsqrt(jnp.mean(out * out, axis=-1, keepdims=True) + EPS)
        attended[block] = out.astype(BF16)
    x_share[...] = x_all[at_rows(h, rows), at_rows(s, cols)]


def project_kernel(n, pos, x_share, *rest):
    weights, pieces, (out, a_all, w_all, sems) = rest[:n], rest[n : 2 * n], rest[2 * n :]
    s, h = pos[1], pos[2]
    cols = weights[0].shape[1]
    copies = []
    for e in range(n):
        copies.append((weights[e], w_all.at[:, pl.ds(pl.multiple_of((h ^ e) * cols, cols), cols)]))
        for d in range(n):
            head = (h ^ e) * n + (s ^ d)
            span = pl.ds(pl.multiple_of(head * HEAD_DIM, HEAD_DIM), HEAD_DIM)
            copies.append((pieces[d].at[e], a_all.at[:, span]))
    run_copies([pltpu.make_async_copy(a, b, sems.at[i]) for i, (a, b) in enumerate(copies)])
    product = lax.dot_general(
        a_all[...], w_all[...], (((1,), (1,)), ((), ())), preferred_element_type=F32
    )
    out[...] = (x_share[...].astype(F32) + product).astype(BF16)


def route_kernel(n, experts, slots, pos, *refs):
    pieces, (pick, place, weight, table) = refs[:n], refs[n:]
    s = pos[1]
    rows = pieces[0].shape[0] - 2 * TOPK
    total = n * rows
    for d in range(n):
        lines = pieces[d][rows:, :].astype(F32)[:TOPK]
        gate = sum(lines[:, (1 + i) * rows : (2 + i) * rows] for i in range(3))
        span = pl.ds(pl.multiple_of((s ^ d) * rows, rows), rows)
        table[:, span] = jnp.concatenate([lines[:, :rows], gate], axis=0)
    first = (s * experts).astype(F32)
    names = lax.broadcasted_iota(jnp.int32, (experts, total), 0).astype(F32) + first
    member = jnp.zeros((experts, total), F32)
    gate = jnp.zeros((experts, total), F32)
    for k in range(TOPK):
        hit = table[k : k + 1, :] == names
        member = jnp.where(hit, 1.0, member)
        gate = jnp.where(hit, table[TOPK + k : TOPK + k + 1, :], gate)
    earlier = (
        lax.broadcasted_iota(jnp.int32, (total, total), 0)
        < lax.broadcasted_iota(jnp.int32, (total, total), 1)
    ).astype(F32).astype(BF16)
    rank = jnp.dot(member.astype(BF16), earlier, preferred_element_type=F32)
    slot = jnp.where(member > 0.0, rank, -1.0).astype(BF16)
    pairs = experts * slots
    expand = (
        lax.broadcasted_iota(jnp.int32, (experts, pairs), 1) // slots
        == lax.broadcasted_iota(jnp.int32, (experts, pairs), 0)
    ).astype(F32).astype(BF16)
    across = lax.dot_general(
        slot, expand, (((0,), (0,)), ((), ())), preferred_element_type=F32
    )
    number = (lax.broadcasted_iota(jnp.int32, (total, pairs), 1) % slots).astype(F32)
    place[...] = jnp.where(across == number, 1.0, 0.0).astype(BF16)
    for e in range(experts):
        span = pl.ds(e * slots, slots)
        number = lax.broadcasted_iota(jnp.int32, (slots, total), 0).astype(F32)
        hit = number == slot[e : e + 1, :].astype(F32)
        pick[span, :] = jnp.where(hit, 1.0, 0.0).astype(BF16)
        chosen = jnp.sum(jnp.where(hit, gate[e : e + 1, :], 0.0), axis=1, keepdims=True)
        weight[span, :] = jnp.broadcast_to(chosen, (slots, weight.shape[1]))


def stream(n_parts, moves):
    parts = [
        [pltpu.make_async_copy(*refs, sem) for refs, sem in moves(i)] for i in range(n_parts)
    ]
    for part in parts:
        for copy in part:
            copy.start()

    def wait(i):
        for copy in parts[i]:
            copy.wait()

    return wait


def hidden_kernel(n, slots, group, distance, last, pos, gain, *refs):
    first = distance == 0
    refs = list(refs)
    pieces = [refs.pop(0) for _ in range(n)]
    pick, w_gate, w_up = (refs.pop(0) for _ in range(3))
    if not first:
        total_in, square_in = refs.pop(0), refs.pop(0)
    if last:
        weight, hidden_out, r_all, scaled, g_all, u_all, sems = refs
    else:
        total_out, square_out, r_all, scaled, g_all, u_all, sems = refs
    s, h = pos[1], pos[2]
    rows, cols = pieces[0].shape
    experts, _, hidden = g_all.shape
    column = pl.ds(pl.multiple_of((s ^ distance) * cols, cols), cols)

    def moves(i):
        part = pl.ds(i * group, group)
        return [
            ((w_gate.at[part, column, :], g_all.at[part]), sems.at[2 * i]),
            ((w_up.at[part, column, :], u_all.at[part]), sems.at[2 * i + 1]),
        ]

    wait = stream(experts // group, moves)
    for e in range(n):
        r_all[pl.ds(pl.multiple_of((h ^ e) * rows, rows), rows), :] = pieces[e][...]
    width = n * cols
    factor = []
    for i in range(experts // group):
        part = slice(i * group * slots, (i + 1) * group * slots)
        taken = jnp.dot(pick[part, :], r_all[...], preferred_element_type=F32)
        square = jnp.sum(taken * taken, axis=1, keepdims=True)
        if not first:
            square = square + square_in[part, :1]
        if last:
            factor.append(lax.rsqrt(square / width + EPS))
        else:
            square_out[part, :] = jnp.broadcast_to(square, (group * slots, square_out.shape[1]))
        scaled[part, :] = (taken * gain[:, column]).astype(BF16)
    for i in range(experts // group):
        wait(i)
        for e in range(i * group, (i + 1) * group):
            span = slice(e * slots, (e + 1) * slots)
            gate_val = jnp.dot(scaled[span, :], g_all[e], preferred_element_type=F32)
            up_val = jnp.dot(scaled[span, :], u_all[e], preferred_element_type=F32)
            if not first:
                gate_val = gate_val + total_in[span, :hidden]
                up_val = up_val + total_in[span, hidden:]
            if last:
                inner = (e - i * group) * slots
                scale = factor[i][inner : inner + slots]
                gate_val, up_val = gate_val * scale, up_val * scale
                value = gate_val * jax.nn.sigmoid(gate_val) * (up_val * weight[span, :1])
                hidden_out[span, :] = value.astype(BF16)
            else:
                total_out[span, :hidden] = gate_val
                total_out[span, hidden:] = up_val


def down_kernel(n, slots, group, distances, pos, hidden, place, w_down, *refs):
    outs, (d_all, y_slots, sems) = refs[: len(distances)], refs[len(distances) :]
    h = pos[2]
    _, experts, _, cols = d_all.shape
    parts = experts // group

    def moves(i):
        k, part = i // parts, pl.ds(i % parts * group, group)
        column = pl.ds(pl.multiple_of((h ^ distances[k]) * cols, cols), cols)
        return [((w_down.at[part, :, column], d_all.at[k, part]), sems.at[i])]

    wait = stream(len(distances) * parts, moves)
    for k in range(len(distances)):
        for i in range(parts):
            wait(k * parts + i)
            for e in range(i * group, (i + 1) * group):
                span = slice(e * slots, (e + 1) * slots)
                product = jnp.dot(hidden[span, :], d_all[k, e], preferred_element_type=F32)
                y_slots[span, :] = product.astype(BF16)
        outs[k][...] = jnp.dot(place[...], y_slots[...], preferred_element_type=F32).astype(BF16)


def square_body(
    n, tokens, attn_weight, attn_gain, moe_gain, routes, gates, expert_gate, expert_up, expert_down
):
    g, s, h = (lax.axis_index(axis) for axis in ("grp", "seq", "head"))
    pos = jnp.stack([g, s, h]).astype(jnp.int32)
    rows, width = tokens.shape
    cols = width // n
    depth = attn_weight.shape[1]
    half = depth // 2
    experts, _, hidden = expert_gate.shape
    total = n * rows
    slots = -(-n * CAP // 16) * 16
    pairs = experts * slots
    sds = jax.ShapeDtypeStruct
    dma = pltpu.SemaphoreType.DMA

    def room(mib):
        return pltpu.CompilerParams(vmem_limit_bytes=mib * MIB)

    def cost(macs, size):
        return pl.CostEstimate(flops=2 * macs, bytes_accessed=size, transcendentals=0)

    def plus(*terms):
        total_value = terms[0].astype(F32)
        for term in terms[1:]:
            total_value = total_value + term.astype(F32)
        return total_value

    lines = 2 * TOPK
    with jax.named_scope("cut_pieces"):
        x_send, w_own, o_own, *w_sends = pl.pallas_call(
            cut_kernel,
            out_shape=[
                sds((rows + lines, cols), BF16),
                sds((depth, 3 * HEAD_DIM), BF16),
                sds((depth, cols), BF16),
            ]
            + [sds((half, 3 * HEAD_DIM), BF16)] * (n - 1),
            in_specs=[SMEM, VMEM, VMEM, ANY, ANY],
            out_specs=[VMEM] * (n + 2),
            scratch_shapes=[dma((2 + 3 * n,))],
            compiler_params=room(8),
        )(pos, routes.T, gates.T, tokens, attn_weight)
    with jax.named_scope("gather_tokens_and_weights"):
        x_far = [swap(x_send, "seq", d) for d in range(1, n)]
        w_near = [swap(w_sends[d - 1], "seq", d) for d in range(1, n - 1)]
        o_pieces = {0: o_own, 2: swap(o_own, "head", 2)}
        w_near.append(swap(after(w_sends[-1], *x_far, *w_near), "seq", n - 1))
        w_far = [swap(w, "grp", 1) for w in w_near]
        x_pieces = {0: after(jnp.stack([x[:rows] for x in x_far]), o_pieces[2])}
        x_pieces[2] = swap(x_pieces[0], "head", 2)
        for pieces in (o_pieces, x_pieces):
            for e in (0, 2):
                pieces[e ^ 1] = swap(pieces[e], "head", 1)
    with jax.named_scope("routing"):
        pick, place, weight = pl.pallas_call(
            functools.partial(route_kernel, n, experts, slots),
            out_shape=[sds((pairs, total), BF16), sds((total, pairs), BF16), sds((pairs, 128), F32)],
            in_specs=[SMEM] + [VMEM] * n,
            out_specs=[VMEM] * 3,
            scratch_shapes=[pltpu.VMEM((2 * TOPK, total), F32)],
            compiler_params=room(16),
        )(pos, x_send, *x_far)
        w_near[-1] = after(w_near[-1], pick)

    with jax.named_scope("attention"):
        attended, x_share = pl.pallas_call(
            functools.partial(attend_kernel, n),
            out_shape=[sds((n, rows, HEAD_DIM), BF16), sds((rows, cols), BF16)],
            in_specs=[SMEM, VMEM] + [ANY] * (2 + n + 2 * (n - 1)),
            out_specs=[VMEM] * 2,
            scratch_shapes=[
                pltpu.VMEM((total, width), BF16),
                pltpu.VMEM((width, 3 * HEAD_DIM), BF16),
                dma((2 + n * (n - 1) + 2 * (n - 1),)),
            ],
            compiler_params=room(20),
        )(
            pos, attn_gain.reshape(1, width), tokens, w_own,
            *[x_pieces[e] for e in range(n)], *w_near, *w_far,
        )

    with jax.named_scope("heads_to_tokens"):
        by_block = [
            lax.dynamic_index_in_dim(attended, h ^ e, 0, keepdims=False) for e in range(n)
        ]
        arrived = jnp.stack([by_block[0]] + [swap(by_block[e], "head", e) for e in range(1, n)])
        a_pieces = [arrived] + [swap(arrived, "seq", d) for d in range(1, n)]

    with jax.named_scope("output_projection"):
        residual = pl.pallas_call(
            functools.partial(project_kernel, n),
            out_shape=sds((rows, cols), BF16),
            in_specs=[SMEM, VMEM] + [ANY] * (2 * n),
            out_specs=VMEM,
            scratch_shapes=[
                pltpu.VMEM((rows, width), BF16),
                pltpu.VMEM((depth, width), BF16),
                dma((n + n * n,)),
            ],
            compiler_params=room(12),
        )(pos, x_share, *[o_pieces[e] for e in range(n)], *a_pieces)

    with jax.named_scope("gather_residual"):
        r_pieces = []
        for d in range(n):
            r = {0: residual if d == 0 else swap(residual, "seq", d)}
            r[2] = swap(r[0], "head", 2)
            for e in (0, 2):
                r[e ^ 1] = swap(r[e], "head", 1)
            r_pieces.append(r)

    group = experts // 4
    state = ()
    for d in range(n):
        last = d == n - 1
        with jax.named_scope(f"hidden_units_{d}"):
            state = pl.pallas_call(
                functools.partial(hidden_kernel, n, slots, group, d, last),
                out_shape=[sds((pairs, hidden), BF16)]
                if last
                else [sds((pairs, 2 * hidden), F32), sds((pairs, 128), F32)],
                in_specs=[SMEM]
                + [VMEM] * (n + 2)
                + [ANY] * 2
                + [VMEM] * (len(state) + last),
                out_specs=[VMEM] * (2 - last),
                scratch_shapes=[
                    pltpu.VMEM((total, cols), BF16),
                    pltpu.VMEM((pairs, cols), BF16),
                    pltpu.VMEM((experts, cols, hidden), BF16),
                    pltpu.VMEM((experts, cols, hidden), BF16),
                    dma((2 * (experts // group),)),
                ],
                compiler_params=room(28),
                cost_estimate=cost(pairs * cols * (total + 2 * hidden), 4 * experts * cols * hidden),
            )(
                pos, moe_gain.reshape(1, width), *[r_pieces[d][e] for e in range(n)],
                pick, held(expert_gate), held(expert_up), *state, *([weight] if last else []),
            )
    (units,) = state

    out = {}
    for distances in ((3,), (2,), (1, 0)):
        with jax.named_scope("down_quarters_" + "_".join(map(str, distances))):
            outs = pl.pallas_call(
                functools.partial(down_kernel, n, slots, group, distances),
                out_shape=[sds((total, cols), BF16)] * len(distances),
                in_specs=[SMEM, VMEM, VMEM, ANY],
                out_specs=[VMEM] * len(distances),
                scratch_shapes=[
                    pltpu.VMEM((len(distances), experts, hidden, cols), BF16),
                    pltpu.VMEM((pairs, cols), BF16),
                    dma((len(distances) * (experts // group),)),
                ],
                compiler_params=room(24),
                cost_estimate=cost(
                    len(distances) * pairs * cols * (total + hidden),
                    2 * len(distances) * experts * cols * hidden,
                ),
            )(pos, units, place, held(expert_down))
            out.update(zip(distances, outs))

    def rows_of(array, d):
        return lax.dynamic_slice_in_dim(array, (s ^ d) * rows, rows, 0)

    with jax.named_scope("sum_over_devices"):
        from_core = {e: swap(out[e ^ 1], "head", 1) for e in (2, 0)}
        mixed = lax.select_n(s ^ h, *[r_pieces[d][d] for d in range(n)]).astype(F32)
        for d in (3, 2, 1, 0):
            near = plus(rows_of(out[2], d), rows_of(from_core[2], d)).astype(BF16)
            summed = plus(
                rows_of(out[0], d), rows_of(from_core[0], d), swap(near, "head", 2)
            )
            if d:
                summed = swap(summed.astype(BF16), "seq", d)
            mixed = mixed + summed
        mixed = mixed.astype(BF16)
    with jax.named_scope("gather_columns"):
        return lax.all_gather(mixed, "head", axis=1, tiled=True)


def solution(mesh):
    sizes = dict(mesh.shape)
    n = sizes["seq"]

    def body(tokens, attn_weight, *rest):
        width = tokens.shape[1]
        square = (
            n == sizes["head"]
            and n == 4
            and sizes["grp"] == 2
            and width == n * attn_weight.shape[1] == n * attn_weight.shape[2]
            and width == n * n * HEAD_DIM
        )
        if square:
            return square_body(n, tokens, attn_weight, *rest)
        return general_body(tokens, attn_weight, *rest)

    return jax.shard_map(
        body,
        mesh=mesh,
        in_specs=(
            P(("grp", "seq"), None),
            P(None, "seq", "head"),
            P(),
            P(),
            P(("grp", "seq"), None),
            P(("grp", "seq"), None),
            P("seq", None, "head"),
            P("seq", None, "head"),
            P("seq", "head", None),
        ),
        out_specs=P(("grp", "seq"), None),
        check_vma=False,
    )
```

```python
import functools

import jax
import jax.numpy as jnp
from jax import lax
from jax.experimental import pallas as pl
from jax.experimental.pallas import tpu as pltpu
from jax.sharding import PartitionSpec as P

HEAD_DIM = 128
EXPERTS = 64
TOPK = 8
CAP = 18
EPS = 1e-06

PRECISE = lax.Precision.HIGHEST
BF16 = jnp.bfloat16
F32 = jnp.float32
ANY = pl.BlockSpec(memory_space=pl.ANY)
SMEM = pl.BlockSpec(memory_space=pltpu.SMEM)
VMEM = pl.BlockSpec(memory_space=pltpu.VMEM)
MIB = 1024 * 1024
SLOW = 10**10


def prefix_2(array, axis, combine, identity):
    peers, position = (lax.axis_size(axis), lax.axis_index(axis))
    everything = lax.all_gather(array.astype(jnp.bfloat16), axis)
    start = jnp.broadcast_to(jnp.asarray(identity, array.dtype), array.shape)

    def hop(k, before):
        reached = k < position
        new = combine(before, everything[k].astype(array.dtype))
        return jnp.where(reached, new, before)

    return lax.fori_loop(0, peers, hop, start)


def rms_scale(row_block, gain_vec):
    widened = row_block.astype(jnp.float32)
    factor = lax.rsqrt(jnp.mean(widened * widened, axis=-1, keepdims=True) + 1e-06)
    return widened * factor * gain_vec


def head_norm(outputs):
    return outputs * lax.rsqrt(jnp.mean(outputs * outputs, axis=-1, keepdims=True) + 1e-06)


def add_states(earlier, later):
    return earlier + later


def slot_numbers(route_flat):
    one_hot = (route_flat[:, None] == jnp.arange(EXPERTS, dtype=jnp.int32)[None, :]).astype(
        jnp.int32
    )
    earlier = jnp.cumsum(one_hot, axis=0) - one_hot
    return route_flat * CAP + jnp.sum(earlier * one_hot, axis=1)


def make_runner(expert_gate, expert_up, expert_down):

    def run_experts(received):
        gate_val = jnp.einsum(
            "necd,edf->necf", received, expert_gate, preferred_element_type=jnp.float32
        )
        up_val = jnp.einsum(
            "necd,edf->necf", received, expert_up, preferred_element_type=jnp.float32
        )
        hidden = (jax.nn.silu(gate_val) * up_val).astype(jnp.bfloat16)
        partial_value = jnp.einsum(
            "necf,efd->necd", hidden, expert_down, preferred_element_type=jnp.float32
        ).astype(jnp.bfloat16)
        groups = lax.axis_size("head")
        shape_now = partial_value.shape
        split = partial_value.reshape(
            shape_now[0], shape_now[1], shape_now[2], groups, shape_now[3] // groups
        )
        by_group = lax.all_to_all(split, "head", split_axis=3, concat_axis=3, tiled=True)
        summed = jnp.sum(by_group.astype(jnp.float32), axis=3)
        return lax.all_to_all(
            summed.astype(jnp.bfloat16), "seq", split_axis=0, concat_axis=0, tiled=True
        ).astype(summed.dtype)

    return run_experts


def general_body(
    tokens, attn_weight, attn_gain, moe_gain, routes, gates, expert_gate, expert_up, expert_down
):
    local_rows = tokens.shape[0]
    normed = rms_scale(tokens, attn_gain).astype(jnp.bfloat16)
    weights = lax.all_gather(attn_weight, "seq", axis=1, tiled=True)
    head_count = weights.shape[2] // HEAD_DIM
    projected = [
        jnp.dot(normed, weights[which], preferred_element_type=jnp.float32)
        .astype(jnp.bfloat16)
        .reshape(local_rows, head_count, HEAD_DIM)
        for which in range(3)
    ]
    query_rows, key_rows, value_rows = projected
    own_state = jnp.einsum("thd,the->hde", key_rows, value_rows, preferred_element_type=jnp.float32)
    prefix = prefix_2(own_state, "seq", add_states, jnp.zeros_like(own_state))
    inter_part = jnp.einsum(
        "thd,hde->the", query_rows.astype(jnp.float32), prefix, precision=PRECISE
    )
    scores = jnp.einsum("thd,shd->hts", query_rows, key_rows, preferred_element_type=jnp.float32)
    lower_mask = jnp.arange(local_rows)[:, None] >= jnp.arange(local_rows)[None, :]
    scores = jnp.where(lower_mask[None], scores, 0.0)
    intra_part = jnp.einsum(
        "hts,she->the", scores, value_rows.astype(jnp.float32), precision=PRECISE
    )
    attended = (
        head_norm(inter_part + intra_part)
        .reshape(local_rows, head_count * HEAD_DIM)
        .astype(jnp.bfloat16)
    )
    out_part = lax.dot_general(
        attended, weights[3], (((1,), (1,)), ((), ())), preferred_element_type=jnp.float32
    )
    residual = (
        tokens.astype(jnp.float32)
        + lax.psum(out_part.astype(jnp.bfloat16), "head").astype(jnp.float32)
    ).astype(jnp.bfloat16)
    moe_in = rms_scale(residual, moe_gain).astype(jnp.bfloat16)
    route_flat = routes.reshape(-1)
    slots = slot_numbers(route_flat)
    owners = lax.axis_size("seq")
    local_experts = expert_gate.shape[0]
    source_row = jnp.arange(route_flat.shape[0], dtype=jnp.int32) // TOPK
    run_experts = make_runner(expert_gate, expert_up, expert_down)
    outbound = (
        jnp.zeros((EXPERTS * CAP, moe_in.shape[1]), jnp.bfloat16).at[slots].set(moe_in[source_row])
    )
    outbound = outbound.reshape(owners, local_experts, CAP, moe_in.shape[1])
    returned = run_experts(lax.all_to_all(outbound, "seq", split_axis=0, concat_axis=0, tiled=True))
    arrived = returned.reshape(EXPERTS * CAP, -1)[slots].reshape(local_rows, TOPK, -1)
    moe_partial = jnp.einsum("tkd,tk->td", arrived, gates, precision=PRECISE)
    column_span = moe_partial.shape[1]
    residual_share = lax.dynamic_slice_in_dim(
        residual, lax.axis_index("head") * column_span, column_span, 1
    )
    mixed_share = (residual_share.astype(jnp.float32) + moe_partial).astype(jnp.bfloat16)
    return lax.all_gather(mixed_share, "head", axis=1, tiled=True)


def swap(array, axis, distance):
    size = lax.axis_size(axis)
    return lax.ppermute(array, axis, [(i, i ^ distance) for i in range(size)])


def run_copies(copies):
    for copy in copies:
        copy.start()
    for copy in copies:
        copy.wait()


def after(array, *earlier):
    return lax.optimization_barrier((array,) + earlier)[0]


def held(array):
    return pltpu.with_memory_space_constraint(array, pltpu.HBM)


def in_step(*arrays):
    return lax.optimization_barrier(arrays)


def cut_kernel(pos, routes, gates, tokens, weight, x_send, w_own, o_own, *rest):
    w_sends, (r_here, g_here, sems) = rest[:-3], rest[-3:]
    g, s, h = pos[0], pos[1], pos[2]
    rows, cols, half = tokens.shape[0], x_send.shape[1], w_sends[0].shape[0]
    copies = [
        (
            tokens.at[:, pl.ds(pl.multiple_of(h * cols, cols), cols)],
            x_send.at[pl.ds(0, rows)],
        ),
        (weight.at[3], o_own),
        (routes, r_here),
        (gates, g_here),
    ]
    for which in range(3):
        span = pl.ds(which * HEAD_DIM, HEAD_DIM)
        for distance, out in enumerate(w_sends, 1):
            column = pl.multiple_of((s ^ distance) * HEAD_DIM, HEAD_DIM)
            own_half = pl.ds(pl.multiple_of(g * half, half), half)
            copies.append(
                (weight.at[which, own_half, pl.ds(column, HEAD_DIM)], out.at[:, span])
            )
        column = pl.multiple_of(s * HEAD_DIM, HEAD_DIM)
        copies.append((weight.at[which, :, pl.ds(column, HEAD_DIM)], w_own.at[:, span]))
    copies = [pltpu.make_async_copy(a, b, sems.at[i]) for i, (a, b) in enumerate(copies)]
    for copy in copies:
        copy.start()
    for copy in copies[2:4]:
        copy.wait()
    parts, left = [r_here[...].astype(F32)], g_here[...]
    for _ in range(3):
        parts.append(left.astype(BF16).astype(F32))
        left = left - parts[-1]
    lines = jnp.concatenate(parts, axis=1)
    lines = jnp.concatenate([lines, jnp.zeros_like(lines)], axis=0)
    blank = jnp.zeros((lines.shape[0], cols - lines.shape[1]), F32)
    if blank.shape[1]:
        lines = jnp.concatenate([lines, blank], axis=1)
    x_send[rows:, :] = lines.astype(BF16)
    for copy in copies[:2] + copies[4:]:
        copy.wait()


def attend_kernel(n, pos, gain, tokens, w_own, *rest):
    x_pieces, rest = rest[:n], rest[n:]
    w_near, rest = rest[: n - 1], rest[n - 1 :]
    w_far, rest = rest[: n - 1], rest[n - 1 :]
    attended, x_share, x_all, w_all, sems = rest
    g, s, h = pos[0], pos[1], pos[2]
    rows, width = tokens.shape
    cols = width // n
    depth, half = w_own.shape[0], w_near[0].shape[0]
    total = n * rows

    def at_rows(block, size):
        return pl.ds(pl.multiple_of(block * size, size), size)

    copies = [(tokens, x_all.at[at_rows(s, rows)])]
    for d in range(1, n):
        for e in range(n):
            copies.append(
                (x_pieces[e].at[d - 1], x_all.at[at_rows(s ^ d, rows), at_rows(h ^ e, cols)])
            )
    n_rows = len(copies)
    copies.append((w_own, w_all.at[at_rows(s, depth)]))
    for d in range(1, n):
        copies.append((w_near[d - 1], w_all.at[at_rows((s ^ d) * 2 + g, half)]))
        copies.append((w_far[d - 1], w_all.at[at_rows((s ^ d) * 2 + (1 - g), half)]))
    copies = [pltpu.make_async_copy(a, b, sems.at[i]) for i, (a, b) in enumerate(copies)]
    for copy in copies:
        copy.start()
    for copy in copies[:n_rows]:
        copy.wait()
    x_share[...] = x_all[at_rows(h, rows), at_rows(s, cols)]

    for block in range(n):
        wide = x_all[block * rows : (block + 1) * rows, :].astype(F32)
        factor = lax.rsqrt(jnp.mean(wide * wide, axis=-1, keepdims=True) + EPS)
        x_all[block * rows : (block + 1) * rows, :] = (wide * factor * gain[...]).astype(BF16)
    for copy in copies[n_rows:]:
        copy.wait()
    projected = [
        jnp.dot(
            x_all[block * rows : (block + 1) * rows, :], w_all[...], preferred_element_type=F32
        ).astype(BF16)
        for block in range(n)
    ]
    whole = jnp.concatenate(projected, axis=0)
    query, key, value = (whole[:, i * HEAD_DIM : (i + 1) * HEAD_DIM] for i in range(3))
    for block in range(n):
        upto = (block + 1) * rows
        scores = lax.dot_general(
            query[block * rows : upto],
            key[:upto],
            (((1,), (1,)), ((), ())),
            preferred_element_type=F32,
        )
        ahead = lax.broadcasted_iota(jnp.int32, scores.shape, 0) + block * rows
        scores = jnp.where(ahead >= lax.broadcasted_iota(jnp.int32, scores.shape, 1), scores, 0.0)
        high = scores.astype(BF16)
        low = (scores - high.astype(F32)).astype(BF16)
        out = jnp.dot(high, value[:upto], preferred_element_type=F32) + jnp.dot(
            low, value[:upto], preferred_element_type=F32
        )
        out = out * lax.rsqrt(jnp.mean(out * out, axis=-1, keepdims=True) + EPS)
        attended[block] = out.astype(BF16)

def project_kernel(n, pos, x_share, *rest):
    weights, pieces, (out, a_all) = rest[:n], rest[n : 2 * n], rest[2 * n :]
    s = pos[1]
    total = x_share[...].astype(F32)
    for e in range(n):
        for d in range(n):
            span = pl.ds(pl.multiple_of((s ^ d) * HEAD_DIM, HEAD_DIM), HEAD_DIM)
            a_all[e, :, span] = pieces[d][e]
        total = total + lax.dot_general(
            a_all[e], weights[e][...], (((1,), (1,)), ((), ())), preferred_element_type=F32
        )
    out[...] = total.astype(BF16)


def route_kernel(n, experts, slots, pos, *refs):
    pieces, (pick, place, weight, table) = refs[:n], refs[n:]
    s = pos[1]
    rows = pieces[0].shape[0] - 2 * TOPK
    total = n * rows
    for d in range(n):
        lines = pieces[d][rows:, :].astype(F32)[:TOPK]
        gate = sum(lines[:, (1 + i) * rows : (2 + i) * rows] for i in range(3))
        span = pl.ds(pl.multiple_of((s ^ d) * rows, rows), rows)
        table[:, span] = jnp.concatenate([lines[:, :rows], gate], axis=0)
    first = (s * experts).astype(F32)
    names = lax.broadcasted_iota(jnp.int32, (experts, total), 0).astype(F32) + first
    member = jnp.zeros((experts, total), F32)
    gate = jnp.zeros((experts, total), F32)
    for k in range(TOPK):
        hit = table[k : k + 1, :] == names
        member = jnp.where(hit, 1.0, member)
        gate = jnp.where(hit, table[TOPK + k : TOPK + k + 1, :], gate)
    earlier = (
        lax.broadcasted_iota(jnp.int32, (total, total), 0)
        < lax.broadcasted_iota(jnp.int32, (total, total), 1)
    ).astype(F32).astype(BF16)
    rank = jnp.dot(member.astype(BF16), earlier, preferred_element_type=F32)
    slot = jnp.where(member > 0.0, rank, -1.0).astype(BF16)
    pairs = experts * slots
    expand = (
        lax.broadcasted_iota(jnp.int32, (experts, pairs), 1) // slots
        == lax.broadcasted_iota(jnp.int32, (experts, pairs), 0)
    ).astype(F32).astype(BF16)
    across = lax.dot_general(
        slot, expand, (((0,), (0,)), ((), ())), preferred_element_type=F32
    )
    number = (lax.broadcasted_iota(jnp.int32, (total, pairs), 1) % slots).astype(F32)
    place[...] = jnp.where(across == number, 1.0, 0.0).astype(BF16)
    for e in range(experts):
        span = pl.ds(e * slots, slots)
        number = lax.broadcasted_iota(jnp.int32, (slots, total), 0).astype(F32)
        hit = number == slot[e : e + 1, :].astype(F32)
        pick[span, :] = jnp.where(hit, 1.0, 0.0).astype(BF16)
        chosen = jnp.sum(jnp.where(hit, gate[e : e + 1, :], 0.0), axis=1, keepdims=True)
        weight[span, :] = jnp.broadcast_to(chosen, (slots, weight.shape[1]))


def stream(n_parts, moves):
    parts = [
        [pltpu.make_async_copy(*refs, sem) for refs, sem in moves(i)] for i in range(n_parts)
    ]
    for part in parts:
        for copy in part:
            copy.start()

    def wait(i):
        for copy in parts[i]:
            copy.wait()

    return wait


def hidden_kernel(n, slots, group, distances, last, pos, gain, pick, w_gate, w_up, *refs):
    first = 0 in distances
    refs = list(refs)
    n_blocks = len(distances)
    pieces = [[refs.pop(0) for _ in range(n)] for _ in range(n_blocks)]
    if not first:
        total_in, square_in = refs.pop(0), refs.pop(0)
    if last:
        weight, hidden_out, r_all, scaled, g_all, u_all, sems = refs
    else:
        total_out, square_out, r_all, scaled, g_all, u_all, sems = refs
    s, h = pos[1], pos[2]
    rows, cols = pieces[0][0].shape
    experts, _, hidden = g_all.shape

    def span(block, size):
        return pl.ds(pl.multiple_of(block * size, size), size)

    def moves(i):
        part = pl.ds(i * group, group)
        out = []
        for k, distance in enumerate(distances):
            column, here = span(s ^ distance, cols), pl.ds(k * cols, cols)
            for which, (w, kept) in enumerate(((w_gate, g_all), (w_up, u_all))):
                sem = sems.at[(i * n_blocks + k) * 2 + which]
                out.append(((w.at[part, column, :], kept.at[part, here, :]), sem))
        return out

    wait = stream(experts // group, moves)
    gains = []
    for k, distance in enumerate(distances):
        here = slice(k * cols, (k + 1) * cols)
        for e in range(n):
            r_all[span(h ^ e, rows), here] = pieces[k][e][...]
        gains.append(gain[:, span(s ^ distance, cols)])
    width = n * cols
    factor = []
    for i in range(experts // group):
        part = slice(i * group * slots, (i + 1) * group * slots)
        square = 0.0 if first else square_in[part, :1]
        for k in range(n_blocks):
            here = slice(k * cols, (k + 1) * cols)
            taken = jnp.dot(pick[part, :], r_all[:, here], preferred_element_type=F32)
            square = square + jnp.sum(taken * taken, axis=1, keepdims=True)
            scaled[part, here] = (taken * gains[k]).astype(BF16)
        if last:
            factor.append(lax.rsqrt(square / width + EPS))
        else:
            square_out[part, :] = jnp.broadcast_to(square, (group * slots, square_out.shape[1]))
    for i in range(experts // group):
        wait(i)
        for e in range(i * group, (i + 1) * group):
            mine = slice(e * slots, (e + 1) * slots)
            gate_val = jnp.dot(scaled[mine, :], g_all[e], preferred_element_type=F32)
            up_val = jnp.dot(scaled[mine, :], u_all[e], preferred_element_type=F32)
            if not first:
                gate_val = gate_val + total_in[mine, :hidden]
                up_val = up_val + total_in[mine, hidden:]
            if last:
                inner = (e - i * group) * slots
                scale = factor[i][inner : inner + slots]
                gate_val, up_val = gate_val * scale, up_val * scale
                value = gate_val * jax.nn.sigmoid(gate_val) * (up_val * weight[mine, :1])
                hidden_out[mine, :] = value.astype(BF16)
            else:
                total_out[mine, :hidden] = gate_val
                total_out[mine, hidden:] = up_val


def down_kernel(n, slots, group, distances, pos, hidden, place, w_down, *refs):
    outs, (d_all, y_slots, sems) = refs[: len(distances)], refs[len(distances) :]
    h = pos[2]
    _, experts, _, cols = d_all.shape
    parts = experts // group

    def moves(i):
        k, part = i // parts, pl.ds(i % parts * group, group)
        column = pl.ds(pl.multiple_of((h ^ distances[k]) * cols, cols), cols)
        return [((w_down.at[part, :, column], d_all.at[k, part]), sems.at[i])]

    wait = stream(len(distances) * parts, moves)
    for k in range(len(distances)):
        for i in range(parts):
            wait(k * parts + i)
            for e in range(i * group, (i + 1) * group):
                span = slice(e * slots, (e + 1) * slots)
                product = jnp.dot(hidden[span, :], d_all[k, e], preferred_element_type=F32)
                y_slots[span, :] = product.astype(BF16)
        outs[k][...] = jnp.dot(place[...], y_slots[...], preferred_element_type=F32).astype(BF16)


def add_kernel(distances, pos, base, core, part, *outs):
    s = pos[1]
    rows = outs[0].shape[0]
    in_half = part.shape[0] // rows
    for d, out in zip(distances, outs):
        block = s ^ d
        everywhere = pl.ds(pl.multiple_of(block * rows, rows), rows)
        inside = pl.ds(pl.multiple_of(block % in_half * rows, rows), rows)
        value = base[everywhere, :].astype(F32) + core[everywhere, :].astype(F32)
        out[...] = (value + part[inside, :].astype(F32)).astype(out.dtype)


def square_body(
    n, tokens, attn_weight, attn_gain, moe_gain, routes, gates, expert_gate, expert_up, expert_down
):
    g, s, h = (lax.axis_index(axis) for axis in ("grp", "seq", "head"))
    pos = jnp.stack([g, s, h]).astype(jnp.int32)
    rows, width = tokens.shape
    cols = width // n
    depth = attn_weight.shape[1]
    half = depth // 2
    experts, _, hidden = expert_gate.shape
    total = n * rows
    slots = -(-n * CAP // 16) * 16
    pairs = experts * slots
    sds = jax.ShapeDtypeStruct
    dma = pltpu.SemaphoreType.DMA

    def room(mib):
        return pltpu.CompilerParams(vmem_limit_bytes=mib * MIB)

    def cost(macs, size):
        return pl.CostEstimate(flops=2 * macs, bytes_accessed=size, transcendentals=0)

    def plus(*terms):
        total_value = terms[0].astype(F32)
        for term in terms[1:]:
            total_value = total_value + term.astype(F32)
        return total_value

    lines = 2 * TOPK
    with jax.named_scope("cut_pieces"):
        x_send, w_own, o_own, *w_sends = pl.pallas_call(
            cut_kernel,
            out_shape=[
                sds((rows + lines, cols), BF16),
                sds((depth, 3 * HEAD_DIM), BF16),
                sds((depth, cols), BF16),
            ]
            + [sds((half, 3 * HEAD_DIM), BF16)] * (n - 1),
            in_specs=[SMEM] + [ANY] * 4,
            out_specs=[VMEM] * (n + 2),
            scratch_shapes=[
                pltpu.VMEM((TOPK, rows), jnp.int32),
                pltpu.VMEM((TOPK, rows), F32),
                dma((4 + 3 * n,)),
            ],
            compiler_params=room(8),
        )(pos, *map(held, (routes.T, gates.T, tokens, attn_weight)))
    with jax.named_scope("gather_tokens_and_weights"):
        x_far = [swap(x_send, "seq", d) for d in range(1, n)]
        w_near = [swap(w_sends[d - 1], "seq", d) for d in range(1, n - 1)]
        step = in_step(*x_far, *w_near, w_sends[-1])
        x_far, w_near, w_last = step[: n - 1], list(step[n - 1 : -1]), step[-1]
        x_pieces = {0: jnp.stack([x[:rows] for x in x_far])}
        x_pieces[2] = swap(x_pieces[0], "head", 2)
        w_far = [swap(w, "grp", 1) for w in w_near]
        w_near.append(swap(w_last, "seq", n - 1))
        x_pieces[2], w_near[-1], o_own, *w_far = in_step(x_pieces[2], w_near[-1], o_own, *w_far)
        w_far.append(swap(w_near[-1], "grp", 1))
        o_pieces = {0: o_own, 2: swap(o_own, "head", 2)}
        for e in (0, 2):
            x_pieces[e ^ 1] = swap(x_pieces[e], "head", 1)
    with jax.named_scope("routing"):
        pick, place, weight = pl.pallas_call(
            functools.partial(route_kernel, n, experts, slots),
            out_shape=[sds((pairs, total), BF16), sds((total, pairs), BF16), sds((pairs, 128), F32)],
            in_specs=[SMEM] + [VMEM] * n,
            out_specs=[VMEM] * 3,
            scratch_shapes=[pltpu.VMEM((2 * TOPK, total), F32)],
            compiler_params=room(16),
        )(pos, x_send, *x_far)
        w_near[-1] = after(w_near[-1], pick)

    with jax.named_scope("attention"):
        attended, x_share = pl.pallas_call(
            functools.partial(attend_kernel, n),
            out_shape=[sds((n, rows, HEAD_DIM), BF16), sds((rows, cols), BF16)],
            in_specs=[SMEM, VMEM] + [ANY] * (2 + n + 2 * (n - 1) - 1) + [VMEM],
            out_specs=[VMEM] * 2,
            scratch_shapes=[
                pltpu.VMEM((total, width), BF16),
                pltpu.VMEM((width, 3 * HEAD_DIM), BF16),
                dma((2 + n * (n - 1) + 2 * (n - 1),)),
            ],
            compiler_params=room(14),
        )(
            pos, attn_gain.reshape(1, width), held(tokens), held(w_own),
            *[held(x_pieces[e]) for e in range(n)], *map(held, w_near), *map(held, w_far[:-1]), w_far[-1],
        )

    with jax.named_scope("heads_to_tokens"):
        for e in (0, 2):
            o_pieces[e ^ 1] = swap(after(o_pieces[e], attended), "head", 1)
        by_block = [
            lax.dynamic_index_in_dim(attended, h ^ e, 0, keepdims=False) for e in range(n)
        ]
        arrived = jnp.stack([by_block[0]] + [swap(by_block[e], "head", e) for e in range(1, n)])
        a_pieces = [arrived, swap(arrived, "seq", 1), swap(arrived, "seq", 2)]
        a_pieces.append(swap(a_pieces[2], "seq", 1))

    with jax.named_scope("output_projection"):
        residual = pl.pallas_call(
            functools.partial(project_kernel, n),
            out_shape=sds((rows, cols), BF16),
            in_specs=[SMEM] + [VMEM] * (1 + 2 * n),
            out_specs=VMEM,
            scratch_shapes=[pltpu.VMEM((n, rows, n * HEAD_DIM), BF16)],
            compiler_params=room(12),
        )(pos, x_share, *[o_pieces[e] for e in range(n)], *a_pieces)

    group = experts // 4

    def add_blocks(distances, pieces, state):
        last = n - 1 in distances
        wide = len(distances) * cols
        with jax.named_scope("hidden_units_" + "_".join(map(str, distances))):
            return pl.pallas_call(
                functools.partial(hidden_kernel, n, slots, group, distances, last),
                out_shape=[sds((pairs, hidden), BF16)]
                if last
                else [sds((pairs, 2 * hidden), F32), sds((pairs, 128), F32)],
                in_specs=[SMEM] + [VMEM] * 2 + [ANY] * 2
                + [VMEM] * (n * len(distances) + len(state) + last),
                out_specs=[VMEM] * (2 - last),
                scratch_shapes=[
                    pltpu.VMEM((total, wide), BF16),
                    pltpu.VMEM((pairs, wide), BF16),
                    pltpu.VMEM((experts, wide, hidden), BF16),
                    pltpu.VMEM((experts, wide, hidden), BF16),
                    dma((2 * len(distances) * (experts // group),)),
                ],
                compiler_params=room(6 + 11 * len(distances)),
                cost_estimate=cost(pairs * wide * (total + 2 * hidden), 4 * experts * wide * hidden),
            )(
                pos, moe_gain.reshape(1, width), pick, held(expert_gate), held(expert_up),
                *[pieces[d][e] for d in distances for e in range(n)],
                *state, *([weight] if last else []),
            )

    with jax.named_scope("gather_residual"):
        early, late = tuple(range(n // 2)), tuple(range(n // 2, n))
        r_pieces = {0: {0: residual}}
        for d in (1, 2):
            r_pieces[d] = {0: swap(residual, "seq", d)}
        r_pieces[3] = {0: swap(r_pieces[2][0], "seq", 1)}
        for d in range(n):
            r_pieces[d][2] = swap(r_pieces[d][0], "head", 2)
            r_pieces[d][1] = swap(r_pieces[d][0], "head", 1)
        for d in early:
            r_pieces[d][3] = swap(r_pieces[d][2], "head", 1)
        r_pieces[0][0] = after(residual, *[r_pieces[d][0] for d in late])
        state = add_blocks(early, r_pieces, ())
        for d in late:
            r_pieces[d][3] = swap(after(r_pieces[d][2], state[1]), "head", 1)
        state = add_blocks(late, r_pieces, state)
        r_choices = [r_pieces[d][d] for d in range(n)]
    (units,) = state

    def down(distances, units):
        with jax.named_scope("down_quarters_" + "_".join(map(str, distances))):
            return pl.pallas_call(
                functools.partial(down_kernel, n, slots, group, distances),
                out_shape=[sds((total, cols), BF16)] * len(distances),
                in_specs=[SMEM, VMEM, VMEM, ANY],
                out_specs=[VMEM] * len(distances),
                scratch_shapes=[
                    pltpu.VMEM((len(distances), experts, hidden, cols), BF16),
                    pltpu.VMEM((pairs, cols), BF16),
                    dma((len(distances) * (experts // group),)),
                ],
                compiler_params=room(4 + 5 * len(distances)),
                cost_estimate=cost(
                    len(distances) * pairs * cols * (total + hidden),
                    2 * len(distances) * experts * cols * hidden,
                ),
            )(pos, units, place, held(expert_down))

    def rows_of(array, block, count=1):
        return lax.dynamic_slice_in_dim(array, block * rows, count * rows, 0)

    with jax.named_scope("sum_over_devices"):
        half_line = n // 2
        here = s // half_line * half_line
        there = half_line - here
        out_3, out_1 = down((3, 1), units)
        core_2, core_0 = swap(out_3, "head", 1), swap(out_1, "head", 1)
        (out_2,) = down((2,), after(units, out_3))
        near = [
            plus(rows_of(out_2, b, half_line), rows_of(core_2, b, half_line)).astype(BF16)
            for b in (there, here)
        ]
        far = [swap(part, "head", 2) for part in near]
        (out_0,) = down((0,), after(units, *near))

        def add_parts(scope, distances, part, macs):
            with jax.named_scope(scope):
                return pl.pallas_call(
                    functools.partial(add_kernel, distances),
                    out_shape=[sds((rows, cols), BF16 if d else F32) for d in distances],
                    in_specs=[SMEM] + [VMEM] * 3,
                    out_specs=[VMEM] * len(distances),
                    compiler_params=room(4),
                    cost_estimate=cost(macs, 4 * part.size),
                )(pos, out_0, core_0, part)

        far_line = tuple(range(half_line, n))
        near_line = tuple(range(half_line))
        far_sums = add_parts("far_half_rows", far_line, far[0], 0)
        from_far = [swap(part, "seq", d) for d, part in zip(far_line, far_sums)]
        own_sum, *near_sums = add_parts("near_half_rows", near_line, far[1], SLOW)
        from_near = [swap(part, "seq", d) for d, part in zip(near_line[1:], near_sums)]
        mixed = plus(lax.select_n(s ^ h, *in_step(*r_choices, own_sum)[:n]), own_sum, *from_far)
        mixed = plus(*in_step(mixed, *from_near))
        mixed = mixed.astype(BF16)
    with jax.named_scope("gather_columns"):
        return lax.all_gather(mixed, "head", axis=1, tiled=True)


def solution(mesh):
    sizes = dict(mesh.shape)
    n = sizes["seq"]

    def body(tokens, attn_weight, *rest):
        width = tokens.shape[1]
        square = (
            n == sizes["head"]
            and n == 4
            and sizes["grp"] == 2
            and width == n * attn_weight.shape[1] == n * attn_weight.shape[2]
            and width == n * n * HEAD_DIM
            and n * tokens.shape[0] <= width // n
        )
        if square:
            return square_body(n, tokens, attn_weight, *rest)
        return general_body(tokens, attn_weight, *rest)

    return jax.shard_map(
        body,
        mesh=mesh,
        in_specs=(
            P(("grp", "seq"), None),
            P(None, "seq", "head"),
            P(),
            P(),
            P(("grp", "seq"), None),
            P(("grp", "seq"), None),
            P("seq", None, "head"),
            P("seq", None, "head"),
            P("seq", "head", None),
        ),
        out_specs=P(("grp", "seq"), None),
        check_vma=False,
    )
```

```python
import functools

import jax
import jax.numpy as jnp
from jax import lax
from jax.experimental import pallas as pl
from jax.experimental.pallas import tpu as pltpu
from jax.sharding import PartitionSpec as P

HEAD_DIM = 128
EXPERTS = 64
TOPK = 8
CAP = 18
EPS = 1e-06

PRECISE = lax.Precision.HIGHEST
BF16 = jnp.bfloat16
F32 = jnp.float32
ANY = pl.BlockSpec(memory_space=pl.ANY)
SMEM = pl.BlockSpec(memory_space=pltpu.SMEM)
VMEM = pl.BlockSpec(memory_space=pltpu.VMEM)
MIB = 1024 * 1024
SLOW = 10**10


def prefix_2(array, axis, combine, identity):
    peers, position = (lax.axis_size(axis), lax.axis_index(axis))
    everything = lax.all_gather(array.astype(jnp.bfloat16), axis)
    start = jnp.broadcast_to(jnp.asarray(identity, array.dtype), array.shape)

    def hop(k, before):
        reached = k < position
        new = combine(before, everything[k].astype(array.dtype))
        return jnp.where(reached, new, before)

    return lax.fori_loop(0, peers, hop, start)


def rms_scale(row_block, gain_vec):
    widened = row_block.astype(jnp.float32)
    factor = lax.rsqrt(jnp.mean(widened * widened, axis=-1, keepdims=True) + 1e-06)
    return widened * factor * gain_vec


def head_norm(outputs):
    return outputs * lax.rsqrt(jnp.mean(outputs * outputs, axis=-1, keepdims=True) + 1e-06)


def add_states(earlier, later):
    return earlier + later


def slot_numbers(route_flat):
    one_hot = (route_flat[:, None] == jnp.arange(EXPERTS, dtype=jnp.int32)[None, :]).astype(
        jnp.int32
    )
    earlier = jnp.cumsum(one_hot, axis=0) - one_hot
    return route_flat * CAP + jnp.sum(earlier * one_hot, axis=1)


def make_runner(expert_gate, expert_up, expert_down):

    def run_experts(received):
        gate_val = jnp.einsum(
            "necd,edf->necf", received, expert_gate, preferred_element_type=jnp.float32
        )
        up_val = jnp.einsum(
            "necd,edf->necf", received, expert_up, preferred_element_type=jnp.float32
        )
        hidden = (jax.nn.silu(gate_val) * up_val).astype(jnp.bfloat16)
        partial_value = jnp.einsum(
            "necf,efd->necd", hidden, expert_down, preferred_element_type=jnp.float32
        ).astype(jnp.bfloat16)
        groups = lax.axis_size("head")
        shape_now = partial_value.shape
        split = partial_value.reshape(
            shape_now[0], shape_now[1], shape_now[2], groups, shape_now[3] // groups
        )
        by_group = lax.all_to_all(split, "head", split_axis=3, concat_axis=3, tiled=True)
        summed = jnp.sum(by_group.astype(jnp.float32), axis=3)
        return lax.all_to_all(
            summed.astype(jnp.bfloat16), "seq", split_axis=0, concat_axis=0, tiled=True
        ).astype(summed.dtype)

    return run_experts


def general_body(
    tokens, attn_weight, attn_gain, moe_gain, routes, gates, expert_gate, expert_up, expert_down
):
    local_rows = tokens.shape[0]
    normed = rms_scale(tokens, attn_gain).astype(jnp.bfloat16)
    weights = lax.all_gather(attn_weight, "seq", axis=1, tiled=True)
    head_count = weights.shape[2] // HEAD_DIM
    projected = [
        jnp.dot(normed, weights[which], preferred_element_type=jnp.float32)
        .astype(jnp.bfloat16)
        .reshape(local_rows, head_count, HEAD_DIM)
        for which in range(3)
    ]
    query_rows, key_rows, value_rows = projected
    own_state = jnp.einsum("thd,the->hde", key_rows, value_rows, preferred_element_type=jnp.float32)
    prefix = prefix_2(own_state, "seq", add_states, jnp.zeros_like(own_state))
    inter_part = jnp.einsum(
        "thd,hde->the", query_rows.astype(jnp.float32), prefix, precision=PRECISE
    )
    scores = jnp.einsum("thd,shd->hts", query_rows, key_rows, preferred_element_type=jnp.float32)
    lower_mask = jnp.arange(local_rows)[:, None] >= jnp.arange(local_rows)[None, :]
    scores = jnp.where(lower_mask[None], scores, 0.0)
    intra_part = jnp.einsum(
        "hts,she->the", scores, value_rows.astype(jnp.float32), precision=PRECISE
    )
    attended = (
        head_norm(inter_part + intra_part)
        .reshape(local_rows, head_count * HEAD_DIM)
        .astype(jnp.bfloat16)
    )
    out_part = lax.dot_general(
        attended, weights[3], (((1,), (1,)), ((), ())), preferred_element_type=jnp.float32
    )
    residual = (
        tokens.astype(jnp.float32)
        + lax.psum(out_part.astype(jnp.bfloat16), "head").astype(jnp.float32)
    ).astype(jnp.bfloat16)
    moe_in = rms_scale(residual, moe_gain).astype(jnp.bfloat16)
    route_flat = routes.reshape(-1)
    slots = slot_numbers(route_flat)
    owners = lax.axis_size("seq")
    local_experts = expert_gate.shape[0]
    source_row = jnp.arange(route_flat.shape[0], dtype=jnp.int32) // TOPK
    run_experts = make_runner(expert_gate, expert_up, expert_down)
    outbound = (
        jnp.zeros((EXPERTS * CAP, moe_in.shape[1]), jnp.bfloat16).at[slots].set(moe_in[source_row])
    )
    outbound = outbound.reshape(owners, local_experts, CAP, moe_in.shape[1])
    returned = run_experts(lax.all_to_all(outbound, "seq", split_axis=0, concat_axis=0, tiled=True))
    arrived = returned.reshape(EXPERTS * CAP, -1)[slots].reshape(local_rows, TOPK, -1)
    moe_partial = jnp.einsum("tkd,tk->td", arrived, gates, precision=PRECISE)
    column_span = moe_partial.shape[1]
    residual_share = lax.dynamic_slice_in_dim(
        residual, lax.axis_index("head") * column_span, column_span, 1
    )
    mixed_share = (residual_share.astype(jnp.float32) + moe_partial).astype(jnp.bfloat16)
    return lax.all_gather(mixed_share, "head", axis=1, tiled=True)


def swap(array, axis, distance):
    size = lax.axis_size(axis)
    return lax.ppermute(array, axis, [(i, i ^ distance) for i in range(size)])


def run_copies(copies):
    for copy in copies:
        copy.start()
    for copy in copies:
        copy.wait()


def after(array, *earlier):
    return lax.optimization_barrier((array,) + earlier)[0]


def held(array):
    return pltpu.with_memory_space_constraint(array, pltpu.HBM)


def here(array):
    return pltpu.with_memory_space_constraint(array, pltpu.VMEM)


def in_step(*arrays):
    return lax.optimization_barrier(arrays)


def cut_kernel(pos, routes, gates, tokens, weight, x_send, w_own, o_own, *rest):
    w_sends, (r_here, g_here, sems) = rest[:-3], rest[-3:]
    g, s, h = pos[0], pos[1], pos[2]
    rows, cols, half = tokens.shape[0], x_send.shape[1], w_sends[0].shape[0]
    copies = [
        (
            tokens.at[:, pl.ds(pl.multiple_of(h * cols, cols), cols)],
            x_send.at[pl.ds(0, rows)],
        ),
        (weight.at[3], o_own),
        (routes, r_here),
        (gates, g_here),
    ]
    for which in range(3):
        span = pl.ds(which * HEAD_DIM, HEAD_DIM)
        for distance, out in enumerate(w_sends, 1):
            column = pl.multiple_of((s ^ distance) * HEAD_DIM, HEAD_DIM)
            own_half = pl.ds(pl.multiple_of(g * half, half), half)
            copies.append(
                (weight.at[which, own_half, pl.ds(column, HEAD_DIM)], out.at[:, span])
            )
        column = pl.multiple_of(s * HEAD_DIM, HEAD_DIM)
        copies.append((weight.at[which, :, pl.ds(column, HEAD_DIM)], w_own.at[:, span]))
    copies = [pltpu.make_async_copy(a, b, sems.at[i]) for i, (a, b) in enumerate(copies)]
    for copy in copies:
        copy.start()
    for copy in copies[2:4]:
        copy.wait()
    parts, left = [r_here[...].astype(F32)], g_here[...]
    for _ in range(3):
        parts.append(left.astype(BF16).astype(F32))
        left = left - parts[-1]
    lines = jnp.concatenate(parts, axis=1)
    lines = jnp.concatenate([lines, jnp.zeros_like(lines)], axis=0)
    blank = jnp.zeros((lines.shape[0], cols - lines.shape[1]), F32)
    if blank.shape[1]:
        lines = jnp.concatenate([lines, blank], axis=1)
    x_send[rows:, :] = lines.astype(BF16)
    for copy in copies[:2] + copies[4:]:
        copy.wait()


def attend_kernel(n, pos, gain, tokens, w_own, *rest):
    x_pieces, rest = rest[:n], rest[n:]
    w_near, rest = rest[: n - 1], rest[n - 1 :]
    w_far, rest = rest[: n - 1], rest[n - 1 :]
    attended, x_share, x_all, w_all, sems = rest
    g, s, h = pos[0], pos[1], pos[2]
    rows, width = tokens.shape
    cols = width // n
    depth, half = w_own.shape[0], w_near[0].shape[0]
    total = n * rows

    def at_rows(block, size):
        return pl.ds(pl.multiple_of(block * size, size), size)

    copies = [(tokens, x_all.at[at_rows(s, rows)])]
    for d in range(1, n):
        for e in range(n):
            copies.append(
                (x_pieces[e].at[d - 1], x_all.at[at_rows(s ^ d, rows), at_rows(h ^ e, cols)])
            )
    n_rows = len(copies)
    copies.append((w_own, w_all.at[at_rows(s, depth)]))
    for d in range(1, n):
        copies.append((w_near[d - 1], w_all.at[at_rows((s ^ d) * 2 + g, half)]))
        copies.append((w_far[d - 1], w_all.at[at_rows((s ^ d) * 2 + (1 - g), half)]))
    copies = [pltpu.make_async_copy(a, b, sems.at[i]) for i, (a, b) in enumerate(copies)]
    for copy in copies:
        copy.start()
    for copy in copies[:n_rows]:
        copy.wait()
    x_share[...] = x_all[at_rows(h, rows), at_rows(s, cols)]

    def normalise(block, carry):
        mine = at_rows(block, rows)
        wide = x_all[mine, :].astype(F32)
        factor = lax.rsqrt(jnp.mean(wide * wide, axis=-1, keepdims=True) + EPS)
        x_all[mine, :] = (wide * factor * gain[...]).astype(BF16)
        return carry

    lax.fori_loop(0, n, normalise, 0)
    for copy in copies[n_rows:]:
        copy.wait()
    projected = [
        jnp.dot(
            x_all[block * rows : (block + 1) * rows, :], w_all[...], preferred_element_type=F32
        ).astype(BF16)
        for block in range(n)
    ]
    whole = jnp.concatenate(projected, axis=0)
    query, key, value = (whole[:, i * HEAD_DIM : (i + 1) * HEAD_DIM] for i in range(3))
    for block in range(n):
        upto = (block + 1) * rows
        scores = lax.dot_general(
            query[block * rows : upto],
            key[:upto],
            (((1,), (1,)), ((), ())),
            preferred_element_type=F32,
        )
        ahead = lax.broadcasted_iota(jnp.int32, scores.shape, 0) + block * rows
        scores = jnp.where(ahead >= lax.broadcasted_iota(jnp.int32, scores.shape, 1), scores, 0.0)
        high = scores.astype(BF16)
        low = (scores - high.astype(F32)).astype(BF16)
        out = jnp.dot(high, value[:upto], preferred_element_type=F32) + jnp.dot(
            low, value[:upto], preferred_element_type=F32
        )
        out = out * lax.rsqrt(jnp.mean(out * out, axis=-1, keepdims=True) + EPS)
        attended[block] = out.astype(BF16)

def bring_kernel(*refs):
    count = len(refs) // 2
    sems = refs[-1]
    copies = [pltpu.make_async_copy(refs[i], refs[count + i], sems.at[i]) for i in range(count)]
    for copy in copies:
        copy.start()
    for copy in copies:
        copy.wait()


def project_kernel(n, pos, x_share, *rest):
    weights, pieces, (out, a_all) = rest[:n], rest[n : 2 * n], rest[2 * n :]
    s = pos[1]
    total = x_share[...].astype(F32)
    for e in range(n):
        for d in range(n):
            span = pl.ds(pl.multiple_of((s ^ d) * HEAD_DIM, HEAD_DIM), HEAD_DIM)
            a_all[e, :, span] = pieces[d][e]
        total = total + lax.dot_general(
            a_all[e], weights[e][...], (((1,), (1,)), ((), ())), preferred_element_type=F32
        )
    out[...] = total.astype(BF16)


def route_kernel(n, experts, slots, pos, *refs):
    pieces, (pick, place, weight, table) = refs[:n], refs[n:]
    s = pos[1]
    rows = pieces[0].shape[0] - 2 * TOPK
    total = n * rows
    for d in range(n):
        lines = pieces[d][rows:, :].astype(F32)[:TOPK]
        gate = sum(lines[:, (1 + i) * rows : (2 + i) * rows] for i in range(3))
        span = pl.ds(pl.multiple_of((s ^ d) * rows, rows), rows)
        table[:, span] = jnp.concatenate([lines[:, :rows], gate], axis=0)
    first = (s * experts).astype(F32)
    names = lax.broadcasted_iota(jnp.int32, (experts, total), 0).astype(F32) + first
    member = jnp.zeros((experts, total), F32)
    gate = jnp.zeros((experts, total), F32)
    for k in range(TOPK):
        hit = table[k : k + 1, :] == names
        member = jnp.where(hit, 1.0, member)
        gate = jnp.where(hit, table[TOPK + k : TOPK + k + 1, :], gate)
    earlier = (
        lax.broadcasted_iota(jnp.int32, (total, total), 0)
        < lax.broadcasted_iota(jnp.int32, (total, total), 1)
    ).astype(F32).astype(BF16)
    rank = jnp.dot(member.astype(BF16), earlier, preferred_element_type=F32)
    slot = jnp.where(member > 0.0, rank, -1.0).astype(BF16)
    pairs = experts * slots
    expand = (
        lax.broadcasted_iota(jnp.int32, (experts, pairs), 1) // slots
        == lax.broadcasted_iota(jnp.int32, (experts, pairs), 0)
    ).astype(F32).astype(BF16)
    across = lax.dot_general(
        slot, expand, (((0,), (0,)), ((), ())), preferred_element_type=F32
    )
    number = (lax.broadcasted_iota(jnp.int32, (total, pairs), 1) % slots).astype(F32)
    place[...] = jnp.where(across == number, 1.0, 0.0).astype(BF16)
    for e in range(experts):
        span = pl.ds(e * slots, slots)
        number = lax.broadcasted_iota(jnp.int32, (slots, total), 0).astype(F32)
        hit = number == slot[e : e + 1, :].astype(F32)
        pick[span, :] = jnp.where(hit, 1.0, 0.0).astype(BF16)
        chosen = jnp.sum(jnp.where(hit, gate[e : e + 1, :], 0.0), axis=1, keepdims=True)
        weight[span, :] = jnp.broadcast_to(chosen, (slots, weight.shape[1]))


def span(block, size):
    return pl.ds(pl.multiple_of(block * size, size), size)


def weight_copies(pos, distances, i, group, ins, outs, sems, first=0):
    source_part, part = pl.ds(first + i * group, group), pl.ds(i * group, group)
    cols = outs[0].shape[1] // len(distances)
    copies = []
    for k, distance in enumerate(distances):
        for which, (w, kept) in enumerate(zip(ins, outs)):
            source = w.at[source_part, span(pos[1] ^ distance, cols), :]
            target = kept.at[part, pl.ds(k * cols, cols), :]
            copies.append(pltpu.make_async_copy(source, target, sems.at[i, 2 * k + which]))
    return copies


def down_copies(pos, distances, i, group, w_down, outs, sems):
    part, cols = pl.ds(i * group, group), outs[0].shape[2]
    copies = []
    for k, (distance, kept) in enumerate(zip(distances, outs)):
        source = w_down.at[part, :, span(pos[2] ^ distance, cols)]
        copies.append(pltpu.make_async_copy(source, kept.at[part], sems.at[i, k]))
    return copies


def load_kernel(group, distances, pos, w_gate, w_up, g_all, u_all, sems):
    copies = []
    for i in range(g_all.shape[0] // group):
        copies += weight_copies(
            pos, distances, i, group, (w_gate, w_up), (g_all, u_all), sems
        )
    for copy in copies:
        copy.start()
    for copy in copies:
        copy.wait()


def place_rows(n, distances, pos, pieces, r_all):
    rows, cols = pieces[0][0].shape
    for k in range(len(distances)):
        for e in range(n):
            r_all[span(pos[2] ^ e, rows), k * cols : (k + 1) * cols] = pieces[k][e][...]


def gather_rows(distances, pos, gain, picked, r_all, square):
    cols = r_all.shape[1] // len(distances)
    scaled = []
    for k, distance in enumerate(distances):
        taken = jnp.dot(picked, r_all[:, k * cols : (k + 1) * cols], preferred_element_type=F32)
        square = square + jnp.sum(taken * taken, axis=1, keepdims=True)
        scaled.append((taken * gain[:, span(pos[1] ^ distance, cols)]).astype(BF16))
    return scaled, square


def first_hidden_kernel(n, slots, group, distances, pos, gain, pick, g_all, u_all, *refs):
    pieces = [refs[k * n : (k + 1) * n] for k in range(len(distances))]
    total_out, square_out, r_all, x_slots = refs[n * len(distances) :]
    experts, wide, hidden = g_all.shape
    place_rows(n, distances, pos, pieces, r_all)
    for i in range(experts // group):
        part = slice(i * group * slots, (i + 1) * group * slots)
        scaled, square = gather_rows(distances, pos, gain, pick[part, :], r_all, 0.0)
        for k, value in enumerate(scaled):
            x_slots[part, k * value.shape[1] : (k + 1) * value.shape[1]] = value
        square_out[part, :] = jnp.broadcast_to(square, (group * slots, square_out.shape[1]))
    for e in range(experts):
        mine = slice(e * slots, (e + 1) * slots)
        total_out[mine, :hidden] = jnp.dot(x_slots[mine, :], g_all[e], preferred_element_type=F32)
        total_out[mine, hidden:] = jnp.dot(x_slots[mine, :], u_all[e], preferred_element_type=F32)


def last_hidden_kernel(
    n, slots, group, distances, downs, pos, gain, pick, w_gate, w_up, w_down, g_some, u_some,
    total_in, square_in, weight, *refs,
):
    pieces = [refs[k * n : (k + 1) * n] for k in range(len(distances))]
    hidden_out, *refs = refs[n * len(distances) :]
    d_outs, (r_all, x_slots, g_all, u_all, sems, d_sems) = refs[: len(downs)], refs[len(downs) :]
    some, wide, hidden = g_some.shape
    ready, parts = some // group, (some + g_all.shape[0]) // group
    width = n * wide // len(distances)

    def copies(i):
        return weight_copies(
            pos, distances, i, group, (w_gate, w_up), (g_all, u_all), sems, first=some
        )

    def start(i, carry):
        for copy in copies(i):
            copy.start()
        return carry

    def d_copies(i):
        return down_copies(pos, downs, i, group, w_down, d_outs, d_sems)

    def start_down(i, carry):
        for copy in d_copies(i):
            copy.start()
        return carry

    def step(g_from, u_from, skipped, i, carry):
        part = span(i, group * slots)
        scaled, square = gather_rows(
            distances, pos, gain, pick[part, :], r_all, square_in[part, :1]
        )
        for k, value in enumerate(scaled):
            x_slots[:, k * value.shape[1] : (k + 1) * value.shape[1]] = value
        scale = lax.rsqrt(square / width + EPS)
        if skipped:
            for copy in copies(i - skipped):
                copy.wait()
        for e in range(group):
            inner = slice(e * slots, (e + 1) * slots)
            mine = pl.ds(pl.multiple_of(i * group * slots + e * slots, slots), slots)
            taken = x_slots[inner, :]
            gate_val = jnp.dot(taken, g_from[(i - skipped) * group + e], preferred_element_type=F32)
            up_val = jnp.dot(taken, u_from[(i - skipped) * group + e], preferred_element_type=F32)
            gate_val = (gate_val + total_in[mine, :hidden]) * scale[inner]
            up_val = (up_val + total_in[mine, hidden:]) * scale[inner]
            value = gate_val * jax.nn.sigmoid(gate_val) * (up_val * weight[mine, :1])
            hidden_out[mine, :] = value.astype(BF16)
        return carry

    lax.fori_loop(0, parts - ready, start, 0)
    lax.fori_loop(0, parts, start_down, 0)
    place_rows(n, distances, pos, pieces, r_all)
    lax.fori_loop(0, ready, functools.partial(step, g_some, u_some, 0), 0)
    lax.fori_loop(ready, parts, functools.partial(step, g_all, u_all, ready), 0)
    for i in range(parts):
        for copy in d_copies(i):
            copy.wait()


def self_down_kernel(slots, group, distances, pos, hidden, place, w_down, out, kept, y_slots, sems):
    copies = [
        down_copies(pos, distances, i, group, w_down, (kept,), sems)[0]
        for i in range(kept.shape[0] // group)
    ]
    for copy in copies:
        copy.start()

    def step(i, carry):
        down_copies(pos, distances, i, group, w_down, (kept,), sems)[0].wait()
        for e in range(group):
            mine = pl.ds(pl.multiple_of(i * group * slots + e * slots, slots), slots)
            product = jnp.dot(hidden[mine, :], kept[i * group + e], preferred_element_type=F32)
            y_slots[mine, :] = product.astype(BF16)
        return carry

    lax.fori_loop(0, len(copies), step, 0)
    out[...] = jnp.dot(place[...], y_slots[...], preferred_element_type=F32).astype(BF16)


def down_kernel(slots, pos, hidden, place, *refs):
    count = len(refs) // 2
    for kept, out in zip(refs[:count], refs[count:]):
        y_slots = refs[-1]
        for e in range(kept.shape[0]):
            mine = slice(e * slots, (e + 1) * slots)
            product = jnp.dot(hidden[mine, :], kept[e], preferred_element_type=F32)
            y_slots[mine, :] = product.astype(BF16)
        out[...] = jnp.dot(place[...], y_slots[...], preferred_element_type=F32).astype(BF16)


def add_kernel(distances, pos, base, core, part, *outs):
    s = pos[1]
    rows = outs[0].shape[0]
    in_half = part.shape[0] // rows
    for d, out in zip(distances, outs):
        block = s ^ d
        everywhere = pl.ds(pl.multiple_of(block * rows, rows), rows)
        inside = pl.ds(pl.multiple_of(block % in_half * rows, rows), rows)
        value = base[everywhere, :].astype(F32) + core[everywhere, :].astype(F32)
        out[...] = (value + part[inside, :].astype(F32)).astype(out.dtype)


def halves_kernel(pos, base, core, far, near):
    rows = near.shape[0]
    blocks = base.shape[0] // rows
    mine = pos[1] // blocks
    for half, out in ((blocks - 1 - mine, far), (mine, near)):
        value = base[span(half, rows), :].astype(F32) + core[span(half, rows), :].astype(F32)
        out[...] = value.astype(out.dtype)


def square_body(
    n, tokens, attn_weight, attn_gain, moe_gain, routes, gates, expert_gate, expert_up, expert_down
):
    g, s, h = (lax.axis_index(axis) for axis in ("grp", "seq", "head"))
    pos = jnp.stack([g, s, h]).astype(jnp.int32)
    rows, width = tokens.shape
    cols = width // n
    depth = attn_weight.shape[1]
    half = depth // 2
    experts, _, hidden = expert_gate.shape
    total = n * rows
    slots = -(-n * CAP // 16) * 16
    pairs = experts * slots
    sds = jax.ShapeDtypeStruct
    dma = pltpu.SemaphoreType.DMA

    def room(mib):
        return pltpu.CompilerParams(vmem_limit_bytes=mib * MIB)

    def cost(macs, size):
        return pl.CostEstimate(flops=2 * macs, bytes_accessed=size, transcendentals=0)

    def plus(*terms):
        total_value = terms[0].astype(F32)
        for term in terms[1:]:
            total_value = total_value + term.astype(F32)
        return total_value

    lines = 2 * TOPK
    with jax.named_scope("cut_pieces"):
        x_send, w_own, o_own, *w_sends = pl.pallas_call(
            cut_kernel,
            out_shape=[
                sds((rows + lines, cols), BF16),
                sds((depth, 3 * HEAD_DIM), BF16),
                sds((depth, cols), BF16),
            ]
            + [sds((half, 3 * HEAD_DIM), BF16)] * (n - 1),
            in_specs=[SMEM] + [ANY] * 4,
            out_specs=[VMEM] * (n + 2),
            scratch_shapes=[
                pltpu.VMEM((TOPK, rows), jnp.int32),
                pltpu.VMEM((TOPK, rows), F32),
                dma((4 + 3 * n,)),
            ],
            compiler_params=room(8),
        )(pos, *map(held, (routes.T, gates.T, tokens, attn_weight)))
    group = experts // 4
    w_gate, w_up, w_down = map(held, (expert_gate, expert_up, expert_down))

    with jax.named_scope("gather_tokens_and_weights"):
        x_far = [swap(x_send, "seq", d) for d in range(1, n)]
        w_near = [swap(w_sends[d - 1], "seq", d) for d in range(1, n - 1)]
        step = in_step(*x_far, *w_near, w_sends[-1])
        x_far, w_near, w_last = step[: n - 1], list(step[n - 1 : -1]), step[-1]
        x_pieces = {0: jnp.stack([x[:rows] for x in x_far])}
        x_pieces[2] = swap(x_pieces[0], "head", 2)
        w_far = [swap(w, "grp", 1) for w in w_near]
        w_near.append(swap(w_last, "seq", n - 1))
        x_pieces[2], w_near[-1], o_own, *w_far = in_step(x_pieces[2], w_near[-1], o_own, *w_far)
        w_far.append(swap(w_near[-1], "grp", 1))
        o_pieces = {0: o_own, 2: swap(o_own, "head", 2)}
        for e in (0, 2):
            x_pieces[e ^ 1] = swap(x_pieces[e], "head", 1)
    with jax.named_scope("routing"):
        pick, place, weight = pl.pallas_call(
            functools.partial(route_kernel, n, experts, slots),
            out_shape=[sds((pairs, total), BF16), sds((total, pairs), BF16), sds((pairs, 128), F32)],
            in_specs=[SMEM] + [VMEM] * n,
            out_specs=[VMEM] * 3,
            scratch_shapes=[pltpu.VMEM((2 * TOPK, total), F32)],
            compiler_params=room(16),
        )(pos, x_send, *x_far)
        w_near[-1] = after(w_near[-1], pick)

    with jax.named_scope("attention"):
        attended, x_share = pl.pallas_call(
            functools.partial(attend_kernel, n),
            out_shape=[sds((n, rows, HEAD_DIM), BF16), sds((rows, cols), BF16)],
            in_specs=[SMEM, VMEM] + [ANY] * (2 + n + 2 * (n - 1) - 1) + [VMEM],
            out_specs=[VMEM] * 2,
            scratch_shapes=[
                pltpu.VMEM((total, width), BF16),
                pltpu.VMEM((width, 3 * HEAD_DIM), BF16),
                dma((2 + n * (n - 1) + 2 * (n - 1),)),
            ],
            compiler_params=room(14),
        )(
            pos, attn_gain.reshape(1, width), held(tokens), held(w_own),
            *[held(x_pieces[e]) for e in range(n)], *map(held, w_near), *map(held, w_far[:-1]), w_far[-1],
        )

    early, late = tuple(range(n // 2)), tuple(range(n // 2, n))
    wide = n // 2 * cols
    gain_row = moe_gain.reshape(1, width)
    ahead = experts // 2
    hidden_cost = cost(pairs * wide * (total + 2 * hidden), 4 * experts * wide * hidden)

    def load(distances, amount, *earlier):
        return pl.pallas_call(
            functools.partial(load_kernel, group, distances),
            out_shape=[pltpu.VMEM((amount, wide, hidden), BF16)] * 2,
            in_specs=[SMEM] + [ANY] * 2,
            out_specs=[VMEM] * 2,
            scratch_shapes=[dma((amount // group, 2 * len(distances)))],
            compiler_params=room(2),
            cost_estimate=cost(0, 4 * amount * wide * hidden),
        )(after(pos, *earlier), w_gate, w_up)

    def first_hidden(pieces, weights):
        return pl.pallas_call(
            functools.partial(first_hidden_kernel, n, slots, group, early),
            out_shape=[sds((pairs, 2 * hidden), F32), sds((pairs, 128), F32)],
            in_specs=[SMEM] + [VMEM] * (4 + n * len(early)),
            out_specs=[VMEM] * 2,
            scratch_shapes=[pltpu.VMEM((total, wide), BF16), pltpu.VMEM((pairs, wide), BF16)],
            compiler_params=room(12),
            cost_estimate=hidden_cost,
        )(pos, gain_row, pick, *map(here, weights), *pieces)

    def last_hidden(pieces, weights, state, downs):
        return pl.pallas_call(
            functools.partial(last_hidden_kernel, n, slots, group, late, downs),
            out_shape=[sds((pairs, hidden), BF16)]
            + [pltpu.VMEM((experts, hidden, cols), BF16)] * len(downs),
            in_specs=[SMEM] + [VMEM] * 2 + [ANY] * 3 + [VMEM] * (5 + n * len(late)),
            out_specs=[VMEM] * (1 + len(downs)),
            scratch_shapes=[pltpu.VMEM((total, wide), BF16), pltpu.VMEM((group * slots, wide), BF16)]
            + [pltpu.VMEM((experts - ahead, wide, hidden), BF16)] * 2
            + [dma(((experts - ahead) // group, 2 * len(late)))]
            + [dma((experts // group, len(downs)))],
            compiler_params=room(16),
            cost_estimate=hidden_cost,
        )(
            pos, gain_row, pick, w_gate, w_up, w_down, *map(here, weights), *state, weight, *pieces
        )

    with jax.named_scope("heads_to_tokens"):
        for e in (0, 2):
            o_pieces[e ^ 1] = swap(after(o_pieces[e], attended), "head", 1)
        by_block = [
            lax.dynamic_index_in_dim(attended, h ^ e, 0, keepdims=False) for e in range(n)
        ]
        arrived = jnp.stack([by_block[0]] + [swap(by_block[e], "head", e) for e in range(1, n)])
        a_pieces = [arrived, swap(arrived, "seq", 1), swap(arrived, "seq", 2)]
        with jax.named_scope("expert_weights"):
            early_weights = load(early, experts, arrived)
        a_pieces[2] = after(a_pieces[2], early_weights[0])
        a_pieces.append(swap(a_pieces[2], "seq", 1))

    with jax.named_scope("bring_out_weights"):
        o_here = pl.pallas_call(
            bring_kernel,
            out_shape=[pltpu.VMEM((depth, cols), BF16)] * n,
            in_specs=[ANY] * n,
            out_specs=[VMEM] * n,
            scratch_shapes=[dma((n,))],
            compiler_params=room(2),
            cost_estimate=cost(0, 2 * n * depth * cols),
        )(*[held(o_pieces[e]) for e in range(n)])
    with jax.named_scope("output_projection"):
        residual = pl.pallas_call(
            functools.partial(project_kernel, n),
            out_shape=sds((rows, cols), BF16),
            in_specs=[SMEM] + [VMEM] * (1 + 2 * n),
            out_specs=VMEM,
            scratch_shapes=[pltpu.VMEM((n, rows, n * HEAD_DIM), BF16)],
            compiler_params=room(12),
        )(pos, x_share, *map(here, o_here), *a_pieces)

    with jax.named_scope("gather_residual"):
        r_pieces = {0: {0: residual}}
        late_weights = load(late, ahead, residual)
        for d in (1, 2):
            r_pieces[d] = {0: swap(residual, "seq", d)}
        r_pieces[3] = {0: swap(r_pieces[2][0], "seq", 1)}
        for d in range(n):
            r_pieces[d][2] = swap(r_pieces[d][0], "head", 2)
            r_pieces[d][1] = swap(r_pieces[d][0], "head", 1)
        for d in early:
            r_pieces[d][3] = swap(r_pieces[d][2], "head", 1)
        r_pieces[0][0] = after(residual, late_weights[0], *[r_pieces[d][0] for d in late])
        pieces = [r_pieces[d][e] for d in early for e in range(n)]
        with jax.named_scope("first_hidden_units"):
            state = first_hidden(pieces, early_weights)
        for d in late:
            r_pieces[d][3] = swap(after(r_pieces[d][2], state[1]), "head", 1)
        pieces = [r_pieces[d][e] for d in late for e in range(n)]
        with jax.named_scope("last_hidden_units"):
            units, d_3, d_1 = last_hidden(pieces, late_weights, state, (3, 1))
        r_choices = [r_pieces[d][d] for d in range(n)]
    def down(units, *weights):
        count = len(weights)
        with jax.named_scope("down_products"):
            return pl.pallas_call(
                functools.partial(down_kernel, slots),
                out_shape=[sds((total, cols), BF16)] * count,
                in_specs=[SMEM] + [VMEM] * (2 + count),
                out_specs=[VMEM] * count,
                scratch_shapes=[pltpu.VMEM((pairs, cols), BF16)],
                compiler_params=room(6),
                cost_estimate=cost(
                    count * pairs * cols * (total + hidden), 2 * count * experts * cols * hidden
                ),
            )(pos, units, place, *map(here, weights))

    def self_down(units, distance):
        with jax.named_scope("down_products_alone"):
            return pl.pallas_call(
                functools.partial(self_down_kernel, slots, group, (distance,)),
                out_shape=sds((total, cols), BF16),
                in_specs=[SMEM] + [VMEM] * 2 + [ANY],
                out_specs=VMEM,
                scratch_shapes=[
                    pltpu.VMEM((experts, hidden, cols), BF16),
                    pltpu.VMEM((pairs, cols), BF16),
                    dma((experts // group, 1)),
                ],
                compiler_params=room(9),
                cost_estimate=cost(pairs * cols * (total + hidden), 2 * experts * cols * hidden),
            )(pos, units, place, w_down)

    with jax.named_scope("sum_over_devices"):
        half_line = n // 2
        out_3, out_1 = down(units, d_3, d_1)
        core_2, core_0 = swap(out_3, "head", 1), swap(out_1, "head", 1)
        out_2 = self_down(after(units, out_3), 2)
        with jax.named_scope("halves_over_cores"):
            near = pl.pallas_call(
                halves_kernel,
                out_shape=[sds((half_line * rows, cols), BF16)] * 2,
                in_specs=[SMEM] + [VMEM] * 2,
                out_specs=[VMEM] * 2,
                compiler_params=room(4),
                cost_estimate=cost(0, 4 * total * cols),
            )(pos, out_2, core_2)
        far = [swap(part, "head", 2) for part in near]
        out_0 = self_down(after(units, *near), 0)

        def add_parts(scope, distances, part, macs):
            with jax.named_scope(scope):
                return pl.pallas_call(
                    functools.partial(add_kernel, distances),
                    out_shape=[sds((rows, cols), BF16 if d else F32) for d in distances],
                    in_specs=[SMEM] + [VMEM] * 3,
                    out_specs=[VMEM] * len(distances),
                    compiler_params=room(4),
                    cost_estimate=cost(macs, 4 * part.size),
                )(pos, out_0, core_0, part)

        far_line = tuple(range(half_line, n))
        near_line = tuple(range(half_line))
        far_sums = add_parts("far_half_rows", far_line, far[0], 0)
        from_far = [swap(part, "seq", d) for d, part in zip(far_line, far_sums)]
        own_sum, *near_sums = add_parts("near_half_rows", near_line, far[1], SLOW)
        from_near = [swap(part, "seq", d) for d, part in zip(near_line[1:], near_sums)]
        mixed = plus(lax.select_n(s ^ h, *in_step(*r_choices, own_sum)[:n]), own_sum, *from_far)
        mixed = plus(*in_step(mixed, *from_near))
        mixed = mixed.astype(BF16)
    with jax.named_scope("gather_columns"):
        return lax.all_gather(mixed, "head", axis=1, tiled=True)


def solution(mesh):
    sizes = dict(mesh.shape)
    n = sizes["seq"]

    def body(tokens, attn_weight, *rest):
        width = tokens.shape[1]
        square = (
            n == sizes["head"]
            and n == 4
            and sizes["grp"] == 2
            and width == n * attn_weight.shape[1] == n * attn_weight.shape[2]
            and width == n * n * HEAD_DIM
            and n * tokens.shape[0] <= width // n
        )
        if square:
            return square_body(n, tokens, attn_weight, *rest)
        return general_body(tokens, attn_weight, *rest)

    return jax.shard_map(
        body,
        mesh=mesh,
        in_specs=(
            P(("grp", "seq"), None),
            P(None, "seq", "head"),
            P(),
            P(),
            P(("grp", "seq"), None),
            P(("grp", "seq"), None),
            P("seq", None, "head"),
            P("seq", None, "head"),
            P("seq", "head", None),
        ),
        out_specs=P(("grp", "seq"), None),
        check_vma=False,
    )
```

```python
import functools

import jax
import jax.numpy as jnp
from jax import lax
from jax.experimental import pallas as pl
from jax.experimental.pallas import tpu as pltpu
from jax.sharding import PartitionSpec as P

HEAD_DIM = 128
EXPERTS = 64
TOPK = 8
CAP = 18
EPS = 1e-06

PRECISE = lax.Precision.HIGHEST
BF16 = jnp.bfloat16
F32 = jnp.float32
ANY = pl.BlockSpec(memory_space=pl.ANY)
SMEM = pl.BlockSpec(memory_space=pltpu.SMEM)
VMEM = pl.BlockSpec(memory_space=pltpu.VMEM)
MIB = 1024 * 1024
SLOW = 10**10


def prefix_2(array, axis, combine, identity):
    peers, position = (lax.axis_size(axis), lax.axis_index(axis))
    everything = lax.all_gather(array.astype(jnp.bfloat16), axis)
    start = jnp.broadcast_to(jnp.asarray(identity, array.dtype), array.shape)

    def hop(k, before):
        reached = k < position
        new = combine(before, everything[k].astype(array.dtype))
        return jnp.where(reached, new, before)

    return lax.fori_loop(0, peers, hop, start)


def rms_scale(row_block, gain_vec):
    widened = row_block.astype(jnp.float32)
    factor = lax.rsqrt(jnp.mean(widened * widened, axis=-1, keepdims=True) + 1e-06)
    return widened * factor * gain_vec


def head_norm(outputs):
    return outputs * lax.rsqrt(jnp.mean(outputs * outputs, axis=-1, keepdims=True) + 1e-06)


def add_states(earlier, later):
    return earlier + later


def slot_numbers(route_flat):
    one_hot = (route_flat[:, None] == jnp.arange(EXPERTS, dtype=jnp.int32)[None, :]).astype(
        jnp.int32
    )
    earlier = jnp.cumsum(one_hot, axis=0) - one_hot
    return route_flat * CAP + jnp.sum(earlier * one_hot, axis=1)


def make_runner(expert_gate, expert_up, expert_down):

    def run_experts(received):
        gate_val = jnp.einsum(
            "necd,edf->necf", received, expert_gate, preferred_element_type=jnp.float32
        )
        up_val = jnp.einsum(
            "necd,edf->necf", received, expert_up, preferred_element_type=jnp.float32
        )
        hidden = (jax.nn.silu(gate_val) * up_val).astype(jnp.bfloat16)
        partial_value = jnp.einsum(
            "necf,efd->necd", hidden, expert_down, preferred_element_type=jnp.float32
        ).astype(jnp.bfloat16)
        groups = lax.axis_size("head")
        shape_now = partial_value.shape
        split = partial_value.reshape(
            shape_now[0], shape_now[1], shape_now[2], groups, shape_now[3] // groups
        )
        by_group = lax.all_to_all(split, "head", split_axis=3, concat_axis=3, tiled=True)
        summed = jnp.sum(by_group.astype(jnp.float32), axis=3)
        return lax.all_to_all(
            summed.astype(jnp.bfloat16), "seq", split_axis=0, concat_axis=0, tiled=True
        ).astype(summed.dtype)

    return run_experts


def general_body(
    tokens, attn_weight, attn_gain, moe_gain, routes, gates, expert_gate, expert_up, expert_down
):
    local_rows = tokens.shape[0]
    normed = rms_scale(tokens, attn_gain).astype(jnp.bfloat16)
    weights = lax.all_gather(attn_weight, "seq", axis=1, tiled=True)
    head_count = weights.shape[2] // HEAD_DIM
    projected = [
        jnp.dot(normed, weights[which], preferred_element_type=jnp.float32)
        .astype(jnp.bfloat16)
        .reshape(local_rows, head_count, HEAD_DIM)
        for which in range(3)
    ]
    query_rows, key_rows, value_rows = projected
    own_state = jnp.einsum("thd,the->hde", key_rows, value_rows, preferred_element_type=jnp.float32)
    prefix = prefix_2(own_state, "seq", add_states, jnp.zeros_like(own_state))
    inter_part = jnp.einsum(
        "thd,hde->the", query_rows.astype(jnp.float32), prefix, precision=PRECISE
    )
    scores = jnp.einsum("thd,shd->hts", query_rows, key_rows, preferred_element_type=jnp.float32)
    lower_mask = jnp.arange(local_rows)[:, None] >= jnp.arange(local_rows)[None, :]
    scores = jnp.where(lower_mask[None], scores, 0.0)
    intra_part = jnp.einsum(
        "hts,she->the", scores, value_rows.astype(jnp.float32), precision=PRECISE
    )
    attended = (
        head_norm(inter_part + intra_part)
        .reshape(local_rows, head_count * HEAD_DIM)
        .astype(jnp.bfloat16)
    )
    out_part = lax.dot_general(
        attended, weights[3], (((1,), (1,)), ((), ())), preferred_element_type=jnp.float32
    )
    residual = (
        tokens.astype(jnp.float32)
        + lax.psum(out_part.astype(jnp.bfloat16), "head").astype(jnp.float32)
    ).astype(jnp.bfloat16)
    moe_in = rms_scale(residual, moe_gain).astype(jnp.bfloat16)
    route_flat = routes.reshape(-1)
    slots = slot_numbers(route_flat)
    owners = lax.axis_size("seq")
    local_experts = expert_gate.shape[0]
    source_row = jnp.arange(route_flat.shape[0], dtype=jnp.int32) // TOPK
    run_experts = make_runner(expert_gate, expert_up, expert_down)
    outbound = (
        jnp.zeros((EXPERTS * CAP, moe_in.shape[1]), jnp.bfloat16).at[slots].set(moe_in[source_row])
    )
    outbound = outbound.reshape(owners, local_experts, CAP, moe_in.shape[1])
    returned = run_experts(lax.all_to_all(outbound, "seq", split_axis=0, concat_axis=0, tiled=True))
    arrived = returned.reshape(EXPERTS * CAP, -1)[slots].reshape(local_rows, TOPK, -1)
    moe_partial = jnp.einsum("tkd,tk->td", arrived, gates, precision=PRECISE)
    column_span = moe_partial.shape[1]
    residual_share = lax.dynamic_slice_in_dim(
        residual, lax.axis_index("head") * column_span, column_span, 1
    )
    mixed_share = (residual_share.astype(jnp.float32) + moe_partial).astype(jnp.bfloat16)
    return lax.all_gather(mixed_share, "head", axis=1, tiled=True)


def swap(array, axis, distance):
    size = lax.axis_size(axis)
    return lax.ppermute(array, axis, [(i, i ^ distance) for i in range(size)])


def run_copies(copies):
    for copy in copies:
        copy.start()
    for copy in copies:
        copy.wait()


def after(array, *earlier):
    return lax.optimization_barrier((array,) + earlier)[0]


def held(array):
    return pltpu.with_memory_space_constraint(array, pltpu.HBM)


def here(array):
    return pltpu.with_memory_space_constraint(array, pltpu.VMEM)


def in_step(*arrays):
    return lax.optimization_barrier(arrays)


def cut_kernel(pos, routes, gates, tokens, weight, x_send, *rest):
    w_sends, (r_here, g_here, sems) = rest[:-3], rest[-3:]
    g, s, h = pos[0], pos[1], pos[2]
    rows, cols, half = tokens.shape[0], x_send.shape[1], w_sends[0].shape[0]
    copies = [
        (
            tokens.at[:, pl.ds(pl.multiple_of(h * cols, cols), cols)],
            x_send.at[pl.ds(0, rows)],
        ),
        (routes, r_here),
        (gates, g_here),
    ]
    for which in range(3):
        span = pl.ds(which * HEAD_DIM, HEAD_DIM)
        for distance, out in enumerate(w_sends, 1):
            column = pl.multiple_of((s ^ distance) * HEAD_DIM, HEAD_DIM)
            own_half = pl.ds(pl.multiple_of(g * half, half), half)
            copies.append(
                (weight.at[which, own_half, pl.ds(column, HEAD_DIM)], out.at[:, span])
            )
    copies = [pltpu.make_async_copy(a, b, sems.at[i]) for i, (a, b) in enumerate(copies)]
    for copy in copies:
        copy.start()
    for copy in copies[1:3]:
        copy.wait()
    parts, left = [r_here[...].astype(F32)], g_here[...]
    for _ in range(3):
        parts.append(left.astype(BF16).astype(F32))
        left = left - parts[-1]
    lines = jnp.concatenate(parts, axis=1)
    lines = jnp.concatenate([lines, jnp.zeros_like(lines)], axis=0)
    blank = jnp.zeros((lines.shape[0], cols - lines.shape[1]), F32)
    if blank.shape[1]:
        lines = jnp.concatenate([lines, blank], axis=1)
    x_send[rows:, :] = lines.astype(BF16)
    for copy in copies[:1] + copies[3:]:
        copy.wait()


def attend_kernel(n, pos, gain, tokens, weight, *rest):
    x_pieces, rest = rest[:n], rest[n:]
    w_near, rest = rest[: n - 1], rest[n - 1 :]
    w_far, rest = rest[: n - 1], rest[n - 1 :]
    attended, (x_share, x_all, w_all, projected, sems) = rest[:n], rest[n:]
    g, s, h = pos[0], pos[1], pos[2]
    rows, width = tokens.shape
    cols = width // n
    depth, half = weight.shape[1], w_near[0].shape[0]
    total = n * rows

    def at_rows(block, size):
        return pl.ds(pl.multiple_of(block * size, size), size)

    copies = [(tokens, x_all.at[at_rows(s, rows)])]
    for d in range(1, n):
        for e in range(n):
            copies.append(
                (x_pieces[e].at[d - 1], x_all.at[at_rows(s ^ d, rows), at_rows(h ^ e, cols)])
            )
    n_rows = len(copies)
    for which in range(3):
        source = weight.at[which, :, at_rows(s, HEAD_DIM)]
        copies.append((source, w_all.at[at_rows(s, depth), pl.ds(which * HEAD_DIM, HEAD_DIM)]))
    for d in range(1, n):
        copies.append((w_near[d - 1], w_all.at[at_rows((s ^ d) * 2 + g, half)]))
        copies.append((w_far[d - 1], w_all.at[at_rows((s ^ d) * 2 + (1 - g), half)]))
    copies = [pltpu.make_async_copy(a, b, sems.at[i]) for i, (a, b) in enumerate(copies)]
    for copy in copies:
        copy.start()
    for copy in copies[:n_rows]:
        copy.wait()
    x_share[...] = x_all[at_rows(h, rows), at_rows(s, cols)]

    def normalise(block, carry):
        mine = at_rows(block, rows)
        wide = x_all[mine, :].astype(F32)
        factor = lax.rsqrt(jnp.mean(wide * wide, axis=-1, keepdims=True) + EPS)
        x_all[mine, :] = (wide * factor * gain[...]).astype(BF16)
        return carry

    lax.fori_loop(0, n, normalise, 0)
    for copy in copies[n_rows:]:
        copy.wait()
    projected[...] = jnp.dot(x_all[...], w_all[...], preferred_element_type=F32).astype(BF16)
    key, value = projected[:, HEAD_DIM : 2 * HEAD_DIM], projected[:, 2 * HEAD_DIM :]
    for e in range(n):
        block = h ^ e
        scores = lax.dot_general(
            projected[at_rows(block, rows), :HEAD_DIM],
            key,
            (((1,), (1,)), ((), ())),
            preferred_element_type=F32,
        )
        position = lax.broadcasted_iota(jnp.int32, scores.shape, 0) + block * rows
        scores = jnp.where(
            position >= lax.broadcasted_iota(jnp.int32, scores.shape, 1), scores, 0.0
        )
        high = scores.astype(BF16)
        low = (scores - high.astype(F32)).astype(BF16)
        out = jnp.dot(high, value, preferred_element_type=F32) + jnp.dot(
            low, value, preferred_element_type=F32
        )
        out = out * lax.rsqrt(jnp.mean(out * out, axis=-1, keepdims=True) + EPS)
        attended[e][...] = out.astype(BF16)


def bring_kernel(*refs):
    count = len(refs) // 2
    sems = refs[-1]
    copies = [pltpu.make_async_copy(refs[i], refs[count + i], sems.at[i]) for i in range(count)]
    for copy in copies:
        copy.start()
    for copy in copies:
        copy.wait()


def project_kernel(n, pos, x_share, *rest):
    weights, pieces, (out, a_all) = rest[:n], rest[n : 2 * n], rest[2 * n :]
    s = pos[1]
    total = x_share[...].astype(F32)
    for e in range(n):
        for d in range(n):
            span = pl.ds(pl.multiple_of((s ^ d) * HEAD_DIM, HEAD_DIM), HEAD_DIM)
            a_all[e, :, span] = pieces[d][e]
        total = total + lax.dot_general(
            a_all[e], weights[e][...], (((1,), (1,)), ((), ())), preferred_element_type=F32
        )
    out[...] = total.astype(BF16)


def route_kernel(n, experts, slots, pos, *refs):
    pieces, (pick, place, weight, table) = refs[:n], refs[n:]
    s = pos[1]
    rows = pieces[0].shape[0] - 2 * TOPK
    total = n * rows
    for d in range(n):
        lines = pieces[d][rows:, :].astype(F32)[:TOPK]
        gate = sum(lines[:, (1 + i) * rows : (2 + i) * rows] for i in range(3))
        span = pl.ds(pl.multiple_of((s ^ d) * rows, rows), rows)
        table[:, span] = jnp.concatenate([lines[:, :rows], gate], axis=0)
    first = (s * experts).astype(F32)
    names = lax.broadcasted_iota(jnp.int32, (experts, total), 0).astype(F32) + first
    member = jnp.zeros((experts, total), F32)
    gate = jnp.zeros((experts, total), F32)
    for k in range(TOPK):
        hit = table[k : k + 1, :] == names
        member = jnp.where(hit, 1.0, member)
        gate = jnp.where(hit, table[TOPK + k : TOPK + k + 1, :], gate)
    earlier = (
        lax.broadcasted_iota(jnp.int32, (total, total), 0)
        < lax.broadcasted_iota(jnp.int32, (total, total), 1)
    ).astype(F32).astype(BF16)
    rank = jnp.dot(member.astype(BF16), earlier, preferred_element_type=F32)
    slot = jnp.where(member > 0.0, rank, -1.0).astype(BF16)
    pairs = experts * slots
    expand = (
        lax.broadcasted_iota(jnp.int32, (experts, pairs), 1) // slots
        == lax.broadcasted_iota(jnp.int32, (experts, pairs), 0)
    ).astype(F32).astype(BF16)
    across = lax.dot_general(
        slot, expand, (((0,), (0,)), ((), ())), preferred_element_type=F32
    )
    number = (lax.broadcasted_iota(jnp.int32, (total, pairs), 1) % slots).astype(F32)
    place[...] = jnp.where(across == number, 1.0, 0.0).astype(BF16)
    for e in range(experts):
        span = pl.ds(e * slots, slots)
        number = lax.broadcasted_iota(jnp.int32, (slots, total), 0).astype(F32)
        hit = number == slot[e : e + 1, :].astype(F32)
        pick[span, :] = jnp.where(hit, 1.0, 0.0).astype(BF16)
        chosen = jnp.sum(jnp.where(hit, gate[e : e + 1, :], 0.0), axis=1, keepdims=True)
        weight[span, :] = jnp.broadcast_to(chosen, (slots, weight.shape[1]))


def span(block, size):
    return pl.ds(pl.multiple_of(block * size, size), size)


def weight_copies(pos, distances, i, group, ins, outs, sems, first=0):
    source_part, part = pl.ds(first + i * group, group), pl.ds(i * group, group)
    cols = outs[0].shape[1] // len(distances)
    copies = []
    for k, distance in enumerate(distances):
        for which, (w, kept) in enumerate(zip(ins, outs)):
            source = w.at[source_part, span(pos[1] ^ distance, cols), :]
            target = kept.at[part, pl.ds(k * cols, cols), :]
            copies.append(pltpu.make_async_copy(source, target, sems.at[i, 2 * k + which]))
    return copies


def down_copies(pos, distances, i, group, w_down, outs, sems):
    part, cols = pl.ds(i * group, group), outs[0].shape[2]
    copies = []
    for k, (distance, kept) in enumerate(zip(distances, outs)):
        source = w_down.at[part, :, span(pos[2] ^ distance, cols)]
        copies.append(pltpu.make_async_copy(source, kept.at[part], sems.at[i, k]))
    return copies


def load_down_kernel(group, distances, pos, w_down, *refs):
    outs, sems = refs[:-1], refs[-1]
    copies = []
    for i in range(outs[0].shape[0] // group):
        copies += down_copies(pos, distances, i, group, w_down, outs, sems)
    for copy in copies:
        copy.start()
    for copy in copies:
        copy.wait()


def load_kernel(group, distances, pos, w_gate, w_up, g_all, u_all, sems):
    copies = []
    for i in range(g_all.shape[0] // group):
        copies += weight_copies(
            pos, distances, i, group, (w_gate, w_up), (g_all, u_all), sems
        )
    for copy in copies:
        copy.start()
    for copy in copies:
        copy.wait()


def place_rows(n, distances, pos, pieces, r_all):
    rows, cols = pieces[0][0].shape
    for k in range(len(distances)):
        for e in range(n):
            r_all[span(pos[2] ^ e, rows), k * cols : (k + 1) * cols] = pieces[k][e][...]


def gather_rows(distances, pos, gain, picked, r_all, square):
    cols = r_all.shape[1] // len(distances)
    scaled = []
    for k, distance in enumerate(distances):
        taken = jnp.dot(picked, r_all[:, k * cols : (k + 1) * cols], preferred_element_type=F32)
        square = square + jnp.sum(taken * taken, axis=1, keepdims=True)
        scaled.append((taken * gain[:, span(pos[1] ^ distance, cols)]).astype(BF16))
    return scaled, square


def first_hidden_kernel(n, slots, group, distances, pos, gain, pick, g_all, u_all, *refs):
    pieces = [refs[k * n : (k + 1) * n] for k in range(len(distances))]
    total_out, square_out, r_all, x_slots = refs[n * len(distances) :]
    experts, wide, hidden = g_all.shape
    place_rows(n, distances, pos, pieces, r_all)
    for i in range(experts // group):
        part = slice(i * group * slots, (i + 1) * group * slots)
        scaled, square = gather_rows(distances, pos, gain, pick[part, :], r_all, 0.0)
        for k, value in enumerate(scaled):
            x_slots[part, k * value.shape[1] : (k + 1) * value.shape[1]] = value
        square_out[part, :] = jnp.broadcast_to(square, (group * slots, square_out.shape[1]))
    for e in range(experts):
        mine = slice(e * slots, (e + 1) * slots)
        total_out[mine, :hidden] = jnp.dot(x_slots[mine, :], g_all[e], preferred_element_type=F32)
        total_out[mine, hidden:] = jnp.dot(x_slots[mine, :], u_all[e], preferred_element_type=F32)


def last_hidden_kernel(
    n, slots, group, distances, downs, pos, gain, pick, w_gate, w_up, w_down, g_some, u_some,
    total_in, square_in, weight, *refs,
):
    pieces = [refs[k * n : (k + 1) * n] for k in range(len(distances))]
    hidden_out, *refs = refs[n * len(distances) :]
    d_outs, (r_all, x_slots, g_all, u_all, sems, d_sems) = refs[: len(downs)], refs[len(downs) :]
    some, wide, hidden = g_some.shape
    ready, parts = some // group, (some + g_all.shape[0]) // group
    width = n * wide // len(distances)

    def copies(i):
        return weight_copies(
            pos, distances, i, group, (w_gate, w_up), (g_all, u_all), sems, first=some
        )

    def start(i, carry):
        for copy in copies(i):
            copy.start()
        return carry

    def d_copies(i):
        return down_copies(pos, downs, i, group, w_down, d_outs, d_sems)

    def start_down(i, carry):
        for copy in d_copies(i):
            copy.start()
        return carry

    def step(g_from, u_from, skipped, i, carry):
        part = span(i, group * slots)
        scaled, square = gather_rows(
            distances, pos, gain, pick[part, :], r_all, square_in[part, :1]
        )
        for k, value in enumerate(scaled):
            x_slots[:, k * value.shape[1] : (k + 1) * value.shape[1]] = value
        scale = lax.rsqrt(square / width + EPS)
        if skipped:
            for copy in copies(i - skipped):
                copy.wait()
        for e in range(group):
            inner = slice(e * slots, (e + 1) * slots)
            mine = pl.ds(pl.multiple_of(i * group * slots + e * slots, slots), slots)
            taken = x_slots[inner, :]
            gate_val = jnp.dot(taken, g_from[(i - skipped) * group + e], preferred_element_type=F32)
            up_val = jnp.dot(taken, u_from[(i - skipped) * group + e], preferred_element_type=F32)
            gate_val = (gate_val + total_in[mine, :hidden]) * scale[inner]
            up_val = (up_val + total_in[mine, hidden:]) * scale[inner]
            value = gate_val * jax.nn.sigmoid(gate_val) * (up_val * weight[mine, :1])
            hidden_out[mine, :] = value.astype(BF16)
        return carry

    lax.fori_loop(0, parts - ready, start, 0)
    lax.fori_loop(0, parts, start_down, 0)
    place_rows(n, distances, pos, pieces, r_all)
    lax.fori_loop(0, ready, functools.partial(step, g_some, u_some, 0), 0)
    lax.fori_loop(ready, parts, functools.partial(step, g_all, u_all, ready), 0)
    for i in range(parts):
        for copy in d_copies(i):
            copy.wait()


def self_down_kernel(slots, group, distances, pos, hidden, place, w_down, out, kept, y_slots, sems):
    copies = [
        down_copies(pos, distances, i, group, w_down, (kept,), sems)[0]
        for i in range(kept.shape[0] // group)
    ]
    for copy in copies:
        copy.start()

    def step(i, carry):
        down_copies(pos, distances, i, group, w_down, (kept,), sems)[0].wait()
        for e in range(group):
            mine = pl.ds(pl.multiple_of(i * group * slots + e * slots, slots), slots)
            product = jnp.dot(hidden[mine, :], kept[i * group + e], preferred_element_type=F32)
            y_slots[mine, :] = product.astype(BF16)
        return carry

    lax.fori_loop(0, len(copies), step, 0)
    out[...] = jnp.dot(place[...], y_slots[...], preferred_element_type=F32).astype(BF16)


def down_kernel(slots, pos, hidden, place, *refs):
    count = len(refs) // 2
    for kept, out in zip(refs[:count], refs[count:]):
        y_slots = refs[-1]
        for e in range(kept.shape[0]):
            mine = slice(e * slots, (e + 1) * slots)
            product = jnp.dot(hidden[mine, :], kept[e], preferred_element_type=F32)
            y_slots[mine, :] = product.astype(BF16)
        out[...] = jnp.dot(place[...], y_slots[...], preferred_element_type=F32).astype(BF16)


def add_kernel(distances, pos, base, core, part, *outs):
    s = pos[1]
    rows = outs[0].shape[0]
    in_half = part.shape[0] // rows
    for d, out in zip(distances, outs):
        block = s ^ d
        everywhere = pl.ds(pl.multiple_of(block * rows, rows), rows)
        inside = pl.ds(pl.multiple_of(block % in_half * rows, rows), rows)
        value = base[everywhere, :].astype(F32) + core[everywhere, :].astype(F32)
        out[...] = (value + part[inside, :].astype(F32)).astype(out.dtype)


def halves_kernel(pos, base, core, far, near):
    rows = near.shape[0]
    blocks = base.shape[0] // rows
    mine = pos[1] // blocks
    for half, out in ((blocks - 1 - mine, far), (mine, near)):
        value = base[span(half, rows), :].astype(F32) + core[span(half, rows), :].astype(F32)
        out[...] = value.astype(out.dtype)


def square_body(
    n, tokens, attn_weight, attn_gain, moe_gain, routes, gates, expert_gate, expert_up, expert_down
):
    g, s, h = (lax.axis_index(axis) for axis in ("grp", "seq", "head"))
    pos = jnp.stack([g, s, h]).astype(jnp.int32)
    rows, width = tokens.shape
    cols = width // n
    depth = attn_weight.shape[1]
    half = depth // 2
    experts, _, hidden = expert_gate.shape
    total = n * rows
    slots = -(-n * CAP // 16) * 16
    pairs = experts * slots
    sds = jax.ShapeDtypeStruct
    dma = pltpu.SemaphoreType.DMA

    def room(mib):
        return pltpu.CompilerParams(vmem_limit_bytes=mib * MIB)

    def cost(macs, size):
        return pl.CostEstimate(flops=2 * macs, bytes_accessed=size, transcendentals=0)

    def plus(*terms):
        total_value = terms[0].astype(F32)
        for term in terms[1:]:
            total_value = total_value + term.astype(F32)
        return total_value

    lines = 2 * TOPK
    with jax.named_scope("cut_pieces"):
        x_send, *w_sends = pl.pallas_call(
            cut_kernel,
            out_shape=[sds((rows + lines, cols), BF16)]
            + [sds((half, 3 * HEAD_DIM), BF16)] * (n - 1),
            in_specs=[SMEM] + [ANY] * 4,
            out_specs=[VMEM] * n,
            scratch_shapes=[
                pltpu.VMEM((TOPK, rows), jnp.int32),
                pltpu.VMEM((TOPK, rows), F32),
                dma((3 + 3 * (n - 1),)),
            ],
            compiler_params=room(8),
        )(pos, *map(held, (routes.T, gates.T, tokens, attn_weight)))
    group = experts // 4
    w_gate, w_up, w_down = map(held, (expert_gate, expert_up, expert_down))

    early, late = tuple(range(n // 2)), tuple(range(n // 2, n))
    wide = n // 2 * cols
    ahead = experts // 2
    hidden_cost = cost(pairs * wide * (total + 2 * hidden), 4 * experts * wide * hidden)

    def load(distances, amount, *earlier):
        return pl.pallas_call(
            functools.partial(load_kernel, group, distances),
            out_shape=[pltpu.VMEM((amount, wide, hidden), BF16)] * 2,
            in_specs=[SMEM] + [ANY] * 2,
            out_specs=[VMEM] * 2,
            scratch_shapes=[dma((amount // group, 2 * len(distances)))],
            compiler_params=room(2),
            cost_estimate=cost(0, 4 * amount * wide * hidden),
        )(after(pos, *earlier), w_gate, w_up)

    def load_down(distances, *earlier):
        count = len(distances)
        return pl.pallas_call(
            functools.partial(load_down_kernel, group, distances),
            out_shape=[pltpu.VMEM((experts, hidden, cols), BF16)] * count,
            in_specs=[SMEM, ANY],
            out_specs=[VMEM] * count,
            scratch_shapes=[dma((experts // group, count))],
            compiler_params=room(2),
            cost_estimate=cost(0, 2 * count * experts * cols * hidden),
        )(after(pos, *earlier), w_down)

    with jax.named_scope("gather_tokens_and_weights"):
        x_far = [swap(x_send, "seq", d) for d in range(1, n)]
        w_near = [swap(w_sends[d - 1], "seq", d) for d in range(1, n - 1)]
        step = in_step(*x_far, *w_near, w_sends[-1])
        x_far, w_near, w_last = step[: n - 1], list(step[n - 1 : -1]), step[-1]
        x_pieces = {0: jnp.stack([x[:rows] for x in x_far])}
        x_pieces[2] = swap(x_pieces[0], "head", 2)
        w_far = [swap(w, "grp", 1) for w in w_near]
        w_near.append(swap(w_last, "seq", n - 1))
        x_pieces[2], w_near[-1], *w_far = in_step(x_pieces[2], w_near[-1], *w_far)
        w_far.append(swap(w_near[-1], "grp", 1))
        for e in (0, 2):
            x_pieces[e ^ 1] = swap(x_pieces[e], "head", 1)
    with jax.named_scope("routing"):
        pick, place, weight = pl.pallas_call(
            functools.partial(route_kernel, n, experts, slots),
            out_shape=[sds((pairs, total), BF16), sds((total, pairs), BF16), sds((pairs, 128), F32)],
            in_specs=[SMEM] + [VMEM] * n,
            out_specs=[VMEM] * 3,
            scratch_shapes=[pltpu.VMEM((2 * TOPK, total), F32)],
            compiler_params=room(16),
        )(pos, x_send, *x_far)
        with jax.named_scope("expert_weights"):
            late_weights = load(late, ahead, w_near[-1])
        w_near[-1] = after(w_near[-1], pick, late_weights[0])
        o_own = after(attn_weight, pick)[3]
        o_pieces = {0: o_own, 2: swap(o_own, "head", 2)}

    with jax.named_scope("attention"):
        *attended, x_share = pl.pallas_call(
            functools.partial(attend_kernel, n),
            out_shape=[sds((rows, HEAD_DIM), BF16)] * n + [sds((rows, cols), BF16)],
            in_specs=[SMEM, VMEM] + [ANY] * (2 + n + 2 * (n - 1) - 1) + [VMEM],
            out_specs=[VMEM] * (n + 1),
            scratch_shapes=[
                pltpu.VMEM((total, width), BF16),
                pltpu.VMEM((width, 3 * HEAD_DIM), BF16),
                pltpu.VMEM((total, 3 * HEAD_DIM), BF16),
                dma((4 + n * (n - 1) + 2 * (n - 1),)),
            ],
            compiler_params=room(14),
        )(
            pos, attn_gain.reshape(1, width), held(tokens), held(attn_weight),
            *[held(x_pieces[e]) for e in range(n)], *map(held, w_near), *map(held, w_far[:-1]), w_far[-1],
        )

    gain_row = moe_gain.reshape(1, width)

    def first_hidden(pieces, weights):
        return pl.pallas_call(
            functools.partial(first_hidden_kernel, n, slots, group, early),
            out_shape=[sds((pairs, 2 * hidden), F32), sds((pairs, 128), F32)],
            in_specs=[SMEM] + [VMEM] * (4 + n * len(early)),
            out_specs=[VMEM] * 2,
            scratch_shapes=[pltpu.VMEM((total, wide), BF16), pltpu.VMEM((pairs, wide), BF16)],
            compiler_params=room(12),
            cost_estimate=hidden_cost,
        )(pos, gain_row, pick, *map(here, weights), *pieces)

    def last_hidden(pieces, weights, state, downs):
        return pl.pallas_call(
            functools.partial(last_hidden_kernel, n, slots, group, late, downs),
            out_shape=[sds((pairs, hidden), BF16)]
            + [pltpu.VMEM((experts, hidden, cols), BF16)] * len(downs),
            in_specs=[SMEM] + [VMEM] * 2 + [ANY] * 3 + [VMEM] * (5 + n * len(late)),
            out_specs=[VMEM] * (1 + len(downs)),
            scratch_shapes=[pltpu.VMEM((total, wide), BF16), pltpu.VMEM((group * slots, wide), BF16)]
            + [pltpu.VMEM((experts - ahead, wide, hidden), BF16)] * 2
            + [dma(((experts - ahead) // group, 2 * len(late)))]
            + [dma((experts // group, len(downs)))],
            compiler_params=room(16),
            cost_estimate=hidden_cost,
        )(
            pos, gain_row, pick, w_gate, w_up, w_down, *map(here, weights), *state, weight, *pieces
        )

    with jax.named_scope("heads_to_tokens"):
        for e in (0, 2):
            o_pieces[e ^ 1] = swap(after(o_pieces[e], attended[0]), "head", 1)
        arrived = jnp.stack([attended[0]] + [swap(attended[e], "head", e) for e in range(1, n)])
        a_pieces = [arrived, swap(arrived, "seq", 1), swap(arrived, "seq", 2)]
        with jax.named_scope("expert_weights"):
            early_weights = load(early, experts, arrived)
        a_pieces[2] = after(a_pieces[2], early_weights[0])
        a_pieces.append(swap(a_pieces[2], "seq", 1))
        with jax.named_scope("expert_weights"):
            (d_2,) = load_down((2,), a_pieces[2])
        x_share = after(x_share, d_2)

    with jax.named_scope("bring_out_weights"):
        o_here = pl.pallas_call(
            bring_kernel,
            out_shape=[pltpu.VMEM((depth, cols), BF16)] * n,
            in_specs=[ANY] * n,
            out_specs=[VMEM] * n,
            scratch_shapes=[dma((n,))],
            compiler_params=room(2),
            cost_estimate=cost(0, 2 * n * depth * cols),
        )(*[o_pieces[e] for e in range(n)])
    with jax.named_scope("output_projection"):
        residual = pl.pallas_call(
            functools.partial(project_kernel, n),
            out_shape=sds((rows, cols), BF16),
            in_specs=[SMEM] + [VMEM] * (1 + 2 * n),
            out_specs=VMEM,
            scratch_shapes=[pltpu.VMEM((n, rows, n * HEAD_DIM), BF16)],
            compiler_params=room(12),
        )(pos, x_share, *map(here, o_here), *a_pieces)

    with jax.named_scope("gather_residual"):
        r_pieces = {0: {0: residual}}
        for d in (1, 2):
            r_pieces[d] = {0: swap(residual, "seq", d)}
        r_pieces[3] = {0: swap(r_pieces[2][0], "seq", 1)}
        for d in range(n):
            r_pieces[d][2] = swap(r_pieces[d][0], "head", 2)
            r_pieces[d][1] = swap(r_pieces[d][0], "head", 1)
        for d in early:
            r_pieces[d][3] = swap(r_pieces[d][2], "head", 1)
        r_pieces[0][0] = after(residual, r_pieces[3][0], r_pieces[2][2])
        pieces = [r_pieces[d][e] for d in early for e in range(n)]
        with jax.named_scope("first_hidden_units"):
            state = first_hidden(pieces, early_weights)
        for d in late:
            r_pieces[d][3] = swap(after(r_pieces[d][2], state[1]), "head", 1)
        pieces = [r_pieces[d][e] for d in late for e in range(n)]
        with jax.named_scope("last_hidden_units"):
            units, d_3, d_1 = last_hidden(pieces, late_weights, state, (3, 1))
        r_choices = [r_pieces[d][d] for d in range(n)]
    def down(units, *weights):
        count = len(weights)
        with jax.named_scope("down_products"):
            return pl.pallas_call(
                functools.partial(down_kernel, slots),
                out_shape=[sds((total, cols), BF16)] * count,
                in_specs=[SMEM] + [VMEM] * (2 + count),
                out_specs=[VMEM] * count,
                scratch_shapes=[pltpu.VMEM((pairs, cols), BF16)],
                compiler_params=room(6),
                cost_estimate=cost(
                    count * pairs * cols * (total + hidden), 2 * count * experts * cols * hidden
                ),
            )(pos, units, place, *map(here, weights))

    def self_down(units, distance):
        with jax.named_scope("down_products_alone"):
            return pl.pallas_call(
                functools.partial(self_down_kernel, slots, group, (distance,)),
                out_shape=sds((total, cols), BF16),
                in_specs=[SMEM] + [VMEM] * 2 + [ANY],
                out_specs=VMEM,
                scratch_shapes=[
                    pltpu.VMEM((experts, hidden, cols), BF16),
                    pltpu.VMEM((pairs, cols), BF16),
                    dma((experts // group, 1)),
                ],
                compiler_params=room(9),
                cost_estimate=cost(pairs * cols * (total + hidden), 2 * experts * cols * hidden),
            )(pos, units, place, w_down)

    with jax.named_scope("sum_over_devices"):
        half_line = n // 2
        out_3, out_1 = down(units, d_3, d_1)
        core_2, core_0 = swap(out_3, "head", 1), swap(out_1, "head", 1)
        (out_2,) = down(after(units, out_3), d_2)
        with jax.named_scope("halves_over_cores"):
            near = pl.pallas_call(
                halves_kernel,
                out_shape=[sds((half_line * rows, cols), BF16)] * 2,
                in_specs=[SMEM] + [VMEM] * 2,
                out_specs=[VMEM] * 2,
                compiler_params=room(4),
                cost_estimate=cost(0, 4 * total * cols),
            )(pos, out_2, core_2)
        far = [swap(part, "head", 2) for part in near]
        out_0 = self_down(after(units, *near), 0)

        def add_parts(scope, distances, part, macs):
            with jax.named_scope(scope):
                return pl.pallas_call(
                    functools.partial(add_kernel, distances),
                    out_shape=[sds((rows, cols), BF16 if d else F32) for d in distances],
                    in_specs=[SMEM] + [VMEM] * 3,
                    out_specs=[VMEM] * len(distances),
                    compiler_params=room(4),
                    cost_estimate=cost(macs, 4 * part.size),
                )(pos, out_0, core_0, part)

        far_line = tuple(range(half_line, n))
        near_line = tuple(range(half_line))
        far_sums = add_parts("far_half_rows", far_line, far[0], 0)
        from_far = [swap(part, "seq", d) for d, part in zip(far_line, far_sums)]
        own_sum, *near_sums = add_parts("near_half_rows", near_line, far[1], SLOW)
        from_near = [swap(part, "seq", d) for d, part in zip(near_line[1:], near_sums)]
        mixed = plus(lax.select_n(s ^ h, *in_step(*r_choices, own_sum)[:n]), own_sum, *from_far)
        mixed = plus(*in_step(mixed, *from_near))
        mixed = mixed.astype(BF16)
    with jax.named_scope("gather_columns"):
        return lax.all_gather(mixed, "head", axis=1, tiled=True)


def solution(mesh):
    sizes = dict(mesh.shape)
    n = sizes["seq"]

    def body(tokens, attn_weight, *rest):
        width = tokens.shape[1]
        square = (
            n == sizes["head"]
            and n == 4
            and sizes["grp"] == 2
            and width == n * attn_weight.shape[1] == n * attn_weight.shape[2]
            and width == n * n * HEAD_DIM
            and n * tokens.shape[0] <= width // n
        )
        if square:
            return square_body(n, tokens, attn_weight, *rest)
        return general_body(tokens, attn_weight, *rest)

    return jax.shard_map(
        body,
        mesh=mesh,
        in_specs=(
            P(("grp", "seq"), None),
            P(None, "seq", "head"),
            P(),
            P(),
            P(("grp", "seq"), None),
            P(("grp", "seq"), None),
            P("seq", None, "head"),
            P("seq", None, "head"),
            P("seq", "head", None),
        ),
        out_specs=P(("grp", "seq"), None),
        check_vma=False,
    )
```

```python
import functools

import jax
import jax.numpy as jnp
from jax import lax
from jax.experimental import pallas as pl
from jax.experimental.pallas import tpu as pltpu
from jax.sharding import PartitionSpec as P

HEAD_DIM = 128
EXPERTS = 64
TOPK = 8
CAP = 18
EPS = 1e-06

PRECISE = lax.Precision.HIGHEST
BF16 = jnp.bfloat16
F32 = jnp.float32
ANY = pl.BlockSpec(memory_space=pl.ANY)
SMEM = pl.BlockSpec(memory_space=pltpu.SMEM)
VMEM = pl.BlockSpec(memory_space=pltpu.VMEM)
MIB = 1024 * 1024
SLOW = 10**10


def prefix_2(array, axis, combine, identity):
    peers, position = (lax.axis_size(axis), lax.axis_index(axis))
    everything = lax.all_gather(array.astype(jnp.bfloat16), axis)
    start = jnp.broadcast_to(jnp.asarray(identity, array.dtype), array.shape)

    def hop(k, before):
        reached = k < position
        new = combine(before, everything[k].astype(array.dtype))
        return jnp.where(reached, new, before)

    return lax.fori_loop(0, peers, hop, start)


def rms_scale(row_block, gain_vec):
    widened = row_block.astype(jnp.float32)
    factor = lax.rsqrt(jnp.mean(widened * widened, axis=-1, keepdims=True) + 1e-06)
    return widened * factor * gain_vec


def head_norm(outputs):
    return outputs * lax.rsqrt(jnp.mean(outputs * outputs, axis=-1, keepdims=True) + 1e-06)


def add_states(earlier, later):
    return earlier + later


def slot_numbers(route_flat):
    one_hot = (route_flat[:, None] == jnp.arange(EXPERTS, dtype=jnp.int32)[None, :]).astype(
        jnp.int32
    )
    earlier = jnp.cumsum(one_hot, axis=0) - one_hot
    return route_flat * CAP + jnp.sum(earlier * one_hot, axis=1)


def make_runner(expert_gate, expert_up, expert_down):

    def run_experts(received):
        gate_val = jnp.einsum(
            "necd,edf->necf", received, expert_gate, preferred_element_type=jnp.float32
        )
        up_val = jnp.einsum(
            "necd,edf->necf", received, expert_up, preferred_element_type=jnp.float32
        )
        hidden = (jax.nn.silu(gate_val) * up_val).astype(jnp.bfloat16)
        partial_value = jnp.einsum(
            "necf,efd->necd", hidden, expert_down, preferred_element_type=jnp.float32
        ).astype(jnp.bfloat16)
        groups = lax.axis_size("head")
        shape_now = partial_value.shape
        split = partial_value.reshape(
            shape_now[0], shape_now[1], shape_now[2], groups, shape_now[3] // groups
        )
        by_group = lax.all_to_all(split, "head", split_axis=3, concat_axis=3, tiled=True)
        summed = jnp.sum(by_group.astype(jnp.float32), axis=3)
        return lax.all_to_all(
            summed.astype(jnp.bfloat16), "seq", split_axis=0, concat_axis=0, tiled=True
        ).astype(summed.dtype)

    return run_experts


def general_body(
    tokens, attn_weight, attn_gain, moe_gain, routes, gates, expert_gate, expert_up, expert_down
):
    local_rows = tokens.shape[0]
    normed = rms_scale(tokens, attn_gain).astype(jnp.bfloat16)
    weights = lax.all_gather(attn_weight, "seq", axis=1, tiled=True)
    head_count = weights.shape[2] // HEAD_DIM
    projected = [
        jnp.dot(normed, weights[which], preferred_element_type=jnp.float32)
        .astype(jnp.bfloat16)
        .reshape(local_rows, head_count, HEAD_DIM)
        for which in range(3)
    ]
    query_rows, key_rows, value_rows = projected
    own_state = jnp.einsum("thd,the->hde", key_rows, value_rows, preferred_element_type=jnp.float32)
    prefix = prefix_2(own_state, "seq", add_states, jnp.zeros_like(own_state))
    inter_part = jnp.einsum(
        "thd,hde->the", query_rows.astype(jnp.float32), prefix, precision=PRECISE
    )
    scores = jnp.einsum("thd,shd->hts", query_rows, key_rows, preferred_element_type=jnp.float32)
    lower_mask = jnp.arange(local_rows)[:, None] >= jnp.arange(local_rows)[None, :]
    scores = jnp.where(lower_mask[None], scores, 0.0)
    intra_part = jnp.einsum(
        "hts,she->the", scores, value_rows.astype(jnp.float32), precision=PRECISE
    )
    attended = (
        head_norm(inter_part + intra_part)
        .reshape(local_rows, head_count * HEAD_DIM)
        .astype(jnp.bfloat16)
    )
    out_part = lax.dot_general(
        attended, weights[3], (((1,), (1,)), ((), ())), preferred_element_type=jnp.float32
    )
    residual = (
        tokens.astype(jnp.float32)
        + lax.psum(out_part.astype(jnp.bfloat16), "head").astype(jnp.float32)
    ).astype(jnp.bfloat16)
    moe_in = rms_scale(residual, moe_gain).astype(jnp.bfloat16)
    route_flat = routes.reshape(-1)
    slots = slot_numbers(route_flat)
    owners = lax.axis_size("seq")
    local_experts = expert_gate.shape[0]
    source_row = jnp.arange(route_flat.shape[0], dtype=jnp.int32) // TOPK
    run_experts = make_runner(expert_gate, expert_up, expert_down)
    outbound = (
        jnp.zeros((EXPERTS * CAP, moe_in.shape[1]), jnp.bfloat16).at[slots].set(moe_in[source_row])
    )
    outbound = outbound.reshape(owners, local_experts, CAP, moe_in.shape[1])
    returned = run_experts(lax.all_to_all(outbound, "seq", split_axis=0, concat_axis=0, tiled=True))
    arrived = returned.reshape(EXPERTS * CAP, -1)[slots].reshape(local_rows, TOPK, -1)
    moe_partial = jnp.einsum("tkd,tk->td", arrived, gates, precision=PRECISE)
    column_span = moe_partial.shape[1]
    residual_share = lax.dynamic_slice_in_dim(
        residual, lax.axis_index("head") * column_span, column_span, 1
    )
    mixed_share = (residual_share.astype(jnp.float32) + moe_partial).astype(jnp.bfloat16)
    return lax.all_gather(mixed_share, "head", axis=1, tiled=True)


def swap(array, axis, distance):
    size = lax.axis_size(axis)
    return lax.ppermute(array, axis, [(i, i ^ distance) for i in range(size)])


def run_copies(copies):
    for copy in copies:
        copy.start()
    for copy in copies:
        copy.wait()


def after(array, *earlier):
    return lax.optimization_barrier((array,) + earlier)[0]


def held(array):
    return pltpu.with_memory_space_constraint(array, pltpu.HBM)


def here(array):
    return pltpu.with_memory_space_constraint(array, pltpu.VMEM)


def in_step(*arrays):
    return lax.optimization_barrier(arrays)


def cut_kernel(pos, routes, gates, tokens, weight, x_send, *rest):
    w_sends, (r_here, g_here, sems) = rest[:-3], rest[-3:]
    g, s, h = pos[0], pos[1], pos[2]
    rows, cols, half = tokens.shape[0], x_send.shape[1], w_sends[0].shape[0]
    copies = [
        (
            tokens.at[:, pl.ds(pl.multiple_of(h * cols, cols), cols)],
            x_send.at[pl.ds(0, rows)],
        ),
        (routes, r_here),
        (gates, g_here),
    ]
    for which in range(3):
        span = pl.ds(which * HEAD_DIM, HEAD_DIM)
        for distance, out in enumerate(w_sends, 1):
            column = pl.multiple_of((s ^ distance) * HEAD_DIM, HEAD_DIM)
            own_half = pl.ds(pl.multiple_of(g * half, half), half)
            copies.append(
                (weight.at[which, own_half, pl.ds(column, HEAD_DIM)], out.at[:, span])
            )
    copies = [pltpu.make_async_copy(a, b, sems.at[i]) for i, (a, b) in enumerate(copies)]
    for copy in copies:
        copy.start()
    for copy in copies[1:3]:
        copy.wait()
    parts, left = [r_here[...].astype(F32)], g_here[...]
    for _ in range(3):
        parts.append(left.astype(BF16).astype(F32))
        left = left - parts[-1]
    lines = jnp.concatenate(parts, axis=1)
    lines = jnp.concatenate([lines, jnp.zeros_like(lines)], axis=0)
    blank = jnp.zeros((lines.shape[0], cols - lines.shape[1]), F32)
    if blank.shape[1]:
        lines = jnp.concatenate([lines, blank], axis=1)
    x_send[rows:, :] = lines.astype(BF16)
    for copy in copies[:1] + copies[3:]:
        copy.wait()


def project_tokens_kernel(n, pos, gain, tokens, weight, *rest):
    x_pieces, w_near, w_far = rest[:n], rest[n : 2 * n - 1], rest[2 * n - 1 : 3 * n - 3]
    partial, x_last, x_share, x_all, w_all, x_sems, w_sems = rest[3 * n - 3 :]
    g, s, h = pos[0], pos[1], pos[2]
    rows, width = tokens.shape
    cols = width // n
    depth, half = weight.shape[1], w_near[0].shape[0]
    missing = (s ^ (n - 1)) * 2 + (1 - g)
    x_copies = [(tokens, x_all.at[span(s, rows)])]
    for d in range(1, n):
        for e in range(n):
            target = x_all.at[span(s ^ d, rows), span(h ^ e, cols)]
            x_copies.append((x_pieces[e].at[d - 1], target))
    w_copies = []
    for which in range(3):
        target = w_all.at[span(s, depth), pl.ds(which * HEAD_DIM, HEAD_DIM)]
        w_copies.append((weight.at[which, :, span(s, HEAD_DIM)], target))
    for d in range(1, n):
        w_copies.append((w_near[d - 1], w_all.at[span((s ^ d) * 2 + g, half)]))
        if d < n - 1:
            w_copies.append((w_far[d - 1], w_all.at[span((s ^ d) * 2 + (1 - g), half)]))
    x_copies = [
        pltpu.make_async_copy(a, b, x_sems.at[i]) for i, (a, b) in enumerate(x_copies)
    ]
    w_copies = [
        pltpu.make_async_copy(a, b, w_sems.at[i]) for i, (a, b) in enumerate(w_copies)
    ]
    for copy in x_copies + w_copies:
        copy.start()
    w_all[span(missing, half), :] = jnp.zeros((half, w_all.shape[1]), BF16)
    for copy in x_copies:
        copy.wait()
    x_share[...] = x_all[span(h, rows), span(s, cols)]

    def normalise(block, carry):
        mine = span(block, rows)
        wide = x_all[mine, :].astype(F32)
        factor = lax.rsqrt(jnp.mean(wide * wide, axis=-1, keepdims=True) + EPS)
        x_all[mine, :] = (wide * factor * gain[...]).astype(BF16)
        return carry

    lax.fori_loop(0, n, normalise, 0)
    x_last[...] = x_all[:, span(missing, half)]
    for copy in w_copies:
        copy.wait()
    partial[...] = jnp.dot(x_all[...], w_all[...], preferred_element_type=F32)


def attend_kernel(n, pos, partial, x_last, w_last, *rest):
    attended, projected = rest[:n], rest[n]
    h = pos[2]
    rows = x_last.shape[0] // n
    projected[...] = (
        partial[...] + jnp.dot(x_last[...], w_last[...], preferred_element_type=F32)
    ).astype(BF16)
    key, value = projected[:, HEAD_DIM : 2 * HEAD_DIM], projected[:, 2 * HEAD_DIM :]
    for e in range(n):
        block = h ^ e
        scores = lax.dot_general(
            projected[span(block, rows), :HEAD_DIM],
            key,
            (((1,), (1,)), ((), ())),
            preferred_element_type=F32,
        )
        position = lax.broadcasted_iota(jnp.int32, scores.shape, 0) + block * rows
        scores = jnp.where(
            position >= lax.broadcasted_iota(jnp.int32, scores.shape, 1), scores, 0.0
        )
        high = scores.astype(BF16)
        low = (scores - high.astype(F32)).astype(BF16)
        out = jnp.dot(high, value, preferred_element_type=F32) + jnp.dot(
            low, value, preferred_element_type=F32
        )
        out = out * lax.rsqrt(jnp.mean(out * out, axis=-1, keepdims=True) + EPS)
        attended[e][...] = out.astype(BF16)


def bring_kernel(*refs):
    count = len(refs) // 2
    sems = refs[-1]
    copies = [pltpu.make_async_copy(refs[i], refs[count + i], sems.at[i]) for i in range(count)]
    for copy in copies:
        copy.start()
    for copy in copies:
        copy.wait()


def project_kernel(n, pos, x_share, *rest):
    weights, pieces, (out, a_all) = rest[:n], rest[n : 2 * n], rest[2 * n :]
    s = pos[1]
    total = x_share[...].astype(F32)
    for e in range(n):
        for d in range(n):
            span = pl.ds(pl.multiple_of((s ^ d) * HEAD_DIM, HEAD_DIM), HEAD_DIM)
            a_all[e, :, span] = pieces[d][e]
        total = total + lax.dot_general(
            a_all[e], weights[e][...], (((1,), (1,)), ((), ())), preferred_element_type=F32
        )
    out[...] = total.astype(BF16)


def route_kernel(n, experts, slots, pos, *refs):
    pieces, (pick, place, weight, table) = refs[:n], refs[n:]
    s = pos[1]
    rows = pieces[0].shape[0] - 2 * TOPK
    total = n * rows
    for d in range(n):
        lines = pieces[d][rows:, :].astype(F32)[:TOPK]
        gate = sum(lines[:, (1 + i) * rows : (2 + i) * rows] for i in range(3))
        span = pl.ds(pl.multiple_of((s ^ d) * rows, rows), rows)
        table[:, span] = jnp.concatenate([lines[:, :rows], gate], axis=0)
    first = (s * experts).astype(F32)
    names = lax.broadcasted_iota(jnp.int32, (experts, total), 0).astype(F32) + first
    member = jnp.zeros((experts, total), F32)
    gate = jnp.zeros((experts, total), F32)
    for k in range(TOPK):
        hit = table[k : k + 1, :] == names
        member = jnp.where(hit, 1.0, member)
        gate = jnp.where(hit, table[TOPK + k : TOPK + k + 1, :], gate)
    earlier = (
        lax.broadcasted_iota(jnp.int32, (total, total), 0)
        < lax.broadcasted_iota(jnp.int32, (total, total), 1)
    ).astype(F32).astype(BF16)
    rank = jnp.dot(member.astype(BF16), earlier, preferred_element_type=F32)
    slot = jnp.where(member > 0.0, rank, -1.0).astype(BF16)
    pairs = experts * slots
    expand = (
        lax.broadcasted_iota(jnp.int32, (experts, pairs), 1) // slots
        == lax.broadcasted_iota(jnp.int32, (experts, pairs), 0)
    ).astype(F32).astype(BF16)
    across = lax.dot_general(
        slot, expand, (((0,), (0,)), ((), ())), preferred_element_type=F32
    )
    number = (lax.broadcasted_iota(jnp.int32, (total, pairs), 1) % slots).astype(F32)
    place[...] = jnp.where(across == number, 1.0, 0.0).astype(BF16)
    for e in range(experts):
        span = pl.ds(e * slots, slots)
        number = lax.broadcasted_iota(jnp.int32, (slots, total), 0).astype(F32)
        hit = number == slot[e : e + 1, :].astype(F32)
        pick[span, :] = jnp.where(hit, 1.0, 0.0).astype(BF16)
        chosen = jnp.sum(jnp.where(hit, gate[e : e + 1, :], 0.0), axis=1, keepdims=True)
        weight[span, :] = jnp.broadcast_to(chosen, (slots, weight.shape[1]))


def span(block, size):
    return pl.ds(pl.multiple_of(block * size, size), size)


def weight_copies(pos, distances, i, group, ins, outs, sems, first=0):
    source_part, part = pl.ds(first + i * group, group), pl.ds(i * group, group)
    cols = outs[0].shape[1] // len(distances)
    copies = []
    for k, distance in enumerate(distances):
        for which, (w, kept) in enumerate(zip(ins, outs)):
            source = w.at[source_part, span(pos[1] ^ distance, cols), :]
            target = kept.at[part, pl.ds(k * cols, cols), :]
            copies.append(pltpu.make_async_copy(source, target, sems.at[i, 2 * k + which]))
    return copies


def down_copies(pos, distances, i, group, w_down, outs, sems):
    part, cols = pl.ds(i * group, group), outs[0].shape[2]
    copies = []
    for k, (distance, kept) in enumerate(zip(distances, outs)):
        source = w_down.at[part, :, span(pos[2] ^ distance, cols)]
        copies.append(pltpu.make_async_copy(source, kept.at[part], sems.at[i, k]))
    return copies


def load_down_kernel(group, distances, pos, w_down, *refs):
    outs, sems = refs[:-1], refs[-1]
    copies = []
    for i in range(outs[0].shape[0] // group):
        copies += down_copies(pos, distances, i, group, w_down, outs, sems)
    for copy in copies:
        copy.start()
    for copy in copies:
        copy.wait()


def load_kernel(group, distances, pos, w_gate, w_up, g_all, u_all, sems):
    copies = []
    for i in range(g_all.shape[0] // group):
        copies += weight_copies(
            pos, distances, i, group, (w_gate, w_up), (g_all, u_all), sems
        )
    for copy in copies:
        copy.start()
    for copy in copies:
        copy.wait()


def place_rows(n, distances, pos, pieces, r_all):
    rows, cols = pieces[0][0].shape
    for k in range(len(distances)):
        for e in range(n):
            r_all[span(pos[2] ^ e, rows), k * cols : (k + 1) * cols] = pieces[k][e][...]


def gather_rows(distances, pos, gain, picked, r_all, square):
    cols = r_all.shape[1] // len(distances)
    scaled = []
    for k, distance in enumerate(distances):
        taken = jnp.dot(picked, r_all[:, k * cols : (k + 1) * cols], preferred_element_type=F32)
        square = square + jnp.sum(taken * taken, axis=1, keepdims=True)
        scaled.append((taken * gain[:, span(pos[1] ^ distance, cols)]).astype(BF16))
    return scaled, square


def first_hidden_kernel(n, slots, group, distances, pos, gain, pick, g_all, u_all, *refs):
    pieces = [refs[k * n : (k + 1) * n] for k in range(len(distances))]
    total_out, square_out, r_all, x_slots = refs[n * len(distances) :]
    experts, wide, hidden = g_all.shape
    place_rows(n, distances, pos, pieces, r_all)
    for i in range(experts // group):
        part = slice(i * group * slots, (i + 1) * group * slots)
        scaled, square = gather_rows(distances, pos, gain, pick[part, :], r_all, 0.0)
        for k, value in enumerate(scaled):
            x_slots[part, k * value.shape[1] : (k + 1) * value.shape[1]] = value
        square_out[part, :] = jnp.broadcast_to(square, (group * slots, square_out.shape[1]))
    for e in range(experts):
        mine = slice(e * slots, (e + 1) * slots)
        total_out[mine, :hidden] = jnp.dot(x_slots[mine, :], g_all[e], preferred_element_type=F32)
        total_out[mine, hidden:] = jnp.dot(x_slots[mine, :], u_all[e], preferred_element_type=F32)


def last_hidden_kernel(
    n, slots, group, distances, downs, pos, gain, pick, w_gate, w_up, w_down, g_some, u_some,
    total_in, square_in, weight, *refs,
):
    pieces = [refs[k * n : (k + 1) * n] for k in range(len(distances))]
    hidden_out, *refs = refs[n * len(distances) :]
    d_outs, (r_all, x_slots, g_all, u_all, sems, d_sems) = refs[: len(downs)], refs[len(downs) :]
    some, wide, hidden = g_some.shape
    ready, parts = some // group, (some + g_all.shape[0]) // group
    width = n * wide // len(distances)

    def copies(i):
        return weight_copies(
            pos, distances, i, group, (w_gate, w_up), (g_all, u_all), sems, first=some
        )

    def start(i, carry):
        for copy in copies(i):
            copy.start()
        return carry

    def d_copies(i):
        return down_copies(pos, downs, i, group, w_down, d_outs, d_sems)

    def start_down(i, carry):
        for copy in d_copies(i):
            copy.start()
        return carry

    def step(g_from, u_from, skipped, i, carry):
        part = span(i, group * slots)
        scaled, square = gather_rows(
            distances, pos, gain, pick[part, :], r_all, square_in[part, :1]
        )
        for k, value in enumerate(scaled):
            x_slots[:, k * value.shape[1] : (k + 1) * value.shape[1]] = value
        scale = lax.rsqrt(square / width + EPS)
        if skipped:
            for copy in copies(i - skipped):
                copy.wait()
        for e in range(group):
            inner = slice(e * slots, (e + 1) * slots)
            mine = pl.ds(pl.multiple_of(i * group * slots + e * slots, slots), slots)
            taken = x_slots[inner, :]
            gate_val = jnp.dot(taken, g_from[(i - skipped) * group + e], preferred_element_type=F32)
            up_val = jnp.dot(taken, u_from[(i - skipped) * group + e], preferred_element_type=F32)
            gate_val = (gate_val + total_in[mine, :hidden]) * scale[inner]
            up_val = (up_val + total_in[mine, hidden:]) * scale[inner]
            value = gate_val * jax.nn.sigmoid(gate_val) * (up_val * weight[mine, :1])
            hidden_out[mine, :] = value.astype(BF16)
        return carry

    lax.fori_loop(0, parts - ready, start, 0)
    lax.fori_loop(0, parts, start_down, 0)
    place_rows(n, distances, pos, pieces, r_all)
    lax.fori_loop(0, ready, functools.partial(step, g_some, u_some, 0), 0)
    lax.fori_loop(ready, parts, functools.partial(step, g_all, u_all, ready), 0)
    for i in range(parts):
        for copy in d_copies(i):
            copy.wait()


def self_down_kernel(slots, group, distances, pos, hidden, place, w_down, out, kept, y_slots, sems):
    copies = [
        down_copies(pos, distances, i, group, w_down, (kept,), sems)[0]
        for i in range(kept.shape[0] // group)
    ]
    for copy in copies:
        copy.start()

    def step(i, carry):
        down_copies(pos, distances, i, group, w_down, (kept,), sems)[0].wait()
        for e in range(group):
            mine = pl.ds(pl.multiple_of(i * group * slots + e * slots, slots), slots)
            product = jnp.dot(hidden[mine, :], kept[i * group + e], preferred_element_type=F32)
            y_slots[mine, :] = product.astype(BF16)
        return carry

    lax.fori_loop(0, len(copies), step, 0)
    out[...] = jnp.dot(place[...], y_slots[...], preferred_element_type=F32).astype(BF16)


def down_kernel(slots, pos, hidden, place, *refs):
    count = len(refs) // 2
    for kept, out in zip(refs[:count], refs[count:]):
        y_slots = refs[-1]
        for e in range(kept.shape[0]):
            mine = slice(e * slots, (e + 1) * slots)
            product = jnp.dot(hidden[mine, :], kept[e], preferred_element_type=F32)
            y_slots[mine, :] = product.astype(BF16)
        out[...] = jnp.dot(place[...], y_slots[...], preferred_element_type=F32).astype(BF16)


def add_kernel(distances, pos, base, part, *refs):
    cores, outs = refs[: len(distances)], refs[len(distances) :]
    rows = outs[0].shape[0]
    in_half = part.shape[0] // rows
    for d, core, out in zip(distances, cores, outs):
        block = pos[1] ^ d
        value = base[span(block, rows), :].astype(F32) + core[...].astype(F32)
        out[...] = (value + part[span(block % in_half, rows), :].astype(F32)).astype(out.dtype)


def down_blocks_kernel(slots, pos, hidden, place, kept, *refs):
    outs, (y_slots, whole) = refs[:-2], refs[-2:]
    rows = outs[0].shape[0]
    for e in range(kept.shape[0]):
        mine = slice(e * slots, (e + 1) * slots)
        product = jnp.dot(hidden[mine, :], kept[e], preferred_element_type=F32)
        y_slots[mine, :] = product.astype(BF16)
    whole[...] = jnp.dot(place[...], y_slots[...], preferred_element_type=F32).astype(BF16)
    for d, out in enumerate(outs):
        out[...] = whole[span(pos[1] ^ d, rows), :]


def cores_kernel(shares, pos, base, core, *outs):
    rows = outs[0].shape[0] // len(shares[0])
    for distances, out in zip(shares, outs):
        for d in distances:
            block = pos[1] ^ d
            inside = block % len(distances)
            value = base[span(block, rows), :].astype(F32) + core[span(block, rows), :].astype(F32)
            out[span(inside, rows), :] = value.astype(out.dtype)


def square_body(
    n, tokens, attn_weight, attn_gain, moe_gain, routes, gates, expert_gate, expert_up, expert_down
):
    g, s, h = (lax.axis_index(axis) for axis in ("grp", "seq", "head"))
    pos = jnp.stack([g, s, h]).astype(jnp.int32)
    rows, width = tokens.shape
    cols = width // n
    depth = attn_weight.shape[1]
    half = depth // 2
    experts, _, hidden = expert_gate.shape
    total = n * rows
    slots = -(-n * CAP // 16) * 16
    pairs = experts * slots
    sds = jax.ShapeDtypeStruct
    dma = pltpu.SemaphoreType.DMA

    def room(mib):
        return pltpu.CompilerParams(vmem_limit_bytes=mib * MIB)

    def cost(macs, size):
        return pl.CostEstimate(flops=2 * macs, bytes_accessed=size, transcendentals=0)

    def plus(*terms):
        total_value = terms[0].astype(F32)
        for term in terms[1:]:
            total_value = total_value + term.astype(F32)
        return total_value

    lines = 2 * TOPK
    with jax.named_scope("cut_pieces"):
        x_send, *w_sends = pl.pallas_call(
            cut_kernel,
            out_shape=[sds((rows + lines, cols), BF16)]
            + [sds((half, 3 * HEAD_DIM), BF16)] * (n - 1),
            in_specs=[SMEM] + [ANY] * 4,
            out_specs=[VMEM] * n,
            scratch_shapes=[
                pltpu.VMEM((TOPK, rows), jnp.int32),
                pltpu.VMEM((TOPK, rows), F32),
                dma((3 + 3 * (n - 1),)),
            ],
            compiler_params=room(8),
        )(pos, *map(held, (routes.T, gates.T, tokens, attn_weight)))
    group = experts // 4
    w_gate, w_up, w_down = map(held, (expert_gate, expert_up, expert_down))

    early, late = tuple(range(n // 2)), tuple(range(n // 2, n))
    wide = n // 2 * cols
    ahead = experts // 2
    hidden_cost = cost(pairs * wide * (total + 2 * hidden), 4 * experts * wide * hidden)

    def load(distances, amount, *earlier):
        return pl.pallas_call(
            functools.partial(load_kernel, group, distances),
            out_shape=[pltpu.VMEM((amount, wide, hidden), BF16)] * 2,
            in_specs=[SMEM] + [ANY] * 2,
            out_specs=[VMEM] * 2,
            scratch_shapes=[dma((amount // group, 2 * len(distances)))],
            compiler_params=room(2),
            cost_estimate=cost(0, 4 * amount * wide * hidden),
        )(after(pos, *earlier), w_gate, w_up)

    def load_down(distances, *earlier):
        count = len(distances)
        return pl.pallas_call(
            functools.partial(load_down_kernel, group, distances),
            out_shape=[pltpu.VMEM((experts, hidden, cols), BF16)] * count,
            in_specs=[SMEM, ANY],
            out_specs=[VMEM] * count,
            scratch_shapes=[dma((experts // group, count))],
            compiler_params=room(2),
            cost_estimate=cost(0, 2 * count * experts * cols * hidden),
        )(after(pos, *earlier), w_down)

    with jax.named_scope("gather_tokens_and_weights"):
        x_far = [swap(x_send, "seq", d) for d in range(1, n)]
        w_near = [swap(w_sends[d - 1], "seq", d) for d in range(1, n - 1)]
        step = in_step(*x_far, *w_near, w_sends[-1])
        x_far, w_near, w_last = step[: n - 1], list(step[n - 1 : -1]), step[-1]
        x_pieces = {0: jnp.stack([x[:rows] for x in x_far])}
        x_pieces[2] = swap(x_pieces[0], "head", 2)
        w_far = [swap(w, "grp", 1) for w in w_near]
        w_near.append(swap(w_last, "seq", n - 1))
        late_weights = list(load(late, ahead, w_near[0]))
        late_weights[0], x_pieces[2], w_near[-1], *w_far = in_step(
            late_weights[0], x_pieces[2], w_near[-1], *w_far
        )
        w_far.append(swap(w_near[-1], "grp", 1))
        for e in (0, 2):
            x_pieces[e ^ 1] = swap(x_pieces[e], "head", 1)
    with jax.named_scope("routing"):
        pick, place, weight = pl.pallas_call(
            functools.partial(route_kernel, n, experts, slots),
            out_shape=[sds((pairs, total), BF16), sds((total, pairs), BF16), sds((pairs, 128), F32)],
            in_specs=[SMEM] + [VMEM] * n,
            out_specs=[VMEM] * 3,
            scratch_shapes=[pltpu.VMEM((2 * TOPK, total), F32)],
            compiler_params=room(16),
        )(pos, x_send, *x_far)
    with jax.named_scope("gather_out_weights"):
        w_near[-1] = after(w_near[-1], pick)
        o_own = after(attn_weight, pick)[3]
        o_pieces = {0: o_own, 2: swap(o_own, "head", 2)}

    with jax.named_scope("projected_tokens"):
        partial, x_last, x_share = pl.pallas_call(
            functools.partial(project_tokens_kernel, n),
            out_shape=[
                sds((total, 3 * HEAD_DIM), F32),
                sds((total, half), BF16),
                sds((rows, cols), BF16),
            ],
            in_specs=[SMEM, VMEM] + [ANY] * (2 + n + 2 * (n - 1) - 1),
            out_specs=[VMEM] * 3,
            scratch_shapes=[
                pltpu.VMEM((total, width), BF16),
                pltpu.VMEM((width, 3 * HEAD_DIM), BF16),
                dma((1 + n * (n - 1),)),
                dma((3 + 2 * (n - 1) - 1,)),
            ],
            compiler_params=room(9),
            cost_estimate=cost(total * width * 3 * HEAD_DIM, 4 * total * width),
        )(
            pos, attn_gain.reshape(1, width), held(tokens), held(attn_weight),
            *[held(x_pieces[e]) for e in range(n)], *map(held, w_near), *map(held, w_far[:-1]),
        )
    with jax.named_scope("attention"):
        attended = pl.pallas_call(
            functools.partial(attend_kernel, n),
            out_shape=[sds((rows, HEAD_DIM), BF16)] * n,
            in_specs=[SMEM] + [VMEM] * 3,
            out_specs=[VMEM] * n,
            scratch_shapes=[pltpu.VMEM((total, 3 * HEAD_DIM), BF16)],
            compiler_params=room(6),
        )(pos, partial, x_last, w_far[-1])

    gain_row = moe_gain.reshape(1, width)

    def first_hidden(pieces, weights):
        return pl.pallas_call(
            functools.partial(first_hidden_kernel, n, slots, group, early),
            out_shape=[sds((pairs, 2 * hidden), F32), sds((pairs, 128), F32)],
            in_specs=[SMEM] + [VMEM] * (4 + n * len(early)),
            out_specs=[VMEM] * 2,
            scratch_shapes=[pltpu.VMEM((total, wide), BF16), pltpu.VMEM((pairs, wide), BF16)],
            compiler_params=room(12),
            cost_estimate=hidden_cost,
        )(pos, gain_row, pick, *map(here, weights), *pieces)

    def last_hidden(pieces, weights, state, downs):
        return pl.pallas_call(
            functools.partial(last_hidden_kernel, n, slots, group, late, downs),
            out_shape=[sds((pairs, hidden), BF16)]
            + [pltpu.VMEM((experts, hidden, cols), BF16)] * len(downs),
            in_specs=[SMEM] + [VMEM] * 2 + [ANY] * 3 + [VMEM] * (5 + n * len(late)),
            out_specs=[VMEM] * (1 + len(downs)),
            scratch_shapes=[pltpu.VMEM((total, wide), BF16), pltpu.VMEM((group * slots, wide), BF16)]
            + [pltpu.VMEM((experts - ahead, wide, hidden), BF16)] * 2
            + [dma(((experts - ahead) // group, 2 * len(late)))]
            + [dma((experts // group, len(downs)))],
            compiler_params=room(16),
            cost_estimate=hidden_cost,
        )(
            pos, gain_row, pick, w_gate, w_up, w_down, *map(here, weights), *state, weight, *pieces
        )

    with jax.named_scope("heads_to_tokens"):
        for e in (0, 2):
            o_pieces[e ^ 1] = swap(after(o_pieces[e], attended[0]), "head", 1)
        arrived = [attended[0]] + [swap(attended[e], "head", e) for e in range(1, n)]
        arrived = jnp.stack(arrived)
        a_pieces = [arrived, swap(arrived, "seq", 1), swap(arrived, "seq", 2)]
        with jax.named_scope("expert_weights"):
            early_weights = load(early, experts, arrived)
        a_pieces[2] = after(a_pieces[2], early_weights[0])
        a_pieces.append(swap(a_pieces[2], "seq", 1))
        with jax.named_scope("expert_weights"):
            (d_2,) = load_down((2,), a_pieces[2])
        x_share = after(x_share, d_2)

    with jax.named_scope("bring_out_weights"):
        o_here = pl.pallas_call(
            bring_kernel,
            out_shape=[pltpu.VMEM((depth, cols), BF16)] * n,
            in_specs=[ANY] * n,
            out_specs=[VMEM] * n,
            scratch_shapes=[dma((n,))],
            compiler_params=room(2),
            cost_estimate=cost(0, 2 * n * depth * cols),
        )(*[o_pieces[e] for e in range(n)])
    with jax.named_scope("output_projection"):
        residual = pl.pallas_call(
            functools.partial(project_kernel, n),
            out_shape=sds((rows, cols), BF16),
            in_specs=[SMEM] + [VMEM] * (1 + 2 * n),
            out_specs=VMEM,
            scratch_shapes=[pltpu.VMEM((n, rows, n * HEAD_DIM), BF16)],
            compiler_params=room(12),
        )(pos, x_share, *map(here, o_here), *a_pieces)

    with jax.named_scope("gather_residual"):
        r_pieces = {0: {0: residual}}
        for d in (1, 2):
            r_pieces[d] = {0: swap(residual, "seq", d)}
        r_pieces[3] = {0: swap(r_pieces[2][0], "seq", 1)}
        for d in range(n):
            r_pieces[d][2] = swap(r_pieces[d][0], "head", 2)
            r_pieces[d][1] = swap(r_pieces[d][0], "head", 1)
        for d in early:
            r_pieces[d][3] = swap(r_pieces[d][2], "head", 1)
        r_pieces[0][0] = after(residual, r_pieces[3][0], r_pieces[2][2])
        pieces = [r_pieces[d][e] for d in early for e in range(n)]
        with jax.named_scope("first_hidden_units"):
            state = first_hidden(pieces, early_weights)
        for d in late:
            r_pieces[d][3] = swap(after(r_pieces[d][2], state[1]), "head", 1)
        pieces = [r_pieces[d][e] for d in late for e in range(n)]
        with jax.named_scope("last_hidden_units"):
            units, d_3, d_1 = last_hidden(pieces, late_weights, state, (3, 1))
        r_choices = [r_pieces[d][d] for d in range(n)]
    def down(units, *weights):
        count = len(weights)
        with jax.named_scope("down_products"):
            return pl.pallas_call(
                functools.partial(down_kernel, slots),
                out_shape=[sds((total, cols), BF16)] * count,
                in_specs=[SMEM] + [VMEM] * (2 + count),
                out_specs=[VMEM] * count,
                scratch_shapes=[pltpu.VMEM((pairs, cols), BF16)],
                compiler_params=room(6),
                cost_estimate=cost(
                    count * pairs * cols * (total + hidden), 2 * count * experts * cols * hidden
                ),
            )(pos, units, place, *map(here, weights))

    def self_down(units, distance):
        with jax.named_scope("down_products_alone"):
            return pl.pallas_call(
                functools.partial(self_down_kernel, slots, group, (distance,)),
                out_shape=sds((total, cols), BF16),
                in_specs=[SMEM] + [VMEM] * 2 + [ANY],
                out_specs=VMEM,
                scratch_shapes=[
                    pltpu.VMEM((experts, hidden, cols), BF16),
                    pltpu.VMEM((pairs, cols), BF16),
                    dma((experts // group, 1)),
                ],
                compiler_params=room(9),
                cost_estimate=cost(0, 0),
            )(pos, units, place, w_down)

    with jax.named_scope("sum_over_devices"):
        (out_3,) = down(units, d_3)
        core_2 = swap(out_3, "head", 1)
        (out_2,) = down(after(units, out_3), d_2)
        halves = (tuple(range(n // 2, n)), tuple(range(n // 2)))
        with jax.named_scope("sums_over_cores"):
            near = pl.pallas_call(
                functools.partial(cores_kernel, halves),
                out_shape=[sds((len(d) * rows, cols), BF16) for d in halves],
                in_specs=[SMEM] + [VMEM] * 2,
                out_specs=[VMEM] * len(halves),
                compiler_params=room(4),
                cost_estimate=cost(0, 4 * total * cols),
            )(pos, out_2, core_2)
        far = [swap(part, "head", 2) for part in near]
        with jax.named_scope("down_products_by_block"):
            out_1 = pl.pallas_call(
                functools.partial(down_blocks_kernel, slots),
                out_shape=[sds((rows, cols), BF16)] * n,
                in_specs=[SMEM] + [VMEM] * 3,
                out_specs=[VMEM] * n,
                scratch_shapes=[pltpu.VMEM((pairs, cols), BF16), pltpu.VMEM((total, cols), BF16)],
                compiler_params=room(6),
                cost_estimate=cost(SLOW, 2 * experts * cols * hidden),
            )(pos, after(units, *near), place, here(d_1))
        core_0 = [swap(part, "head", 1) for part in out_1]
        out_0 = self_down(after(units, out_1[0]), 0)

        def add_parts(distances, part, macs):
            with jax.named_scope("rows_" + "_".join(map(str, distances))):
                return pl.pallas_call(
                    functools.partial(add_kernel, distances),
                    out_shape=[sds((rows, cols), BF16 if d else F32) for d in distances],
                    in_specs=[SMEM] + [VMEM] * (2 + len(distances)),
                    out_specs=[VMEM] * len(distances),
                    compiler_params=room(4),
                    cost_estimate=cost(macs, 4 * part.size),
                )(pos, out_0, part, *[core_0[d] for d in distances])

        far_line, near_line = halves
        far_sums = add_parts(far_line, far[0], 0)
        from_far = [swap(part, "seq", d) for d, part in zip(far_line, far_sums)]
        own_sum, *near_sums = add_parts(near_line, far[1], SLOW)
        from_near = [swap(part, "seq", d) for d, part in zip(near_line[1:], near_sums)]
        mixed = plus(lax.select_n(s ^ h, *in_step(*r_choices, own_sum)[:n]), own_sum, *from_far)
        mixed = plus(*in_step(mixed, *from_near))
        mixed = mixed.astype(BF16)
    with jax.named_scope("gather_columns"):
        return lax.all_gather(mixed, "head", axis=1, tiled=True)


def solution(mesh):
    sizes = dict(mesh.shape)
    n = sizes["seq"]

    def body(tokens, attn_weight, *rest):
        width = tokens.shape[1]
        square = (
            n == sizes["head"]
            and n == 4
            and sizes["grp"] == 2
            and width == n * attn_weight.shape[1] == n * attn_weight.shape[2]
            and width == n * n * HEAD_DIM
            and n * tokens.shape[0] <= width // n
        )
        if square:
            return square_body(n, tokens, attn_weight, *rest)
        return general_body(tokens, attn_weight, *rest)

    return jax.shard_map(
        body,
        mesh=mesh,
        in_specs=(
            P(("grp", "seq"), None),
            P(None, "seq", "head"),
            P(),
            P(),
            P(("grp", "seq"), None),
            P(("grp", "seq"), None),
            P("seq", None, "head"),
            P("seq", None, "head"),
            P("seq", "head", None),
        ),
        out_specs=P(("grp", "seq"), None),
        check_vma=False,
    )
```

```python
import functools

import jax
import jax.numpy as jnp
from jax import lax
from jax.experimental import pallas as pl
from jax.experimental.pallas import tpu as pltpu
from jax.sharding import PartitionSpec as P

HEAD_DIM = 128
EXPERTS = 64
TOPK = 8
CAP = 18
EPS = 1e-06

PRECISE = lax.Precision.HIGHEST
BF16 = jnp.bfloat16
F32 = jnp.float32
ANY = pl.BlockSpec(memory_space=pl.ANY)
SMEM = pl.BlockSpec(memory_space=pltpu.SMEM)
VMEM = pl.BlockSpec(memory_space=pltpu.VMEM)
MIB = 1024 * 1024
SLOW = 10**10


def prefix_2(array, axis, combine, identity):
    peers, position = (lax.axis_size(axis), lax.axis_index(axis))
    everything = lax.all_gather(array.astype(jnp.bfloat16), axis)
    start = jnp.broadcast_to(jnp.asarray(identity, array.dtype), array.shape)

    def hop(k, before):
        reached = k < position
        new = combine(before, everything[k].astype(array.dtype))
        return jnp.where(reached, new, before)

    return lax.fori_loop(0, peers, hop, start)


def rms_scale(row_block, gain_vec):
    widened = row_block.astype(jnp.float32)
    factor = lax.rsqrt(jnp.mean(widened * widened, axis=-1, keepdims=True) + 1e-06)
    return widened * factor * gain_vec


def head_norm(outputs):
    return outputs * lax.rsqrt(jnp.mean(outputs * outputs, axis=-1, keepdims=True) + 1e-06)


def add_states(earlier, later):
    return earlier + later


def slot_numbers(route_flat):
    one_hot = (route_flat[:, None] == jnp.arange(EXPERTS, dtype=jnp.int32)[None, :]).astype(
        jnp.int32
    )
    earlier = jnp.cumsum(one_hot, axis=0) - one_hot
    return route_flat * CAP + jnp.sum(earlier * one_hot, axis=1)


def make_runner(expert_gate, expert_up, expert_down):

    def run_experts(received):
        gate_val = jnp.einsum(
            "necd,edf->necf", received, expert_gate, preferred_element_type=jnp.float32
        )
        up_val = jnp.einsum(
            "necd,edf->necf", received, expert_up, preferred_element_type=jnp.float32
        )
        hidden = (jax.nn.silu(gate_val) * up_val).astype(jnp.bfloat16)
        partial_value = jnp.einsum(
            "necf,efd->necd", hidden, expert_down, preferred_element_type=jnp.float32
        ).astype(jnp.bfloat16)
        groups = lax.axis_size("head")
        shape_now = partial_value.shape
        split = partial_value.reshape(
            shape_now[0], shape_now[1], shape_now[2], groups, shape_now[3] // groups
        )
        by_group = lax.all_to_all(split, "head", split_axis=3, concat_axis=3, tiled=True)
        summed = jnp.sum(by_group.astype(jnp.float32), axis=3)
        return lax.all_to_all(
            summed.astype(jnp.bfloat16), "seq", split_axis=0, concat_axis=0, tiled=True
        ).astype(summed.dtype)

    return run_experts


def general_body(
    tokens, attn_weight, attn_gain, moe_gain, routes, gates, expert_gate, expert_up, expert_down
):
    local_rows = tokens.shape[0]
    normed = rms_scale(tokens, attn_gain).astype(jnp.bfloat16)
    weights = lax.all_gather(attn_weight, "seq", axis=1, tiled=True)
    head_count = weights.shape[2] // HEAD_DIM
    projected = [
        jnp.dot(normed, weights[which], preferred_element_type=jnp.float32)
        .astype(jnp.bfloat16)
        .reshape(local_rows, head_count, HEAD_DIM)
        for which in range(3)
    ]
    query_rows, key_rows, value_rows = projected
    own_state = jnp.einsum("thd,the->hde", key_rows, value_rows, preferred_element_type=jnp.float32)
    prefix = prefix_2(own_state, "seq", add_states, jnp.zeros_like(own_state))
    inter_part = jnp.einsum(
        "thd,hde->the", query_rows.astype(jnp.float32), prefix, precision=PRECISE
    )
    scores = jnp.einsum("thd,shd->hts", query_rows, key_rows, preferred_element_type=jnp.float32)
    lower_mask = jnp.arange(local_rows)[:, None] >= jnp.arange(local_rows)[None, :]
    scores = jnp.where(lower_mask[None], scores, 0.0)
    intra_part = jnp.einsum(
        "hts,she->the", scores, value_rows.astype(jnp.float32), precision=PRECISE
    )
    attended = (
        head_norm(inter_part + intra_part)
        .reshape(local_rows, head_count * HEAD_DIM)
        .astype(jnp.bfloat16)
    )
    out_part = lax.dot_general(
        attended, weights[3], (((1,), (1,)), ((), ())), preferred_element_type=jnp.float32
    )
    residual = (
        tokens.astype(jnp.float32)
        + lax.psum(out_part.astype(jnp.bfloat16), "head").astype(jnp.float32)
    ).astype(jnp.bfloat16)
    moe_in = rms_scale(residual, moe_gain).astype(jnp.bfloat16)
    route_flat = routes.reshape(-1)
    slots = slot_numbers(route_flat)
    owners = lax.axis_size("seq")
    local_experts = expert_gate.shape[0]
    source_row = jnp.arange(route_flat.shape[0], dtype=jnp.int32) // TOPK
    run_experts = make_runner(expert_gate, expert_up, expert_down)
    outbound = (
        jnp.zeros((EXPERTS * CAP, moe_in.shape[1]), jnp.bfloat16).at[slots].set(moe_in[source_row])
    )
    outbound = outbound.reshape(owners, local_experts, CAP, moe_in.shape[1])
    returned = run_experts(lax.all_to_all(outbound, "seq", split_axis=0, concat_axis=0, tiled=True))
    arrived = returned.reshape(EXPERTS * CAP, -1)[slots].reshape(local_rows, TOPK, -1)
    moe_partial = jnp.einsum("tkd,tk->td", arrived, gates, precision=PRECISE)
    column_span = moe_partial.shape[1]
    residual_share = lax.dynamic_slice_in_dim(
        residual, lax.axis_index("head") * column_span, column_span, 1
    )
    mixed_share = (residual_share.astype(jnp.float32) + moe_partial).astype(jnp.bfloat16)
    return lax.all_gather(mixed_share, "head", axis=1, tiled=True)


def swap(array, axis, distance):
    size = lax.axis_size(axis)
    return lax.ppermute(array, axis, [(i, i ^ distance) for i in range(size)])


def run_copies(copies):
    for copy in copies:
        copy.start()
    for copy in copies:
        copy.wait()


def after(array, *earlier):
    return lax.optimization_barrier((array,) + earlier)[0]


def held(array):
    return pltpu.with_memory_space_constraint(array, pltpu.HBM)


def here(array):
    return pltpu.with_memory_space_constraint(array, pltpu.VMEM)


def in_step(*arrays):
    return lax.optimization_barrier(arrays)


def cut_kernel(pos, routes, gates, tokens, weight, x_send, *rest):
    w_sends, (r_here, g_here, sems) = rest[:-3], rest[-3:]
    g, s, h = pos[0], pos[1], pos[2]
    rows, cols, half = tokens.shape[0], x_send.shape[1], w_sends[0].shape[0]
    copies = [
        (
            tokens.at[:, pl.ds(pl.multiple_of(h * cols, cols), cols)],
            x_send.at[pl.ds(0, rows)],
        ),
        (routes, r_here),
        (gates, g_here),
    ]
    for which in range(3):
        span = pl.ds(which * HEAD_DIM, HEAD_DIM)
        for distance, out in enumerate(w_sends, 1):
            column = pl.multiple_of((s ^ distance) * HEAD_DIM, HEAD_DIM)
            own_half = pl.ds(pl.multiple_of(g * half, half), half)
            copies.append(
                (weight.at[which, own_half, pl.ds(column, HEAD_DIM)], out.at[:, span])
            )
    copies = [pltpu.make_async_copy(a, b, sems.at[i]) for i, (a, b) in enumerate(copies)]
    for copy in copies:
        copy.start()
    for copy in copies[1:3]:
        copy.wait()
    parts, left = [r_here[...].astype(F32)], g_here[...]
    for _ in range(3):
        parts.append(left.astype(BF16).astype(F32))
        left = left - parts[-1]
    lines = jnp.concatenate(parts, axis=1)
    lines = jnp.concatenate([lines, jnp.zeros_like(lines)], axis=0)
    blank = jnp.zeros((lines.shape[0], cols - lines.shape[1]), F32)
    if blank.shape[1]:
        lines = jnp.concatenate([lines, blank], axis=1)
    x_send[rows:, :] = lines.astype(BF16)
    for copy in copies[:1] + copies[3:]:
        copy.wait()


def project_tokens_kernel(n, pos, gain, tokens, weight, *rest):
    x_pieces, w_near, w_far = rest[:n], rest[n : 2 * n - 1], rest[2 * n - 1 : 3 * n - 3]
    partial, x_last, x_share, x_all, w_all, x_sems, w_sems = rest[3 * n - 3 :]
    g, s, h = pos[0], pos[1], pos[2]
    rows, width = tokens.shape
    cols = width // n
    depth, half = weight.shape[1], w_near[0].shape[0]
    missing = (s ^ (n - 1)) * 2 + (1 - g)
    x_copies = [(tokens, x_all.at[span(s, rows)])]
    for d in range(1, n):
        for e in range(n):
            target = x_all.at[span(s ^ d, rows), span(h ^ e, cols)]
            x_copies.append((x_pieces[e].at[d - 1], target))
    w_copies = []
    for which in range(3):
        target = w_all.at[span(s, depth), pl.ds(which * HEAD_DIM, HEAD_DIM)]
        w_copies.append((weight.at[which, :, span(s, HEAD_DIM)], target))
    for d in range(1, n):
        w_copies.append((w_near[d - 1], w_all.at[span((s ^ d) * 2 + g, half)]))
        if d < n - 1:
            w_copies.append((w_far[d - 1], w_all.at[span((s ^ d) * 2 + (1 - g), half)]))
    x_copies = [
        pltpu.make_async_copy(a, b, x_sems.at[i]) for i, (a, b) in enumerate(x_copies)
    ]
    w_copies = [
        pltpu.make_async_copy(a, b, w_sems.at[i]) for i, (a, b) in enumerate(w_copies)
    ]
    for copy in x_copies + w_copies:
        copy.start()
    w_all[span(missing, half), :] = jnp.zeros((half, w_all.shape[1]), BF16)
    for copy in x_copies:
        copy.wait()
    x_share[...] = x_all[span(h, rows), span(s, cols)]

    def normalise(block, carry):
        mine = span(block, rows)
        wide = x_all[mine, :].astype(F32)
        factor = lax.rsqrt(jnp.mean(wide * wide, axis=-1, keepdims=True) + EPS)
        x_all[mine, :] = (wide * factor * gain[...]).astype(BF16)
        return carry

    lax.fori_loop(0, n, normalise, 0)
    x_last[...] = x_all[:, span(missing, half)]
    for copy in w_copies:
        copy.wait()
    partial[...] = jnp.dot(x_all[...], w_all[...], preferred_element_type=F32)


def attend_kernel(n, pos, partial, x_last, w_last, *rest):
    attended, projected = rest[:n], rest[n]
    h = pos[2]
    rows = x_last.shape[0] // n
    projected[...] = (
        partial[...] + jnp.dot(x_last[...], w_last[...], preferred_element_type=F32)
    ).astype(BF16)
    key, value = projected[:, HEAD_DIM : 2 * HEAD_DIM], projected[:, 2 * HEAD_DIM :]
    for e in range(n):
        block = h ^ e
        scores = lax.dot_general(
            projected[span(block, rows), :HEAD_DIM],
            key,
            (((1,), (1,)), ((), ())),
            preferred_element_type=F32,
        )
        position = lax.broadcasted_iota(jnp.int32, scores.shape, 0) + block * rows
        scores = jnp.where(
            position >= lax.broadcasted_iota(jnp.int32, scores.shape, 1), scores, 0.0
        )
        high = scores.astype(BF16)
        low = (scores - high.astype(F32)).astype(BF16)
        out = jnp.dot(high, value, preferred_element_type=F32) + jnp.dot(
            low, value, preferred_element_type=F32
        )
        out = out * lax.rsqrt(jnp.mean(out * out, axis=-1, keepdims=True) + EPS)
        attended[e][...] = out.astype(BF16)


def bring_kernel(*refs):
    count = len(refs) // 2
    sems = refs[-1]
    copies = [pltpu.make_async_copy(refs[i], refs[count + i], sems.at[i]) for i in range(count)]
    for copy in copies:
        copy.start()
    for copy in copies:
        copy.wait()


def project_kernel(n, pos, x_share, *rest):
    weights, pieces, (out, a_all) = rest[:n], rest[n : 2 * n], rest[2 * n :]
    s = pos[1]
    total = x_share[...].astype(F32)
    for e in range(n):
        for d in range(n):
            span = pl.ds(pl.multiple_of((s ^ d) * HEAD_DIM, HEAD_DIM), HEAD_DIM)
            a_all[e, :, span] = pieces[d][e]
        total = total + lax.dot_general(
            a_all[e], weights[e][...], (((1,), (1,)), ((), ())), preferred_element_type=F32
        )
    out[...] = total.astype(BF16)


def route_kernel(n, experts, slots, pos, *refs):
    pieces, (pick, place, weight, table) = refs[:n], refs[n:]
    s = pos[1]
    rows = pieces[0].shape[0] - 2 * TOPK
    total = n * rows
    for d in range(n):
        lines = pieces[d][rows:, :].astype(F32)[:TOPK]
        gate = sum(lines[:, (1 + i) * rows : (2 + i) * rows] for i in range(3))
        span = pl.ds(pl.multiple_of((s ^ d) * rows, rows), rows)
        table[:, span] = jnp.concatenate([lines[:, :rows], gate], axis=0)
    first = (s * experts).astype(F32)
    names = lax.broadcasted_iota(jnp.int32, (experts, total), 0).astype(F32) + first
    member = jnp.zeros((experts, total), F32)
    gate = jnp.zeros((experts, total), F32)
    for k in range(TOPK):
        hit = table[k : k + 1, :] == names
        member = jnp.where(hit, 1.0, member)
        gate = jnp.where(hit, table[TOPK + k : TOPK + k + 1, :], gate)
    earlier = (
        lax.broadcasted_iota(jnp.int32, (total, total), 0)
        < lax.broadcasted_iota(jnp.int32, (total, total), 1)
    ).astype(F32).astype(BF16)
    rank = jnp.dot(member.astype(BF16), earlier, preferred_element_type=F32)
    slot = jnp.where(member > 0.0, rank, -1.0).astype(BF16)
    pairs = experts * slots
    expand = (
        lax.broadcasted_iota(jnp.int32, (experts, pairs), 1) // slots
        == lax.broadcasted_iota(jnp.int32, (experts, pairs), 0)
    ).astype(F32).astype(BF16)
    across = lax.dot_general(
        slot, expand, (((0,), (0,)), ((), ())), preferred_element_type=F32
    )
    number = (lax.broadcasted_iota(jnp.int32, (total, pairs), 1) % slots).astype(F32)
    place[...] = jnp.where(across == number, 1.0, 0.0).astype(BF16)
    for e in range(experts):
        span = pl.ds(e * slots, slots)
        number = lax.broadcasted_iota(jnp.int32, (slots, total), 0).astype(F32)
        hit = number == slot[e : e + 1, :].astype(F32)
        pick[span, :] = jnp.where(hit, 1.0, 0.0).astype(BF16)
        chosen = jnp.sum(jnp.where(hit, gate[e : e + 1, :], 0.0), axis=1, keepdims=True)
        weight[span, :] = jnp.broadcast_to(chosen, (slots, weight.shape[1]))


def span(block, size):
    return pl.ds(pl.multiple_of(block * size, size), size)


def weight_copies(pos, distances, i, group, ins, outs, sems, first=0):
    source_part, part = pl.ds(first + i * group, group), pl.ds(i * group, group)
    cols = outs[0].shape[1] // len(distances)
    copies = []
    for k, distance in enumerate(distances):
        for which, (w, kept) in enumerate(zip(ins, outs)):
            source = w.at[source_part, span(pos[1] ^ distance, cols), :]
            target = kept.at[part, pl.ds(k * cols, cols), :]
            copies.append(pltpu.make_async_copy(source, target, sems.at[i, 2 * k + which]))
    return copies


def down_copies(pos, distances, i, group, w_down, outs, sems):
    part, cols = pl.ds(i * group, group), outs[0].shape[2]
    copies = []
    for k, (distance, kept) in enumerate(zip(distances, outs)):
        source = w_down.at[part, :, span(pos[2] ^ distance, cols)]
        copies.append(pltpu.make_async_copy(source, kept.at[part], sems.at[i, k]))
    return copies


def load_down_kernel(group, distances, pos, w_down, *refs):
    outs, sems = refs[:-1], refs[-1]
    copies = []
    for i in range(outs[0].shape[0] // group):
        copies += down_copies(pos, distances, i, group, w_down, outs, sems)
    for copy in copies:
        copy.start()
    for copy in copies:
        copy.wait()


def load_kernel(group, distances, pos, w_gate, w_up, g_all, u_all, sems):
    copies = []
    for i in range(g_all.shape[0] // group):
        copies += weight_copies(
            pos, distances, i, group, (w_gate, w_up), (g_all, u_all), sems
        )
    for copy in copies:
        copy.start()
    for copy in copies:
        copy.wait()


def place_rows(n, distances, pos, pieces, r_all):
    rows, cols = pieces[0][0].shape
    for k in range(len(distances)):
        for e in range(n):
            r_all[span(pos[2] ^ e, rows), k * cols : (k + 1) * cols] = pieces[k][e][...]


def gather_rows(distances, pos, gain, picked, r_all, square):
    cols = r_all.shape[1] // len(distances)
    scaled = []
    for k, distance in enumerate(distances):
        taken = jnp.dot(picked, r_all[:, k * cols : (k + 1) * cols], preferred_element_type=F32)
        square = square + jnp.sum(taken * taken, axis=1, keepdims=True)
        scaled.append((taken * gain[:, span(pos[1] ^ distance, cols)]).astype(BF16))
    return scaled, square


def first_hidden_kernel(n, slots, group, distances, pos, gain, pick, g_all, u_all, *refs):
    pieces = [refs[k * n : (k + 1) * n] for k in range(len(distances))]
    total_out, square_out, r_all, x_slots = refs[n * len(distances) :]
    experts, wide, hidden = g_all.shape
    place_rows(n, distances, pos, pieces, r_all)
    for i in range(experts // group):
        part = slice(i * group * slots, (i + 1) * group * slots)
        scaled, square = gather_rows(distances, pos, gain, pick[part, :], r_all, 0.0)
        for k, value in enumerate(scaled):
            x_slots[part, k * value.shape[1] : (k + 1) * value.shape[1]] = value
        square_out[part, :] = jnp.broadcast_to(square, (group * slots, square_out.shape[1]))
    for e in range(experts):
        mine = slice(e * slots, (e + 1) * slots)
        total_out[mine, :hidden] = jnp.dot(x_slots[mine, :], g_all[e], preferred_element_type=F32)
        total_out[mine, hidden:] = jnp.dot(x_slots[mine, :], u_all[e], preferred_element_type=F32)


def last_hidden_kernel(
    n, slots, group, distances, downs, pos, gain, pick, w_gate, w_up, w_down, g_some, u_some,
    total_in, square_in, weight, *refs,
):
    pieces = [refs[k * n : (k + 1) * n] for k in range(len(distances))]
    hidden_out, *refs = refs[n * len(distances) :]
    d_outs, (r_all, x_slots, g_all, u_all, sems, d_sems) = refs[: len(downs)], refs[len(downs) :]
    some, wide, hidden = g_some.shape
    ready, parts = some // group, (some + g_all.shape[0]) // group
    width = n * wide // len(distances)

    def copies(i):
        return weight_copies(
            pos, distances, i, group, (w_gate, w_up), (g_all, u_all), sems, first=some
        )

    def start(i, carry):
        for copy in copies(i):
            copy.start()
        return carry

    def d_copies(i):
        return down_copies(pos, downs, i, group, w_down, d_outs, d_sems)

    def start_down(i, carry):
        for copy in d_copies(i):
            copy.start()
        return carry

    def step(g_from, u_from, skipped, i, carry):
        part = span(i, group * slots)
        scaled, square = gather_rows(
            distances, pos, gain, pick[part, :], r_all, square_in[part, :1]
        )
        for k, value in enumerate(scaled):
            x_slots[:, k * value.shape[1] : (k + 1) * value.shape[1]] = value
        scale = lax.rsqrt(square / width + EPS)
        if skipped:
            for copy in copies(i - skipped):
                copy.wait()
        for e in range(group):
            inner = slice(e * slots, (e + 1) * slots)
            mine = pl.ds(pl.multiple_of(i * group * slots + e * slots, slots), slots)
            taken = x_slots[inner, :]
            gate_val = jnp.dot(taken, g_from[(i - skipped) * group + e], preferred_element_type=F32)
            up_val = jnp.dot(taken, u_from[(i - skipped) * group + e], preferred_element_type=F32)
            gate_val = (gate_val + total_in[mine, :hidden]) * scale[inner]
            up_val = (up_val + total_in[mine, hidden:]) * scale[inner]
            value = gate_val * jax.nn.sigmoid(gate_val) * (up_val * weight[mine, :1])
            hidden_out[mine, :] = value.astype(BF16)
        return carry

    lax.fori_loop(0, parts - ready, start, 0)
    lax.fori_loop(0, parts, start_down, 0)
    place_rows(n, distances, pos, pieces, r_all)
    lax.fori_loop(0, ready, functools.partial(step, g_some, u_some, 0), 0)
    lax.fori_loop(ready, parts, functools.partial(step, g_all, u_all, ready), 0)
    for i in range(parts):
        for copy in d_copies(i):
            copy.wait()


def self_down_kernel(slots, group, distances, pos, hidden, place, w_down, out, kept, y_slots, sems):
    copies = [
        down_copies(pos, distances, i, group, w_down, (kept,), sems)[0]
        for i in range(kept.shape[0] // group)
    ]
    for copy in copies:
        copy.start()

    def step(i, carry):
        down_copies(pos, distances, i, group, w_down, (kept,), sems)[0].wait()
        for e in range(group):
            mine = pl.ds(pl.multiple_of(i * group * slots + e * slots, slots), slots)
            product = jnp.dot(hidden[mine, :], kept[i * group + e], preferred_element_type=F32)
            y_slots[mine, :] = product.astype(BF16)
        return carry

    lax.fori_loop(0, len(copies), step, 0)
    out[...] = jnp.dot(place[...], y_slots[...], preferred_element_type=F32).astype(BF16)


def down_kernel(slots, pos, hidden, place, *refs):
    count = len(refs) // 2
    for kept, out in zip(refs[:count], refs[count:]):
        y_slots = refs[-1]
        for e in range(kept.shape[0]):
            mine = slice(e * slots, (e + 1) * slots)
            product = jnp.dot(hidden[mine, :], kept[e], preferred_element_type=F32)
            y_slots[mine, :] = product.astype(BF16)
        out[...] = jnp.dot(place[...], y_slots[...], preferred_element_type=F32).astype(BF16)


def add_kernel(distances, pos, base, part, *refs):
    cores, outs = refs[: len(distances)], refs[len(distances) :]
    rows = outs[0].shape[0]
    in_half = part.shape[0] // rows
    for d, core, out in zip(distances, cores, outs):
        block = pos[1] ^ d
        value = base[span(block, rows), :].astype(F32) + core[...].astype(F32)
        out[...] = (value + part[span(block % in_half, rows), :].astype(F32)).astype(out.dtype)


def down_blocks_kernel(slots, pos, hidden, place, kept, *refs):
    outs, (y_slots, whole) = refs[:-2], refs[-2:]
    rows = outs[0].shape[0]
    for e in range(kept.shape[0]):
        mine = slice(e * slots, (e + 1) * slots)
        product = jnp.dot(hidden[mine, :], kept[e], preferred_element_type=F32)
        y_slots[mine, :] = product.astype(BF16)
    whole[...] = jnp.dot(place[...], y_slots[...], preferred_element_type=F32).astype(BF16)
    for d, out in enumerate(outs):
        out[...] = whole[span(pos[1] ^ d, rows), :]


def cores_kernel(shares, pos, base, core, *outs):
    rows = outs[0].shape[0] // len(shares[0])
    for distances, out in zip(shares, outs):
        for d in distances:
            block = pos[1] ^ d
            inside = block % len(distances)
            value = base[span(block, rows), :].astype(F32) + core[span(block, rows), :].astype(F32)
            out[span(inside, rows), :] = value.astype(out.dtype)


def square_body(
    n, tokens, attn_weight, attn_gain, moe_gain, routes, gates, expert_gate, expert_up, expert_down
):
    g, s, h = (lax.axis_index(axis) for axis in ("grp", "seq", "head"))
    pos = jnp.stack([g, s, h]).astype(jnp.int32)
    rows, width = tokens.shape
    cols = width // n
    depth = attn_weight.shape[1]
    half = depth // 2
    experts, _, hidden = expert_gate.shape
    total = n * rows
    slots = -(-n * CAP // 16) * 16
    pairs = experts * slots
    sds = jax.ShapeDtypeStruct
    dma = pltpu.SemaphoreType.DMA

    def room(mib):
        return pltpu.CompilerParams(vmem_limit_bytes=mib * MIB)

    def cost(macs, size):
        return pl.CostEstimate(flops=2 * macs, bytes_accessed=size, transcendentals=0)

    def plus(*terms):
        total_value = terms[0].astype(F32)
        for term in terms[1:]:
            total_value = total_value + term.astype(F32)
        return total_value

    lines = 2 * TOPK
    with jax.named_scope("cut_pieces"):
        x_send, *w_sends = pl.pallas_call(
            cut_kernel,
            out_shape=[sds((rows + lines, cols), BF16)]
            + [sds((half, 3 * HEAD_DIM), BF16)] * (n - 1),
            in_specs=[SMEM] + [ANY] * 4,
            out_specs=[VMEM] * n,
            scratch_shapes=[
                pltpu.VMEM((TOPK, rows), jnp.int32),
                pltpu.VMEM((TOPK, rows), F32),
                dma((3 + 3 * (n - 1),)),
            ],
            compiler_params=room(8),
        )(pos, *map(held, (routes.T, gates.T, tokens, attn_weight)))
    group = experts // 4
    w_gate, w_up, w_down = map(held, (expert_gate, expert_up, expert_down))

    early, late = tuple(range(n // 2)), tuple(range(n // 2, n))
    wide = n // 2 * cols
    ahead = experts // 2
    hidden_cost = cost(pairs * wide * (total + 2 * hidden), 4 * experts * wide * hidden)

    def load(distances, amount, *earlier):
        return pl.pallas_call(
            functools.partial(load_kernel, group, distances),
            out_shape=[pltpu.VMEM((amount, wide, hidden), BF16)] * 2,
            in_specs=[SMEM] + [ANY] * 2,
            out_specs=[VMEM] * 2,
            scratch_shapes=[dma((amount // group, 2 * len(distances)))],
            compiler_params=room(2),
            cost_estimate=cost(0, 4 * amount * wide * hidden),
        )(after(pos, *earlier), w_gate, w_up)

    def load_down(distances, *earlier):
        count = len(distances)
        return pl.pallas_call(
            functools.partial(load_down_kernel, group, distances),
            out_shape=[pltpu.VMEM((experts, hidden, cols), BF16)] * count,
            in_specs=[SMEM, ANY],
            out_specs=[VMEM] * count,
            scratch_shapes=[dma((experts // group, count))],
            compiler_params=room(2),
            cost_estimate=cost(0, 2 * count * experts * cols * hidden),
        )(after(pos, *earlier), w_down)

    with jax.named_scope("gather_tokens_and_weights"):
        x_far = [swap(x_send, "seq", d) for d in range(1, n)]
        w_near = [swap(w_sends[d - 1], "seq", d) for d in range(1, n - 1)]
        step = in_step(*x_far, *w_near, w_sends[-1])
        x_far, w_near, w_last = step[: n - 1], list(step[n - 1 : -1]), step[-1]
        x_pieces = {0: jnp.stack([x[:rows] for x in x_far])}
        x_pieces[2] = swap(x_pieces[0], "head", 2)
        w_far = [swap(w, "grp", 1) for w in w_near]
        w_near.append(swap(w_last, "seq", n - 1))
        late_weights = list(load(late, ahead, w_near[0]))
        late_weights[0], x_pieces[2], w_near[-1], *w_far = in_step(
            late_weights[0], x_pieces[2], w_near[-1], *w_far
        )
        w_far.append(swap(w_near[-1], "grp", 1))
        for e in (0, 2):
            x_pieces[e ^ 1] = swap(x_pieces[e], "head", 1)
    with jax.named_scope("routing"):
        pick, place, weight = pl.pallas_call(
            functools.partial(route_kernel, n, experts, slots),
            out_shape=[sds((pairs, total), BF16), sds((total, pairs), BF16), sds((pairs, 128), F32)],
            in_specs=[SMEM] + [VMEM] * n,
            out_specs=[VMEM] * 3,
            scratch_shapes=[pltpu.VMEM((2 * TOPK, total), F32)],
            compiler_params=room(16),
        )(pos, x_send, *x_far)
    with jax.named_scope("gather_out_weights"):
        w_near[-1] = after(w_near[-1], pick)
        o_own = after(attn_weight, pick)[3]
        o_pieces = {0: o_own, 2: swap(o_own, "head", 2)}

    with jax.named_scope("projected_tokens"):
        partial, x_last, x_share = pl.pallas_call(
            functools.partial(project_tokens_kernel, n),
            out_shape=[
                sds((total, 3 * HEAD_DIM), F32),
                sds((total, half), BF16),
                sds((rows, cols), BF16),
            ],
            in_specs=[SMEM, VMEM] + [ANY] * (2 + n + 2 * (n - 1) - 1),
            out_specs=[VMEM] * 3,
            scratch_shapes=[
                pltpu.VMEM((total, width), BF16),
                pltpu.VMEM((width, 3 * HEAD_DIM), BF16),
                dma((1 + n * (n - 1),)),
                dma((3 + 2 * (n - 1) - 1,)),
            ],
            compiler_params=room(9),
            cost_estimate=cost(total * width * 3 * HEAD_DIM, 4 * total * width),
        )(
            pos, attn_gain.reshape(1, width), held(tokens), held(attn_weight),
            *[held(x_pieces[e]) for e in range(n)], *map(held, w_near), *map(held, w_far[:-1]),
        )
    with jax.named_scope("attention"):
        attended = pl.pallas_call(
            functools.partial(attend_kernel, n),
            out_shape=[sds((rows, HEAD_DIM), BF16)] * n,
            in_specs=[SMEM] + [VMEM] * 3,
            out_specs=[VMEM] * n,
            scratch_shapes=[pltpu.VMEM((total, 3 * HEAD_DIM), BF16)],
            compiler_params=room(6),
        )(pos, partial, x_last, w_far[-1])

    gain_row = moe_gain.reshape(1, width)

    def first_hidden(pieces, weights):
        return pl.pallas_call(
            functools.partial(first_hidden_kernel, n, slots, group, early),
            out_shape=[sds((pairs, 2 * hidden), F32), sds((pairs, 128), F32)],
            in_specs=[SMEM] + [VMEM] * (4 + n * len(early)),
            out_specs=[VMEM] * 2,
            scratch_shapes=[pltpu.VMEM((total, wide), BF16), pltpu.VMEM((pairs, wide), BF16)],
            compiler_params=room(12),
            cost_estimate=hidden_cost,
        )(pos, gain_row, pick, *map(here, weights), *pieces)

    def last_hidden(pieces, weights, state, downs):
        return pl.pallas_call(
            functools.partial(last_hidden_kernel, n, slots, group, late, downs),
            out_shape=[sds((pairs, hidden), BF16)]
            + [pltpu.VMEM((experts, hidden, cols), BF16)] * len(downs),
            in_specs=[SMEM] + [VMEM] * 2 + [ANY] * 3 + [VMEM] * (5 + n * len(late)),
            out_specs=[VMEM] * (1 + len(downs)),
            scratch_shapes=[pltpu.VMEM((total, wide), BF16), pltpu.VMEM((group * slots, wide), BF16)]
            + [pltpu.VMEM((experts - ahead, wide, hidden), BF16)] * 2
            + [dma(((experts - ahead) // group, 2 * len(late)))]
            + [dma((experts // group, len(downs)))],
            compiler_params=room(16),
            cost_estimate=hidden_cost,
        )(
            pos, gain_row, pick, w_gate, w_up, w_down, *map(here, weights), *state, weight, *pieces
        )

    with jax.named_scope("heads_to_tokens"):
        for e in (0, 2):
            o_pieces[e ^ 1] = swap(after(o_pieces[e], attended[0]), "head", 1)
        arrived = [attended[0]] + [swap(attended[e], "head", e) for e in range(1, n)]
        arrived = jnp.stack(arrived)
        a_pieces = [arrived, swap(arrived, "seq", 1), swap(arrived, "seq", 2)]
        with jax.named_scope("expert_weights"):
            early_weights = load(early, experts, arrived)
        a_pieces[2] = after(a_pieces[2], early_weights[0])
        a_pieces.append(swap(a_pieces[2], "seq", 1))
        with jax.named_scope("expert_weights"):
            (d_2,) = load_down((2,), a_pieces[2])
        x_share = after(x_share, d_2)

    with jax.named_scope("bring_out_weights"):
        o_here = pl.pallas_call(
            bring_kernel,
            out_shape=[pltpu.VMEM((depth, cols), BF16)] * n,
            in_specs=[ANY] * n,
            out_specs=[VMEM] * n,
            scratch_shapes=[dma((n,))],
            compiler_params=room(2),
            cost_estimate=cost(0, 2 * n * depth * cols),
        )(*[o_pieces[e] for e in range(n)])
    with jax.named_scope("output_projection"):
        residual = pl.pallas_call(
            functools.partial(project_kernel, n),
            out_shape=sds((rows, cols), BF16),
            in_specs=[SMEM] + [VMEM] * (1 + 2 * n),
            out_specs=VMEM,
            scratch_shapes=[pltpu.VMEM((n, rows, n * HEAD_DIM), BF16)],
            compiler_params=room(12),
        )(pos, x_share, *map(here, o_here), *a_pieces)

    with jax.named_scope("gather_residual"):
        r_pieces = {0: {0: residual}}
        for d in (1, 2):
            r_pieces[d] = {0: swap(residual, "seq", d)}
        r_pieces[3] = {0: swap(r_pieces[2][0], "seq", 1)}
        for d in range(n):
            r_pieces[d][2] = swap(r_pieces[d][0], "head", 2)
            r_pieces[d][1] = swap(r_pieces[d][0], "head", 1)
        for d in early:
            r_pieces[d][3] = swap(r_pieces[d][2], "head", 1)
        r_pieces[0][0] = after(residual, r_pieces[3][0])
        pieces = [r_pieces[d][e] for d in early for e in range(n)]
        with jax.named_scope("first_hidden_units"):
            state = first_hidden(pieces, early_weights)
        for d in late:
            r_pieces[d][3] = swap(after(r_pieces[d][2], state[1]), "head", 1)
        pieces = [r_pieces[d][e] for d in late for e in range(n)]
        with jax.named_scope("last_hidden_units"):
            units, d_3, d_1 = last_hidden(pieces, late_weights, state, (3, 1))
        r_choices = [r_pieces[d][d] for d in range(n)]
    def down(units, *weights):
        count = len(weights)
        with jax.named_scope("down_products"):
            return pl.pallas_call(
                functools.partial(down_kernel, slots),
                out_shape=[sds((total, cols), BF16)] * count,
                in_specs=[SMEM] + [VMEM] * (2 + count),
                out_specs=[VMEM] * count,
                scratch_shapes=[pltpu.VMEM((pairs, cols), BF16)],
                compiler_params=room(6),
                cost_estimate=cost(
                    count * pairs * cols * (total + hidden), 2 * count * experts * cols * hidden
                ),
            )(pos, units, place, *map(here, weights))

    def self_down(units, distance):
        with jax.named_scope("down_products_alone"):
            return pl.pallas_call(
                functools.partial(self_down_kernel, slots, group, (distance,)),
                out_shape=sds((total, cols), BF16),
                in_specs=[SMEM] + [VMEM] * 2 + [ANY],
                out_specs=VMEM,
                scratch_shapes=[
                    pltpu.VMEM((experts, hidden, cols), BF16),
                    pltpu.VMEM((pairs, cols), BF16),
                    dma((experts // group, 1)),
                ],
                compiler_params=room(9),
                cost_estimate=cost(0, 0),
            )(pos, units, place, w_down)

    with jax.named_scope("sum_over_devices"):
        (out_3,) = down(units, d_3)
        core_2 = swap(out_3, "head", 1)
        (out_2,) = down(after(units, out_3), d_2)
        halves = (tuple(range(n // 2, n)), tuple(range(n // 2)))
        with jax.named_scope("sums_over_cores"):
            near = pl.pallas_call(
                functools.partial(cores_kernel, halves),
                out_shape=[sds((len(d) * rows, cols), BF16) for d in halves],
                in_specs=[SMEM] + [VMEM] * 2,
                out_specs=[VMEM] * len(halves),
                compiler_params=room(4),
                cost_estimate=cost(0, 4 * total * cols),
            )(pos, out_2, core_2)
        far = [swap(part, "head", 2) for part in near]
        with jax.named_scope("down_products_by_block"):
            out_1 = pl.pallas_call(
                functools.partial(down_blocks_kernel, slots),
                out_shape=[pltpu.VMEM((rows, cols), BF16)] * n,
                in_specs=[SMEM] + [VMEM] * 3,
                out_specs=[VMEM] * n,
                scratch_shapes=[pltpu.VMEM((pairs, cols), BF16), pltpu.VMEM((total, cols), BF16)],
                compiler_params=room(6),
                cost_estimate=cost(SLOW, 2 * experts * cols * hidden),
            )(pos, after(units, *near), place, here(d_1))
        core_0 = [swap(part, "head", 1) for part in out_1]
        out_0 = self_down(after(units, out_1[0]), 0)

        def add_parts(distances, part, macs):
            with jax.named_scope("rows_" + "_".join(map(str, distances))):
                return pl.pallas_call(
                    functools.partial(add_kernel, distances),
                    out_shape=[sds((rows, cols), BF16 if d else F32) for d in distances],
                    in_specs=[SMEM] + [VMEM] * (2 + len(distances)),
                    out_specs=[VMEM] * len(distances),
                    compiler_params=room(4),
                    cost_estimate=cost(macs, 4 * part.size),
                )(pos, out_0, part, *[core_0[d] for d in distances])

        far_line, near_line = halves
        far_sums = add_parts(far_line, far[0], 0)
        from_far = [swap(part, "seq", d) for d, part in zip(far_line, far_sums)]
        own_sum, *near_sums = add_parts(near_line, far[1], SLOW)
        from_near = [swap(part, "seq", d) for d, part in zip(near_line[1:], near_sums)]
        mixed = plus(lax.select_n(s ^ h, *in_step(*r_choices, own_sum)[:n]), own_sum, *from_far)
        mixed = plus(*in_step(mixed, *from_near))
        mixed = mixed.astype(BF16)
    with jax.named_scope("gather_columns"):
        return lax.all_gather(mixed, "head", axis=1, tiled=True)


def solution(mesh):
    sizes = dict(mesh.shape)
    n = sizes["seq"]

    def body(tokens, attn_weight, *rest):
        width = tokens.shape[1]
        square = (
            n == sizes["head"]
            and n == 4
            and sizes["grp"] == 2
            and width == n * attn_weight.shape[1] == n * attn_weight.shape[2]
            and width == n * n * HEAD_DIM
            and n * tokens.shape[0] <= width // n
        )
        if square:
            return square_body(n, tokens, attn_weight, *rest)
        return general_body(tokens, attn_weight, *rest)

    return jax.shard_map(
        body,
        mesh=mesh,
        in_specs=(
            P(("grp", "seq"), None),
            P(None, "seq", "head"),
            P(),
            P(),
            P(("grp", "seq"), None),
            P(("grp", "seq"), None),
            P("seq", None, "head"),
            P("seq", None, "head"),
            P("seq", "head", None),
        ),
        out_specs=P(("grp", "seq"), None),
        check_vma=False,
    )
```

```python
import functools

import jax
import jax.numpy as jnp
from jax import lax
from jax.experimental import pallas as pl
from jax.experimental.pallas import tpu as pltpu
from jax.sharding import PartitionSpec as P

HEAD_DIM = 128
EXPERTS = 64
TOPK = 8
CAP = 18
EPS = 1e-06

PRECISE = lax.Precision.HIGHEST
BF16 = jnp.bfloat16
F32 = jnp.float32
ANY = pl.BlockSpec(memory_space=pl.ANY)
SMEM = pl.BlockSpec(memory_space=pltpu.SMEM)
VMEM = pl.BlockSpec(memory_space=pltpu.VMEM)
MIB = 1024 * 1024
SLOW = 10**10


def prefix_2(array, axis, combine, identity):
    peers, position = (lax.axis_size(axis), lax.axis_index(axis))
    everything = lax.all_gather(array.astype(jnp.bfloat16), axis)
    start = jnp.broadcast_to(jnp.asarray(identity, array.dtype), array.shape)

    def hop(k, before):
        reached = k < position
        new = combine(before, everything[k].astype(array.dtype))
        return jnp.where(reached, new, before)

    return lax.fori_loop(0, peers, hop, start)


def rms_scale(row_block, gain_vec):
    widened = row_block.astype(jnp.float32)
    factor = lax.rsqrt(jnp.mean(widened * widened, axis=-1, keepdims=True) + 1e-06)
    return widened * factor * gain_vec


def head_norm(outputs):
    return outputs * lax.rsqrt(jnp.mean(outputs * outputs, axis=-1, keepdims=True) + 1e-06)


def add_states(earlier, later):
    return earlier + later


def slot_numbers(route_flat):
    one_hot = (route_flat[:, None] == jnp.arange(EXPERTS, dtype=jnp.int32)[None, :]).astype(
        jnp.int32
    )
    earlier = jnp.cumsum(one_hot, axis=0) - one_hot
    return route_flat * CAP + jnp.sum(earlier * one_hot, axis=1)


def make_runner(expert_gate, expert_up, expert_down):

    def run_experts(received):
        gate_val = jnp.einsum(
            "necd,edf->necf", received, expert_gate, preferred_element_type=jnp.float32
        )
        up_val = jnp.einsum(
            "necd,edf->necf", received, expert_up, preferred_element_type=jnp.float32
        )
        hidden = (jax.nn.silu(gate_val) * up_val).astype(jnp.bfloat16)
        partial_value = jnp.einsum(
            "necf,efd->necd", hidden, expert_down, preferred_element_type=jnp.float32
        ).astype(jnp.bfloat16)
        groups = lax.axis_size("head")
        shape_now = partial_value.shape
        split = partial_value.reshape(
            shape_now[0], shape_now[1], shape_now[2], groups, shape_now[3] // groups
        )
        by_group = lax.all_to_all(split, "head", split_axis=3, concat_axis=3, tiled=True)
        summed = jnp.sum(by_group.astype(jnp.float32), axis=3)
        return lax.all_to_all(
            summed.astype(jnp.bfloat16), "seq", split_axis=0, concat_axis=0, tiled=True
        ).astype(summed.dtype)

    return run_experts


def general_body(
    tokens, attn_weight, attn_gain, moe_gain, routes, gates, expert_gate, expert_up, expert_down
):
    local_rows = tokens.shape[0]
    normed = rms_scale(tokens, attn_gain).astype(jnp.bfloat16)
    weights = lax.all_gather(attn_weight, "seq", axis=1, tiled=True)
    head_count = weights.shape[2] // HEAD_DIM
    projected = [
        jnp.dot(normed, weights[which], preferred_element_type=jnp.float32)
        .astype(jnp.bfloat16)
        .reshape(local_rows, head_count, HEAD_DIM)
        for which in range(3)
    ]
    query_rows, key_rows, value_rows = projected
    own_state = jnp.einsum("thd,the->hde", key_rows, value_rows, preferred_element_type=jnp.float32)
    prefix = prefix_2(own_state, "seq", add_states, jnp.zeros_like(own_state))
    inter_part = jnp.einsum(
        "thd,hde->the", query_rows.astype(jnp.float32), prefix, precision=PRECISE
    )
    scores = jnp.einsum("thd,shd->hts", query_rows, key_rows, preferred_element_type=jnp.float32)
    lower_mask = jnp.arange(local_rows)[:, None] >= jnp.arange(local_rows)[None, :]
    scores = jnp.where(lower_mask[None], scores, 0.0)
    intra_part = jnp.einsum(
        "hts,she->the", scores, value_rows.astype(jnp.float32), precision=PRECISE
    )
    attended = (
        head_norm(inter_part + intra_part)
        .reshape(local_rows, head_count * HEAD_DIM)
        .astype(jnp.bfloat16)
    )
    out_part = lax.dot_general(
        attended, weights[3], (((1,), (1,)), ((), ())), preferred_element_type=jnp.float32
    )
    residual = (
        tokens.astype(jnp.float32)
        + lax.psum(out_part.astype(jnp.bfloat16), "head").astype(jnp.float32)
    ).astype(jnp.bfloat16)
    moe_in = rms_scale(residual, moe_gain).astype(jnp.bfloat16)
    route_flat = routes.reshape(-1)
    slots = slot_numbers(route_flat)
    owners = lax.axis_size("seq")
    local_experts = expert_gate.shape[0]
    source_row = jnp.arange(route_flat.shape[0], dtype=jnp.int32) // TOPK
    run_experts = make_runner(expert_gate, expert_up, expert_down)
    outbound = (
        jnp.zeros((EXPERTS * CAP, moe_in.shape[1]), jnp.bfloat16).at[slots].set(moe_in[source_row])
    )
    outbound = outbound.reshape(owners, local_experts, CAP, moe_in.shape[1])
    returned = run_experts(lax.all_to_all(outbound, "seq", split_axis=0, concat_axis=0, tiled=True))
    arrived = returned.reshape(EXPERTS * CAP, -1)[slots].reshape(local_rows, TOPK, -1)
    moe_partial = jnp.einsum("tkd,tk->td", arrived, gates, precision=PRECISE)
    column_span = moe_partial.shape[1]
    residual_share = lax.dynamic_slice_in_dim(
        residual, lax.axis_index("head") * column_span, column_span, 1
    )
    mixed_share = (residual_share.astype(jnp.float32) + moe_partial).astype(jnp.bfloat16)
    return lax.all_gather(mixed_share, "head", axis=1, tiled=True)


def swap(array, axis, distance):
    size = lax.axis_size(axis)
    return lax.ppermute(array, axis, [(i, i ^ distance) for i in range(size)])


def run_copies(copies):
    for copy in copies:
        copy.start()
    for copy in copies:
        copy.wait()


def after(array, *earlier):
    return lax.optimization_barrier((array,) + earlier)[0]


def held(array):
    return pltpu.with_memory_space_constraint(array, pltpu.HBM)


def here(array):
    return pltpu.with_memory_space_constraint(array, pltpu.VMEM)


def in_step(*arrays):
    return lax.optimization_barrier(arrays)


def cut_kernel(pos, routes, gates, tokens, weight, x_send, *rest):
    w_sends, (r_here, g_here, sems) = rest[:-3], rest[-3:]
    g, s, h = pos[0], pos[1], pos[2]
    rows, cols, half = tokens.shape[0], x_send.shape[1], w_sends[0].shape[0]
    copies = [
        (
            tokens.at[:, pl.ds(pl.multiple_of(h * cols, cols), cols)],
            x_send.at[pl.ds(0, rows)],
        ),
        (routes, r_here),
        (gates, g_here),
    ]
    for which in range(3):
        span = pl.ds(which * HEAD_DIM, HEAD_DIM)
        for distance, out in enumerate(w_sends, 1):
            column = pl.multiple_of((s ^ distance) * HEAD_DIM, HEAD_DIM)
            own_half = pl.ds(pl.multiple_of(g * half, half), half)
            copies.append(
                (weight.at[which, own_half, pl.ds(column, HEAD_DIM)], out.at[:, span])
            )
    copies = [pltpu.make_async_copy(a, b, sems.at[i]) for i, (a, b) in enumerate(copies)]
    for copy in copies:
        copy.start()
    for copy in copies[1:3]:
        copy.wait()
    parts, left = [r_here[...].astype(F32)], g_here[...]
    for _ in range(3):
        parts.append(left.astype(BF16).astype(F32))
        left = left - parts[-1]
    lines = jnp.concatenate(parts, axis=1)
    lines = jnp.concatenate([lines, jnp.zeros_like(lines)], axis=0)
    blank = jnp.zeros((lines.shape[0], cols - lines.shape[1]), F32)
    if blank.shape[1]:
        lines = jnp.concatenate([lines, blank], axis=1)
    x_send[rows:, :] = lines.astype(BF16)
    for copy in copies[:1] + copies[3:]:
        copy.wait()


def project_tokens_kernel(n, pos, gain, tokens, weight, *rest):
    x_pieces, w_near, w_far = rest[:n], rest[n : 2 * n - 1], rest[2 * n - 1 : 3 * n - 3]
    partial, x_last, x_share, x_all, w_all, x_sems, w_sems = rest[3 * n - 3 :]
    g, s, h = pos[0], pos[1], pos[2]
    rows, width = tokens.shape
    cols = width // n
    depth, half = weight.shape[1], w_near[0].shape[0]
    missing = (s ^ (n - 1)) * 2 + (1 - g)
    x_copies = [(tokens, x_all.at[span(s, rows)])]
    for d in range(1, n):
        for e in range(n):
            target = x_all.at[span(s ^ d, rows), span(h ^ e, cols)]
            x_copies.append((x_pieces[e].at[d - 1], target))
    w_copies = []
    for which in range(3):
        target = w_all.at[span(s, depth), pl.ds(which * HEAD_DIM, HEAD_DIM)]
        w_copies.append((weight.at[which, :, span(s, HEAD_DIM)], target))
    for d in range(1, n):
        w_copies.append((w_near[d - 1], w_all.at[span((s ^ d) * 2 + g, half)]))
        if d < n - 1:
            w_copies.append((w_far[d - 1], w_all.at[span((s ^ d) * 2 + (1 - g), half)]))
    x_copies = [
        pltpu.make_async_copy(a, b, x_sems.at[i]) for i, (a, b) in enumerate(x_copies)
    ]
    w_copies = [
        pltpu.make_async_copy(a, b, w_sems.at[i]) for i, (a, b) in enumerate(w_copies)
    ]
    for copy in x_copies + w_copies:
        copy.start()
    w_all[span(missing, half), :] = jnp.zeros((half, w_all.shape[1]), BF16)
    for copy in x_copies:
        copy.wait()
    x_share[...] = x_all[span(h, rows), span(s, cols)]

    def normalise(block, carry):
        mine = span(block, rows)
        wide = x_all[mine, :].astype(F32)
        factor = lax.rsqrt(jnp.mean(wide * wide, axis=-1, keepdims=True) + EPS)
        x_all[mine, :] = (wide * factor * gain[...]).astype(BF16)
        return carry

    lax.fori_loop(0, n, normalise, 0)
    x_last[...] = x_all[:, span(missing, half)]
    for copy in w_copies:
        copy.wait()
    partial[...] = jnp.dot(x_all[...], w_all[...], preferred_element_type=F32)


def attend_kernel(n, pos, partial, x_last, w_last, *rest):
    attended, projected = rest[:n], rest[n]
    h = pos[2]
    rows = x_last.shape[0] // n
    projected[...] = (
        partial[...] + jnp.dot(x_last[...], w_last[...], preferred_element_type=F32)
    ).astype(BF16)
    key, value = projected[:, HEAD_DIM : 2 * HEAD_DIM], projected[:, 2 * HEAD_DIM :]
    for e in range(n):
        block = h ^ e
        scores = lax.dot_general(
            projected[span(block, rows), :HEAD_DIM],
            key,
            (((1,), (1,)), ((), ())),
            preferred_element_type=F32,
        )
        position = lax.broadcasted_iota(jnp.int32, scores.shape, 0) + block * rows
        scores = jnp.where(
            position >= lax.broadcasted_iota(jnp.int32, scores.shape, 1), scores, 0.0
        )
        high = scores.astype(BF16)
        low = (scores - high.astype(F32)).astype(BF16)
        out = jnp.dot(high, value, preferred_element_type=F32) + jnp.dot(
            low, value, preferred_element_type=F32
        )
        out = out * lax.rsqrt(jnp.mean(out * out, axis=-1, keepdims=True) + EPS)
        attended[e][...] = out.astype(BF16)


def bring_kernel(*refs):
    count = len(refs) // 2
    sems = refs[-1]
    copies = [pltpu.make_async_copy(refs[i], refs[count + i], sems.at[i]) for i in range(count)]
    for copy in copies:
        copy.start()
    for copy in copies:
        copy.wait()


def project_kernel(n, pos, x_share, *rest):
    weights, pieces, (out, a_all) = rest[:n], rest[n : 2 * n], rest[2 * n :]
    s = pos[1]
    total = x_share[...].astype(F32)
    for e in range(n):
        for d in range(n):
            span = pl.ds(pl.multiple_of((s ^ d) * HEAD_DIM, HEAD_DIM), HEAD_DIM)
            a_all[e, :, span] = pieces[d][e]
        total = total + lax.dot_general(
            a_all[e], weights[e][...], (((1,), (1,)), ((), ())), preferred_element_type=F32
        )
    out[...] = total.astype(BF16)


def route_kernel(n, experts, slots, pos, *refs):
    pieces, (pick, place, weight, table) = refs[:n], refs[n:]
    s = pos[1]
    rows = pieces[0].shape[0] - 2 * TOPK
    total = n * rows
    for d in range(n):
        lines = pieces[d][rows:, :].astype(F32)[:TOPK]
        gate = sum(lines[:, (1 + i) * rows : (2 + i) * rows] for i in range(3))
        span = pl.ds(pl.multiple_of((s ^ d) * rows, rows), rows)
        table[:, span] = jnp.concatenate([lines[:, :rows], gate], axis=0)
    first = (s * experts).astype(F32)
    names = lax.broadcasted_iota(jnp.int32, (experts, total), 0).astype(F32) + first
    member = jnp.zeros((experts, total), F32)
    gate = jnp.zeros((experts, total), F32)
    for k in range(TOPK):
        hit = table[k : k + 1, :] == names
        member = jnp.where(hit, 1.0, member)
        gate = jnp.where(hit, table[TOPK + k : TOPK + k + 1, :], gate)
    earlier = (
        lax.broadcasted_iota(jnp.int32, (total, total), 0)
        < lax.broadcasted_iota(jnp.int32, (total, total), 1)
    ).astype(F32).astype(BF16)
    rank = jnp.dot(member.astype(BF16), earlier, preferred_element_type=F32)
    slot = jnp.where(member > 0.0, rank, -1.0).astype(BF16)
    pairs = experts * slots
    expand = (
        lax.broadcasted_iota(jnp.int32, (experts, pairs), 1) // slots
        == lax.broadcasted_iota(jnp.int32, (experts, pairs), 0)
    ).astype(F32).astype(BF16)
    across = lax.dot_general(
        slot, expand, (((0,), (0,)), ((), ())), preferred_element_type=F32
    )
    number = (lax.broadcasted_iota(jnp.int32, (total, pairs), 1) % slots).astype(F32)
    place[...] = jnp.where(across == number, 1.0, 0.0).astype(BF16)
    for e in range(experts):
        span = pl.ds(e * slots, slots)
        number = lax.broadcasted_iota(jnp.int32, (slots, total), 0).astype(F32)
        hit = number == slot[e : e + 1, :].astype(F32)
        pick[span, :] = jnp.where(hit, 1.0, 0.0).astype(BF16)
        chosen = jnp.sum(jnp.where(hit, gate[e : e + 1, :], 0.0), axis=1, keepdims=True)
        weight[span, :] = jnp.broadcast_to(chosen, (slots, weight.shape[1]))


def span(block, size):
    return pl.ds(pl.multiple_of(block * size, size), size)


def weight_copies(pos, distances, i, group, ins, outs, sems, first=0):
    source_part, part = pl.ds(first + i * group, group), pl.ds(i * group, group)
    cols = outs[0].shape[1] // len(distances)
    copies = []
    for k, distance in enumerate(distances):
        for which, (w, kept) in enumerate(zip(ins, outs)):
            source = w.at[source_part, span(pos[1] ^ distance, cols), :]
            target = kept.at[part, pl.ds(k * cols, cols), :]
            copies.append(pltpu.make_async_copy(source, target, sems.at[i, 2 * k + which]))
    return copies


def down_copies(pos, distances, i, group, w_down, outs, sems):
    part, cols = pl.ds(i * group, group), outs[0].shape[2]
    copies = []
    for k, (distance, kept) in enumerate(zip(distances, outs)):
        source = w_down.at[part, :, span(pos[2] ^ distance, cols)]
        copies.append(pltpu.make_async_copy(source, kept.at[part], sems.at[i, k]))
    return copies


def load_down_kernel(group, distances, pos, w_down, *refs):
    outs, sems = refs[:-1], refs[-1]
    copies = []
    for i in range(outs[0].shape[0] // group):
        copies += down_copies(pos, distances, i, group, w_down, outs, sems)
    for copy in copies:
        copy.start()
    for copy in copies:
        copy.wait()


def load_kernel(group, distances, pos, w_gate, w_up, g_all, u_all, sems):
    copies = []
    for i in range(g_all.shape[0] // group):
        copies += weight_copies(
            pos, distances, i, group, (w_gate, w_up), (g_all, u_all), sems
        )
    for copy in copies:
        copy.start()
    for copy in copies:
        copy.wait()


def place_rows(n, distances, pos, pieces, r_all):
    rows, cols = pieces[0][0].shape
    for k in range(len(distances)):
        for e in range(n):
            r_all[span(pos[2] ^ e, rows), k * cols : (k + 1) * cols] = pieces[k][e][...]


def gather_rows(distances, pos, gain, picked, r_all, square):
    cols = r_all.shape[1] // len(distances)
    scaled = []
    for k, distance in enumerate(distances):
        taken = jnp.dot(picked, r_all[:, k * cols : (k + 1) * cols], preferred_element_type=F32)
        square = square + jnp.sum(taken * taken, axis=1, keepdims=True)
        scaled.append((taken * gain[:, span(pos[1] ^ distance, cols)]).astype(BF16))
    return scaled, square


def first_hidden_kernel(n, slots, group, distances, pos, gain, pick, g_all, u_all, *refs):
    pieces = [refs[k * n : (k + 1) * n] for k in range(len(distances))]
    total_out, square_out, r_all, x_slots = refs[n * len(distances) :]
    experts, wide, hidden = g_all.shape
    place_rows(n, distances, pos, pieces, r_all)
    for i in range(experts // group):
        part = slice(i * group * slots, (i + 1) * group * slots)
        scaled, square = gather_rows(distances, pos, gain, pick[part, :], r_all, 0.0)
        for k, value in enumerate(scaled):
            x_slots[part, k * value.shape[1] : (k + 1) * value.shape[1]] = value
        square_out[part, :] = jnp.broadcast_to(square, (group * slots, square_out.shape[1]))
    for e in range(experts):
        mine = slice(e * slots, (e + 1) * slots)
        total_out[mine, :hidden] = jnp.dot(x_slots[mine, :], g_all[e], preferred_element_type=F32)
        total_out[mine, hidden:] = jnp.dot(x_slots[mine, :], u_all[e], preferred_element_type=F32)


def last_hidden_kernel(
    n, slots, group, distances, downs, pos, gain, pick, w_gate, w_up, w_down, g_some, u_some,
    total_in, square_in, weight, place, *refs,
):
    pieces = [refs[k * n : (k + 1) * n] for k in range(len(distances))]
    hidden_out, out, d_next, r_all, x_slots, g_all, u_all, d_here, y_slots, sems, d_sems = refs[
        n * len(distances) :
    ]
    d_outs = (d_here, d_next)
    some, wide, hidden = g_some.shape
    ready, parts = some // group, (some + g_all.shape[0]) // group
    width = n * wide // len(distances)

    def copies(i):
        return weight_copies(
            pos, distances, i, group, (w_gate, w_up), (g_all, u_all), sems, first=some
        )

    def start(i, carry):
        for copy in copies(i):
            copy.start()
        return carry

    def d_copies(i):
        return down_copies(pos, downs, i, group, w_down, d_outs, d_sems)

    def start_down(i, carry):
        for copy in d_copies(i):
            copy.start()
        return carry

    def step(g_from, u_from, skipped, i, carry):
        part = span(i, group * slots)
        scaled, square = gather_rows(
            distances, pos, gain, pick[part, :], r_all, square_in[part, :1]
        )
        for k, value in enumerate(scaled):
            x_slots[:, k * value.shape[1] : (k + 1) * value.shape[1]] = value
        scale = lax.rsqrt(square / width + EPS)
        if skipped:
            for copy in copies(i - skipped):
                copy.wait()
        for e in range(group):
            inner = slice(e * slots, (e + 1) * slots)
            mine = pl.ds(pl.multiple_of(i * group * slots + e * slots, slots), slots)
            taken = x_slots[inner, :]
            gate_val = jnp.dot(taken, g_from[(i - skipped) * group + e], preferred_element_type=F32)
            up_val = jnp.dot(taken, u_from[(i - skipped) * group + e], preferred_element_type=F32)
            gate_val = (gate_val + total_in[mine, :hidden]) * scale[inner]
            up_val = (up_val + total_in[mine, hidden:]) * scale[inner]
            value = gate_val * jax.nn.sigmoid(gate_val) * (up_val * weight[mine, :1])
            hidden_out[mine, :] = value.astype(BF16)
        return carry

    lax.fori_loop(0, parts - ready, start, 0)
    lax.fori_loop(0, parts, start_down, 0)
    place_rows(n, distances, pos, pieces, r_all)
    lax.fori_loop(0, ready, functools.partial(step, g_some, u_some, 0), 0)
    lax.fori_loop(ready, parts, functools.partial(step, g_all, u_all, ready), 0)
    for i in range(parts):
        for copy in d_copies(i):
            copy.wait()
    for e in range(d_here.shape[0]):
        mine = slice(e * slots, (e + 1) * slots)
        product = jnp.dot(hidden_out[mine, :], d_here[e], preferred_element_type=F32)
        y_slots[mine, :] = product.astype(BF16)
    out[...] = jnp.dot(place[...], y_slots[...], preferred_element_type=F32).astype(BF16)


def self_down_kernel(slots, group, distances, pos, hidden, place, w_down, out, kept, y_slots, sems):
    copies = [
        down_copies(pos, distances, i, group, w_down, (kept,), sems)[0]
        for i in range(kept.shape[0] // group)
    ]
    for copy in copies:
        copy.start()

    def step(i, carry):
        down_copies(pos, distances, i, group, w_down, (kept,), sems)[0].wait()
        for e in range(group):
            mine = pl.ds(pl.multiple_of(i * group * slots + e * slots, slots), slots)
            product = jnp.dot(hidden[mine, :], kept[i * group + e], preferred_element_type=F32)
            y_slots[mine, :] = product.astype(BF16)
        return carry

    lax.fori_loop(0, len(copies), step, 0)
    out[...] = jnp.dot(place[...], y_slots[...], preferred_element_type=F32).astype(BF16)


def down_kernel(slots, pos, hidden, place, *refs):
    count = len(refs) // 2
    for kept, out in zip(refs[:count], refs[count:]):
        y_slots = refs[-1]
        for e in range(kept.shape[0]):
            mine = slice(e * slots, (e + 1) * slots)
            product = jnp.dot(hidden[mine, :], kept[e], preferred_element_type=F32)
            y_slots[mine, :] = product.astype(BF16)
        out[...] = jnp.dot(place[...], y_slots[...], preferred_element_type=F32).astype(BF16)


def add_kernel(distances, pos, base, part, *refs):
    cores, outs = refs[: len(distances)], refs[len(distances) :]
    rows = outs[0].shape[0]
    in_half = part.shape[0] // rows
    for d, core, out in zip(distances, cores, outs):
        block = pos[1] ^ d
        value = base[span(block, rows), :].astype(F32) + core[...].astype(F32)
        out[...] = (value + part[span(block % in_half, rows), :].astype(F32)).astype(out.dtype)


def down_blocks_kernel(slots, pos, hidden, place, kept, *refs):
    outs, (y_slots, whole) = refs[:-2], refs[-2:]
    rows = outs[0].shape[0]
    for e in range(kept.shape[0]):
        mine = slice(e * slots, (e + 1) * slots)
        product = jnp.dot(hidden[mine, :], kept[e], preferred_element_type=F32)
        y_slots[mine, :] = product.astype(BF16)
    whole[...] = jnp.dot(place[...], y_slots[...], preferred_element_type=F32).astype(BF16)
    for d, out in enumerate(outs):
        out[...] = whole[span(pos[1] ^ d, rows), :]


def cores_kernel(shares, pos, base, core, *outs):
    rows = outs[0].shape[0] // len(shares[0])
    for distances, out in zip(shares, outs):
        for d in distances:
            block = pos[1] ^ d
            inside = block % len(distances)
            value = base[span(block, rows), :].astype(F32) + core[span(block, rows), :].astype(F32)
            out[span(inside, rows), :] = value.astype(out.dtype)


def square_body(
    n, tokens, attn_weight, attn_gain, moe_gain, routes, gates, expert_gate, expert_up, expert_down
):
    g, s, h = (lax.axis_index(axis) for axis in ("grp", "seq", "head"))
    pos = jnp.stack([g, s, h]).astype(jnp.int32)
    rows, width = tokens.shape
    cols = width // n
    depth = attn_weight.shape[1]
    half = depth // 2
    experts, _, hidden = expert_gate.shape
    total = n * rows
    slots = -(-n * CAP // 16) * 16
    pairs = experts * slots
    sds = jax.ShapeDtypeStruct
    dma = pltpu.SemaphoreType.DMA

    def room(mib):
        return pltpu.CompilerParams(vmem_limit_bytes=mib * MIB)

    def cost(macs, size):
        return pl.CostEstimate(flops=2 * macs, bytes_accessed=size, transcendentals=0)

    def plus(*terms):
        total_value = terms[0].astype(F32)
        for term in terms[1:]:
            total_value = total_value + term.astype(F32)
        return total_value

    lines = 2 * TOPK
    with jax.named_scope("cut_pieces"):
        x_send, *w_sends = pl.pallas_call(
            cut_kernel,
            out_shape=[sds((rows + lines, cols), BF16)]
            + [sds((half, 3 * HEAD_DIM), BF16)] * (n - 1),
            in_specs=[SMEM] + [ANY] * 4,
            out_specs=[VMEM] * n,
            scratch_shapes=[
                pltpu.VMEM((TOPK, rows), jnp.int32),
                pltpu.VMEM((TOPK, rows), F32),
                dma((3 + 3 * (n - 1),)),
            ],
            compiler_params=room(8),
        )(pos, *map(held, (routes.T, gates.T, tokens, attn_weight)))
    group = experts // 4
    w_gate, w_up, w_down = map(held, (expert_gate, expert_up, expert_down))

    early, late = tuple(range(n // 2)), tuple(range(n // 2, n))
    wide = n // 2 * cols
    ahead = experts // 2
    hidden_cost = cost(pairs * wide * (total + 2 * hidden), 4 * experts * wide * hidden)

    def load(distances, amount, *earlier):
        return pl.pallas_call(
            functools.partial(load_kernel, group, distances),
            out_shape=[pltpu.VMEM((amount, wide, hidden), BF16)] * 2,
            in_specs=[SMEM] + [ANY] * 2,
            out_specs=[VMEM] * 2,
            scratch_shapes=[dma((amount // group, 2 * len(distances)))],
            compiler_params=room(2),
            cost_estimate=cost(0, 4 * amount * wide * hidden),
        )(after(pos, *earlier), w_gate, w_up)

    def load_down(distances, *earlier):
        count = len(distances)
        return pl.pallas_call(
            functools.partial(load_down_kernel, group, distances),
            out_shape=[pltpu.VMEM((experts, hidden, cols), BF16)] * count,
            in_specs=[SMEM, ANY],
            out_specs=[VMEM] * count,
            scratch_shapes=[dma((experts // group, count))],
            compiler_params=room(2),
            cost_estimate=cost(0, 2 * count * experts * cols * hidden),
        )(after(pos, *earlier), w_down)

    with jax.named_scope("gather_tokens_and_weights"):
        x_far = [swap(x_send, "seq", d) for d in range(1, n)]
        w_near = [swap(w_sends[d - 1], "seq", d) for d in range(1, n - 1)]
        step = in_step(*x_far, *w_near, w_sends[-1])
        x_far, w_near, w_last = step[: n - 1], list(step[n - 1 : -1]), step[-1]
        x_pieces = {0: jnp.stack([x[:rows] for x in x_far])}
        x_pieces[2] = swap(x_pieces[0], "head", 2)
        w_far = [swap(w, "grp", 1) for w in w_near]
        w_near.append(swap(w_last, "seq", n - 1))
        late_weights = list(load(late, ahead, w_near[0]))
        late_weights[0], x_pieces[2], w_near[-1], *w_far = in_step(
            late_weights[0], x_pieces[2], w_near[-1], *w_far
        )
        w_far.append(swap(w_near[-1], "grp", 1))
        for e in (0, 2):
            x_pieces[e ^ 1] = swap(x_pieces[e], "head", 1)
    with jax.named_scope("routing"):
        pick, place, weight = pl.pallas_call(
            functools.partial(route_kernel, n, experts, slots),
            out_shape=[sds((pairs, total), BF16), sds((total, pairs), BF16), sds((pairs, 128), F32)],
            in_specs=[SMEM] + [VMEM] * n,
            out_specs=[VMEM] * 3,
            scratch_shapes=[pltpu.VMEM((2 * TOPK, total), F32)],
            compiler_params=room(16),
        )(pos, x_send, *x_far)
    with jax.named_scope("gather_out_weights"):
        w_near[-1] = after(w_near[-1], pick)
        o_own = after(attn_weight, pick)[3]
        o_pieces = {0: o_own, 2: swap(o_own, "head", 2)}

    with jax.named_scope("projected_tokens"):
        partial, x_last, x_share = pl.pallas_call(
            functools.partial(project_tokens_kernel, n),
            out_shape=[
                sds((total, 3 * HEAD_DIM), F32),
                sds((total, half), BF16),
                sds((rows, cols), BF16),
            ],
            in_specs=[SMEM, VMEM] + [ANY] * (2 + n + 2 * (n - 1) - 1),
            out_specs=[VMEM] * 3,
            scratch_shapes=[
                pltpu.VMEM((total, width), BF16),
                pltpu.VMEM((width, 3 * HEAD_DIM), BF16),
                dma((1 + n * (n - 1),)),
                dma((3 + 2 * (n - 1) - 1,)),
            ],
            compiler_params=room(9),
            cost_estimate=cost(total * width * 3 * HEAD_DIM, 4 * total * width),
        )(
            pos, attn_gain.reshape(1, width), held(tokens), held(attn_weight),
            *[held(x_pieces[e]) for e in range(n)], *map(held, w_near), *map(held, w_far[:-1]),
        )
    with jax.named_scope("attention"):
        attended = pl.pallas_call(
            functools.partial(attend_kernel, n),
            out_shape=[sds((rows, HEAD_DIM), BF16)] * n,
            in_specs=[SMEM] + [VMEM] * 3,
            out_specs=[VMEM] * n,
            scratch_shapes=[pltpu.VMEM((total, 3 * HEAD_DIM), BF16)],
            compiler_params=room(6),
        )(pos, partial, x_last, w_far[-1])

    gain_row = moe_gain.reshape(1, width)

    def first_hidden(pieces, weights):
        return pl.pallas_call(
            functools.partial(first_hidden_kernel, n, slots, group, early),
            out_shape=[sds((pairs, 2 * hidden), F32), sds((pairs, 128), F32)],
            in_specs=[SMEM] + [VMEM] * (4 + n * len(early)),
            out_specs=[VMEM] * 2,
            scratch_shapes=[pltpu.VMEM((total, wide), BF16), pltpu.VMEM((pairs, wide), BF16)],
            compiler_params=room(12),
            cost_estimate=hidden_cost,
        )(pos, gain_row, pick, *map(here, weights), *pieces)

    def last_hidden(pieces, weights, state, downs):
        return pl.pallas_call(
            functools.partial(last_hidden_kernel, n, slots, group, late, downs),
            out_shape=[
                sds((pairs, hidden), BF16),
                sds((total, cols), BF16),
                pltpu.VMEM((experts, hidden, cols), BF16),
            ],
            in_specs=[SMEM] + [VMEM] * 2 + [ANY] * 3 + [VMEM] * (6 + n * len(late)),
            out_specs=[VMEM] * 3,
            scratch_shapes=[pltpu.VMEM((total, wide), BF16), pltpu.VMEM((group * slots, wide), BF16)]
            + [pltpu.VMEM((experts - ahead, wide, hidden), BF16)] * 2
            + [pltpu.VMEM((experts, hidden, cols), BF16), pltpu.VMEM((pairs, cols), BF16)]
            + [dma(((experts - ahead) // group, 2 * len(late)))]
            + [dma((experts // group, len(downs)))],
            compiler_params=room(21),
            cost_estimate=hidden_cost,
        )(
            pos, gain_row, pick, w_gate, w_up, w_down, *map(here, weights), *state,
            weight, place, *pieces,
        )

    with jax.named_scope("heads_to_tokens"):
        for e in (0, 2):
            o_pieces[e ^ 1] = swap(after(o_pieces[e], attended[0]), "head", 1)
        arrived = [attended[0]] + [swap(attended[e], "head", e) for e in range(1, n)]
        arrived = jnp.stack(arrived)
        a_pieces = [arrived, swap(arrived, "seq", 1), swap(arrived, "seq", 2)]
        with jax.named_scope("expert_weights"):
            early_weights = load(early, experts, arrived)
        a_pieces[2] = after(a_pieces[2], early_weights[0])
        a_pieces.append(swap(a_pieces[2], "seq", 1))
        with jax.named_scope("expert_weights"):
            (d_2,) = load_down((2,), a_pieces[2])
        x_share = after(x_share, d_2)

    with jax.named_scope("bring_out_weights"):
        o_here = pl.pallas_call(
            bring_kernel,
            out_shape=[pltpu.VMEM((depth, cols), BF16)] * n,
            in_specs=[ANY] * n,
            out_specs=[VMEM] * n,
            scratch_shapes=[dma((n,))],
            compiler_params=room(2),
            cost_estimate=cost(0, 2 * n * depth * cols),
        )(*[o_pieces[e] for e in range(n)])
    with jax.named_scope("output_projection"):
        residual = pl.pallas_call(
            functools.partial(project_kernel, n),
            out_shape=sds((rows, cols), BF16),
            in_specs=[SMEM] + [VMEM] * (1 + 2 * n),
            out_specs=VMEM,
            scratch_shapes=[pltpu.VMEM((n, rows, n * HEAD_DIM), BF16)],
            compiler_params=room(12),
        )(pos, x_share, *map(here, o_here), *a_pieces)

    with jax.named_scope("gather_residual"):
        r_pieces = {0: {0: residual}}
        for d in (1, 2):
            r_pieces[d] = {0: swap(residual, "seq", d)}
        r_pieces[3] = {0: swap(r_pieces[2][0], "seq", 1)}
        for d in range(n):
            r_pieces[d][2] = swap(r_pieces[d][0], "head", 2)
            r_pieces[d][1] = swap(r_pieces[d][0], "head", 1)
        for d in early:
            r_pieces[d][3] = swap(r_pieces[d][2], "head", 1)
        r_pieces[0][0] = after(residual, r_pieces[3][0])
        pieces = [r_pieces[d][e] for d in early for e in range(n)]
        with jax.named_scope("first_hidden_units"):
            state = first_hidden(pieces, early_weights)
        for d in late:
            r_pieces[d][3] = swap(after(r_pieces[d][2], state[1]), "head", 1)
        pieces = [r_pieces[d][e] for d in late for e in range(n)]
        with jax.named_scope("last_hidden_units"):
            units, out_3, d_1 = last_hidden(pieces, late_weights, state, (3, 1))
        r_choices = [r_pieces[d][d] for d in range(n)]
    def down(units, *weights):
        count = len(weights)
        with jax.named_scope("down_products"):
            return pl.pallas_call(
                functools.partial(down_kernel, slots),
                out_shape=[sds((total, cols), BF16)] * count,
                in_specs=[SMEM] + [VMEM] * (2 + count),
                out_specs=[VMEM] * count,
                scratch_shapes=[pltpu.VMEM((pairs, cols), BF16)],
                compiler_params=room(6),
                cost_estimate=cost(
                    count * pairs * cols * (total + hidden), 2 * count * experts * cols * hidden
                ),
            )(pos, units, place, *map(here, weights))

    def self_down(units, distance):
        with jax.named_scope("down_products_alone"):
            return pl.pallas_call(
                functools.partial(self_down_kernel, slots, group, (distance,)),
                out_shape=sds((total, cols), BF16),
                in_specs=[SMEM] + [VMEM] * 2 + [ANY],
                out_specs=VMEM,
                scratch_shapes=[
                    pltpu.VMEM((experts, hidden, cols), BF16),
                    pltpu.VMEM((pairs, cols), BF16),
                    dma((experts // group, 1)),
                ],
                compiler_params=room(9),
                cost_estimate=cost(0, 0),
            )(pos, units, place, w_down)

    with jax.named_scope("sum_over_devices"):
        core_2 = swap(out_3, "head", 1)
        (out_2,) = down(after(units, out_3), d_2)
        halves = (tuple(range(n // 2, n)), tuple(range(n // 2)))
        with jax.named_scope("sums_over_cores"):
            near = pl.pallas_call(
                functools.partial(cores_kernel, halves),
                out_shape=[sds((len(d) * rows, cols), BF16) for d in halves],
                in_specs=[SMEM] + [VMEM] * 2,
                out_specs=[VMEM] * len(halves),
                compiler_params=room(4),
                cost_estimate=cost(0, 4 * total * cols),
            )(pos, out_2, core_2)
        far = [swap(part, "head", 2) for part in near]
        with jax.named_scope("down_products_by_block"):
            out_1 = pl.pallas_call(
                functools.partial(down_blocks_kernel, slots),
                out_shape=[pltpu.VMEM((rows, cols), BF16)] * n,
                in_specs=[SMEM] + [VMEM] * 3,
                out_specs=[VMEM] * n,
                scratch_shapes=[pltpu.VMEM((pairs, cols), BF16), pltpu.VMEM((total, cols), BF16)],
                compiler_params=room(6),
                cost_estimate=cost(SLOW, 2 * experts * cols * hidden),
            )(pos, after(units, *near), place, here(d_1))
        core_0 = [swap(part, "head", 1) for part in out_1]
        out_0 = self_down(after(units, out_1[0]), 0)

        def add_parts(distances, part, macs):
            with jax.named_scope("rows_" + "_".join(map(str, distances))):
                return pl.pallas_call(
                    functools.partial(add_kernel, distances),
                    out_shape=[sds((rows, cols), BF16 if d else F32) for d in distances],
                    in_specs=[SMEM] + [VMEM] * (2 + len(distances)),
                    out_specs=[VMEM] * len(distances),
                    compiler_params=room(4),
                    cost_estimate=cost(macs, 4 * part.size),
                )(pos, out_0, part, *[core_0[d] for d in distances])

        far_line, near_line = halves
        far_sums = add_parts(far_line, far[0], 0)
        from_far = [swap(part, "seq", d) for d, part in zip(far_line, far_sums)]
        own_sum, *near_sums = add_parts(near_line, far[1], SLOW)
        from_near = [swap(part, "seq", d) for d, part in zip(near_line[1:], near_sums)]
        mixed = plus(lax.select_n(s ^ h, *in_step(*r_choices, own_sum)[:n]), own_sum, *from_far)
        mixed = plus(*in_step(mixed, *from_near))
        mixed = mixed.astype(BF16)
    with jax.named_scope("gather_columns"):
        return lax.all_gather(mixed, "head", axis=1, tiled=True)


def solution(mesh):
    sizes = dict(mesh.shape)
    n = sizes["seq"]

    def body(tokens, attn_weight, *rest):
        width = tokens.shape[1]
        square = (
            n == sizes["head"]
            and n == 4
            and sizes["grp"] == 2
            and width == n * attn_weight.shape[1] == n * attn_weight.shape[2]
            and width == n * n * HEAD_DIM
            and n * tokens.shape[0] <= width // n
        )
        if square:
            return square_body(n, tokens, attn_weight, *rest)
        return general_body(tokens, attn_weight, *rest)

    return jax.shard_map(
        body,
        mesh=mesh,
        in_specs=(
            P(("grp", "seq"), None),
            P(None, "seq", "head"),
            P(),
            P(),
            P(("grp", "seq"), None),
            P(("grp", "seq"), None),
            P("seq", None, "head"),
            P("seq", None, "head"),
            P("seq", "head", None),
        ),
        out_specs=P(("grp", "seq"), None),
        check_vma=False,
    )
```

```python
import functools

import jax
import jax.numpy as jnp
from jax import lax
from jax.experimental import pallas as pl
from jax.experimental.pallas import tpu as pltpu
from jax.sharding import PartitionSpec as P

HEAD_DIM = 128
EXPERTS = 64
TOPK = 8
CAP = 18
EPS = 1e-06

PRECISE = lax.Precision.HIGHEST
BF16 = jnp.bfloat16
F32 = jnp.float32
ANY = pl.BlockSpec(memory_space=pl.ANY)
SMEM = pl.BlockSpec(memory_space=pltpu.SMEM)
VMEM = pl.BlockSpec(memory_space=pltpu.VMEM)
MIB = 1024 * 1024
SLOW = 10**10


def prefix_2(array, axis, combine, identity):
    peers, position = (lax.axis_size(axis), lax.axis_index(axis))
    everything = lax.all_gather(array.astype(jnp.bfloat16), axis)
    start = jnp.broadcast_to(jnp.asarray(identity, array.dtype), array.shape)

    def hop(k, before):
        reached = k < position
        new = combine(before, everything[k].astype(array.dtype))
        return jnp.where(reached, new, before)

    return lax.fori_loop(0, peers, hop, start)


def rms_scale(row_block, gain_vec):
    widened = row_block.astype(jnp.float32)
    factor = lax.rsqrt(jnp.mean(widened * widened, axis=-1, keepdims=True) + 1e-06)
    return widened * factor * gain_vec


def head_norm(outputs):
    return outputs * lax.rsqrt(jnp.mean(outputs * outputs, axis=-1, keepdims=True) + 1e-06)


def add_states(earlier, later):
    return earlier + later


def slot_numbers(route_flat):
    one_hot = (route_flat[:, None] == jnp.arange(EXPERTS, dtype=jnp.int32)[None, :]).astype(
        jnp.int32
    )
    earlier = jnp.cumsum(one_hot, axis=0) - one_hot
    return route_flat * CAP + jnp.sum(earlier * one_hot, axis=1)


def make_runner(expert_gate, expert_up, expert_down):

    def run_experts(received):
        gate_val = jnp.einsum(
            "necd,edf->necf", received, expert_gate, preferred_element_type=jnp.float32
        )
        up_val = jnp.einsum(
            "necd,edf->necf", received, expert_up, preferred_element_type=jnp.float32
        )
        hidden = (jax.nn.silu(gate_val) * up_val).astype(jnp.bfloat16)
        partial_value = jnp.einsum(
            "necf,efd->necd", hidden, expert_down, preferred_element_type=jnp.float32
        ).astype(jnp.bfloat16)
        groups = lax.axis_size("head")
        shape_now = partial_value.shape
        split = partial_value.reshape(
            shape_now[0], shape_now[1], shape_now[2], groups, shape_now[3] // groups
        )
        by_group = lax.all_to_all(split, "head", split_axis=3, concat_axis=3, tiled=True)
        summed = jnp.sum(by_group.astype(jnp.float32), axis=3)
        return lax.all_to_all(
            summed.astype(jnp.bfloat16), "seq", split_axis=0, concat_axis=0, tiled=True
        ).astype(summed.dtype)

    return run_experts


def general_body(
    tokens, attn_weight, attn_gain, moe_gain, routes, gates, expert_gate, expert_up, expert_down
):
    local_rows = tokens.shape[0]
    normed = rms_scale(tokens, attn_gain).astype(jnp.bfloat16)
    weights = lax.all_gather(attn_weight, "seq", axis=1, tiled=True)
    head_count = weights.shape[2] // HEAD_DIM
    projected = [
        jnp.dot(normed, weights[which], preferred_element_type=jnp.float32)
        .astype(jnp.bfloat16)
        .reshape(local_rows, head_count, HEAD_DIM)
        for which in range(3)
    ]
    query_rows, key_rows, value_rows = projected
    own_state = jnp.einsum("thd,the->hde", key_rows, value_rows, preferred_element_type=jnp.float32)
    prefix = prefix_2(own_state, "seq", add_states, jnp.zeros_like(own_state))
    inter_part = jnp.einsum(
        "thd,hde->the", query_rows.astype(jnp.float32), prefix, precision=PRECISE
    )
    scores = jnp.einsum("thd,shd->hts", query_rows, key_rows, preferred_element_type=jnp.float32)
    lower_mask = jnp.arange(local_rows)[:, None] >= jnp.arange(local_rows)[None, :]
    scores = jnp.where(lower_mask[None], scores, 0.0)
    intra_part = jnp.einsum(
        "hts,she->the", scores, value_rows.astype(jnp.float32), precision=PRECISE
    )
    attended = (
        head_norm(inter_part + intra_part)
        .reshape(local_rows, head_count * HEAD_DIM)
        .astype(jnp.bfloat16)
    )
    out_part = lax.dot_general(
        attended, weights[3], (((1,), (1,)), ((), ())), preferred_element_type=jnp.float32
    )
    residual = (
        tokens.astype(jnp.float32)
        + lax.psum(out_part.astype(jnp.bfloat16), "head").astype(jnp.float32)
    ).astype(jnp.bfloat16)
    moe_in = rms_scale(residual, moe_gain).astype(jnp.bfloat16)
    route_flat = routes.reshape(-1)
    slots = slot_numbers(route_flat)
    owners = lax.axis_size("seq")
    local_experts = expert_gate.shape[0]
    source_row = jnp.arange(route_flat.shape[0], dtype=jnp.int32) // TOPK
    run_experts = make_runner(expert_gate, expert_up, expert_down)
    outbound = (
        jnp.zeros((EXPERTS * CAP, moe_in.shape[1]), jnp.bfloat16).at[slots].set(moe_in[source_row])
    )
    outbound = outbound.reshape(owners, local_experts, CAP, moe_in.shape[1])
    returned = run_experts(lax.all_to_all(outbound, "seq", split_axis=0, concat_axis=0, tiled=True))
    arrived = returned.reshape(EXPERTS * CAP, -1)[slots].reshape(local_rows, TOPK, -1)
    moe_partial = jnp.einsum("tkd,tk->td", arrived, gates, precision=PRECISE)
    column_span = moe_partial.shape[1]
    residual_share = lax.dynamic_slice_in_dim(
        residual, lax.axis_index("head") * column_span, column_span, 1
    )
    mixed_share = (residual_share.astype(jnp.float32) + moe_partial).astype(jnp.bfloat16)
    return lax.all_gather(mixed_share, "head", axis=1, tiled=True)


def swap(array, axis, distance):
    size = lax.axis_size(axis)
    return lax.ppermute(array, axis, [(i, i ^ distance) for i in range(size)])


def run_copies(copies):
    for copy in copies:
        copy.start()
    for copy in copies:
        copy.wait()


def after(array, *earlier):
    return lax.optimization_barrier((array,) + earlier)[0]


def held(array):
    return pltpu.with_memory_space_constraint(array, pltpu.HBM)


def here(array):
    return pltpu.with_memory_space_constraint(array, pltpu.VMEM)


def in_step(*arrays):
    return lax.optimization_barrier(arrays)


def cut_kernel(pos, routes, gates, tokens, weight, x_send, *rest):
    w_sends, (r_here, g_here, sems) = rest[:-3], rest[-3:]
    g, s, h = pos[0], pos[1], pos[2]
    rows, cols, half = tokens.shape[0], x_send.shape[1], w_sends[0].shape[0]
    copies = [
        (
            tokens.at[:, pl.ds(pl.multiple_of(h * cols, cols), cols)],
            x_send.at[pl.ds(0, rows)],
        ),
        (routes, r_here),
        (gates, g_here),
    ]
    for which in range(3):
        span = pl.ds(which * HEAD_DIM, HEAD_DIM)
        for distance, out in enumerate(w_sends, 1):
            column = pl.multiple_of((s ^ distance) * HEAD_DIM, HEAD_DIM)
            own_half = pl.ds(pl.multiple_of(g * half, half), half)
            copies.append(
                (weight.at[which, own_half, pl.ds(column, HEAD_DIM)], out.at[:, span])
            )
    copies = [pltpu.make_async_copy(a, b, sems.at[i]) for i, (a, b) in enumerate(copies)]
    for copy in copies:
        copy.start()
    for copy in copies[1:3]:
        copy.wait()
    parts, left = [r_here[...].astype(F32)], g_here[...]
    for _ in range(3):
        parts.append(left.astype(BF16).astype(F32))
        left = left - parts[-1]
    lines = jnp.concatenate(parts, axis=1)
    lines = jnp.concatenate([lines, jnp.zeros_like(lines)], axis=0)
    blank = jnp.zeros((lines.shape[0], cols - lines.shape[1]), F32)
    if blank.shape[1]:
        lines = jnp.concatenate([lines, blank], axis=1)
    x_send[rows:, :] = lines.astype(BF16)
    for copy in copies[:1] + copies[3:]:
        copy.wait()


def project_tokens_kernel(n, pos, gain, tokens, weight, *rest):
    x_pieces, w_near, w_far = rest[:n], rest[n : 2 * n - 1], rest[2 * n - 1 : 3 * n - 3]
    partial, x_last, x_share, x_all, w_all, x_sems, w_sems = rest[3 * n - 3 :]
    g, s, h = pos[0], pos[1], pos[2]
    rows, width = tokens.shape
    cols = width // n
    depth, half = weight.shape[1], w_near[0].shape[0]
    missing = (s ^ (n - 1)) * 2 + (1 - g)
    x_copies = [(tokens, x_all.at[span(s, rows)])]
    for d in range(1, n):
        for e in range(n):
            target = x_all.at[span(s ^ d, rows), span(h ^ e, cols)]
            x_copies.append((x_pieces[e].at[d - 1], target))
    w_copies = []
    for which in range(3):
        target = w_all.at[span(s, depth), pl.ds(which * HEAD_DIM, HEAD_DIM)]
        w_copies.append((weight.at[which, :, span(s, HEAD_DIM)], target))
    for d in range(1, n):
        w_copies.append((w_near[d - 1], w_all.at[span((s ^ d) * 2 + g, half)]))
        if d < n - 1:
            w_copies.append((w_far[d - 1], w_all.at[span((s ^ d) * 2 + (1 - g), half)]))
    x_copies = [
        pltpu.make_async_copy(a, b, x_sems.at[i]) for i, (a, b) in enumerate(x_copies)
    ]
    w_copies = [
        pltpu.make_async_copy(a, b, w_sems.at[i]) for i, (a, b) in enumerate(w_copies)
    ]
    for copy in x_copies + w_copies:
        copy.start()
    w_all[span(missing, half), :] = jnp.zeros((half, w_all.shape[1]), BF16)
    for copy in x_copies:
        copy.wait()
    x_share[...] = x_all[span(h, rows), span(s, cols)]

    def normalise(block, carry):
        mine = span(block, rows)
        wide = x_all[mine, :].astype(F32)
        factor = lax.rsqrt(jnp.mean(wide * wide, axis=-1, keepdims=True) + EPS)
        x_all[mine, :] = (wide * factor * gain[...]).astype(BF16)
        return carry

    lax.fori_loop(0, n, normalise, 0)
    x_last[...] = x_all[:, span(missing, half)]
    for copy in w_copies:
        copy.wait()
    partial[...] = jnp.dot(x_all[...], w_all[...], preferred_element_type=F32)


def attend_kernel(n, pos, partial, x_last, w_last, *rest):
    attended, projected = rest[:n], rest[n]
    h = pos[2]
    rows = x_last.shape[0] // n
    projected[...] = (
        partial[...] + jnp.dot(x_last[...], w_last[...], preferred_element_type=F32)
    ).astype(BF16)
    key, value = projected[:, HEAD_DIM : 2 * HEAD_DIM], projected[:, 2 * HEAD_DIM :]
    for e in range(n):
        block = h ^ e
        scores = lax.dot_general(
            projected[span(block, rows), :HEAD_DIM],
            key,
            (((1,), (1,)), ((), ())),
            preferred_element_type=F32,
        )
        position = lax.broadcasted_iota(jnp.int32, scores.shape, 0) + block * rows
        scores = jnp.where(
            position >= lax.broadcasted_iota(jnp.int32, scores.shape, 1), scores, 0.0
        )
        high = scores.astype(BF16)
        low = (scores - high.astype(F32)).astype(BF16)
        out = jnp.dot(high, value, preferred_element_type=F32) + jnp.dot(
            low, value, preferred_element_type=F32
        )
        out = out * lax.rsqrt(jnp.mean(out * out, axis=-1, keepdims=True) + EPS)
        attended[e][...] = out.astype(BF16)


def bring_kernel(*refs):
    count = len(refs) // 2
    sems = refs[-1]
    copies = [pltpu.make_async_copy(refs[i], refs[count + i], sems.at[i]) for i in range(count)]
    for copy in copies:
        copy.start()
    for copy in copies:
        copy.wait()


def project_kernel(n, pos, x_share, *rest):
    weights, pieces, (out, a_all) = rest[:n], rest[n : 2 * n], rest[2 * n :]
    s = pos[1]
    total = x_share[...].astype(F32)
    for e in range(n):
        for d in range(n):
            span = pl.ds(pl.multiple_of((s ^ d) * HEAD_DIM, HEAD_DIM), HEAD_DIM)
            a_all[e, :, span] = pieces[d][e]
        total = total + lax.dot_general(
            a_all[e], weights[e][...], (((1,), (1,)), ((), ())), preferred_element_type=F32
        )
    out[...] = total.astype(BF16)


def route_kernel(n, experts, slots, pos, *refs):
    pieces, (pick, place, weight, table) = refs[:n], refs[n:]
    s = pos[1]
    rows = pieces[0].shape[0] - 2 * TOPK
    total = n * rows
    for d in range(n):
        lines = pieces[d][rows:, :].astype(F32)[:TOPK]
        gate = sum(lines[:, (1 + i) * rows : (2 + i) * rows] for i in range(3))
        span = pl.ds(pl.multiple_of((s ^ d) * rows, rows), rows)
        table[:, span] = jnp.concatenate([lines[:, :rows], gate], axis=0)
    first = (s * experts).astype(F32)
    names = lax.broadcasted_iota(jnp.int32, (experts, total), 0).astype(F32) + first
    member = jnp.zeros((experts, total), F32)
    gate = jnp.zeros((experts, total), F32)
    for k in range(TOPK):
        hit = table[k : k + 1, :] == names
        member = jnp.where(hit, 1.0, member)
        gate = jnp.where(hit, table[TOPK + k : TOPK + k + 1, :], gate)
    earlier = (
        lax.broadcasted_iota(jnp.int32, (total, total), 0)
        < lax.broadcasted_iota(jnp.int32, (total, total), 1)
    ).astype(F32).astype(BF16)
    rank = jnp.dot(member.astype(BF16), earlier, preferred_element_type=F32)
    slot = jnp.where(member > 0.0, rank, -1.0).astype(BF16)
    pairs = experts * slots
    expand = (
        lax.broadcasted_iota(jnp.int32, (experts, pairs), 1) // slots
        == lax.broadcasted_iota(jnp.int32, (experts, pairs), 0)
    ).astype(F32).astype(BF16)
    across = lax.dot_general(
        slot, expand, (((0,), (0,)), ((), ())), preferred_element_type=F32
    )
    number = (lax.broadcasted_iota(jnp.int32, (total, pairs), 1) % slots).astype(F32)
    place[...] = jnp.where(across == number, 1.0, 0.0).astype(BF16)
    for e in range(experts):
        span = pl.ds(e * slots, slots)
        number = lax.broadcasted_iota(jnp.int32, (slots, total), 0).astype(F32)
        hit = number == slot[e : e + 1, :].astype(F32)
        pick[span, :] = jnp.where(hit, 1.0, 0.0).astype(BF16)
        chosen = jnp.sum(jnp.where(hit, gate[e : e + 1, :], 0.0), axis=1, keepdims=True)
        weight[span, :] = jnp.broadcast_to(chosen, (slots, weight.shape[1]))


def span(block, size):
    return pl.ds(pl.multiple_of(block * size, size), size)


def weight_copies(pos, distances, i, group, ins, outs, sems, first=0):
    source_part, part = pl.ds(first + i * group, group), pl.ds(i * group, group)
    cols = outs[0].shape[1] // len(distances)
    copies = []
    for k, distance in enumerate(distances):
        for which, (w, kept) in enumerate(zip(ins, outs)):
            source = w.at[source_part, span(pos[1] ^ distance, cols), :]
            target = kept.at[part, pl.ds(k * cols, cols), :]
            copies.append(pltpu.make_async_copy(source, target, sems.at[i, 2 * k + which]))
    return copies


def down_copies(pos, distances, i, group, w_down, outs, sems):
    part, cols = pl.ds(i * group, group), outs[0].shape[2]
    copies = []
    for k, (distance, kept) in enumerate(zip(distances, outs)):
        source = w_down.at[part, :, span(pos[2] ^ distance, cols)]
        copies.append(pltpu.make_async_copy(source, kept.at[part], sems.at[i, k]))
    return copies


def load_down_kernel(group, distances, pos, w_down, *refs):
    outs, sems = refs[:-1], refs[-1]
    copies = []
    for i in range(outs[0].shape[0] // group):
        copies += down_copies(pos, distances, i, group, w_down, outs, sems)
    for copy in copies:
        copy.start()
    for copy in copies:
        copy.wait()


def load_kernel(group, distances, pos, w_gate, w_up, g_all, u_all, sems):
    copies = []
    for i in range(g_all.shape[0] // group):
        copies += weight_copies(
            pos, distances, i, group, (w_gate, w_up), (g_all, u_all), sems
        )
    for copy in copies:
        copy.start()
    for copy in copies:
        copy.wait()


def place_rows(n, distances, pos, pieces, r_all):
    rows, cols = pieces[0][0].shape
    for k in range(len(distances)):
        for e in range(n):
            r_all[span(pos[2] ^ e, rows), k * cols : (k + 1) * cols] = pieces[k][e][...]


def gather_rows(distances, pos, gain, picked, r_all, square):
    cols = r_all.shape[1] // len(distances)
    scaled = []
    for k, distance in enumerate(distances):
        taken = jnp.dot(picked, r_all[:, k * cols : (k + 1) * cols], preferred_element_type=F32)
        square = square + jnp.sum(taken * taken, axis=1, keepdims=True)
        scaled.append((taken * gain[:, span(pos[1] ^ distance, cols)]).astype(BF16))
    return scaled, square


def first_hidden_kernel(n, slots, group, distances, pos, gain, pick, g_all, u_all, *refs):
    pieces = [refs[k * n : (k + 1) * n] for k in range(len(distances))]
    total_out, square_out, r_all, x_slots = refs[n * len(distances) :]
    experts, wide, hidden = g_all.shape
    place_rows(n, distances, pos, pieces, r_all)
    for i in range(experts // group):
        part = slice(i * group * slots, (i + 1) * group * slots)
        scaled, square = gather_rows(distances, pos, gain, pick[part, :], r_all, 0.0)
        for k, value in enumerate(scaled):
            x_slots[part, k * value.shape[1] : (k + 1) * value.shape[1]] = value
        square_out[part, :] = jnp.broadcast_to(square, (group * slots, square_out.shape[1]))
    for e in range(experts):
        mine = slice(e * slots, (e + 1) * slots)
        total_out[mine, :hidden] = jnp.dot(x_slots[mine, :], g_all[e], preferred_element_type=F32)
        total_out[mine, hidden:] = jnp.dot(x_slots[mine, :], u_all[e], preferred_element_type=F32)


def last_hidden_kernel(
    n, slots, group, distances, downs, pos, gain, pick, w_gate, w_up, w_down, g_some, u_some,
    total_in, square_in, weight, place, *refs,
):
    pieces = [refs[k * n : (k + 1) * n] for k in range(len(distances))]
    hidden_out, out, d_next, r_all, x_slots, g_all, u_all, d_here, y_slots, sems, d_sems = refs[
        n * len(distances) :
    ]
    d_outs = (d_here, d_next)
    some, wide, hidden = g_some.shape
    ready, parts = some // group, (some + g_all.shape[0]) // group
    width = n * wide // len(distances)

    def copies(i):
        return weight_copies(
            pos, distances, i, group, (w_gate, w_up), (g_all, u_all), sems, first=some
        )

    def start(i, carry):
        for copy in copies(i):
            copy.start()
        return carry

    def d_copy(k, i):
        return down_copies(pos, downs, i, group, w_down, d_outs, d_sems)[k]

    def start_down(k, i, carry):
        d_copy(k, i).start()
        return carry

    def step(g_from, u_from, skipped, i, carry):
        part = span(i, group * slots)
        scaled, square = gather_rows(
            distances, pos, gain, pick[part, :], r_all, square_in[part, :1]
        )
        for k, value in enumerate(scaled):
            x_slots[:, k * value.shape[1] : (k + 1) * value.shape[1]] = value
        scale = lax.rsqrt(square / width + EPS)
        if skipped:
            for copy in copies(i - skipped):
                copy.wait()
        for e in range(group):
            inner = slice(e * slots, (e + 1) * slots)
            mine = pl.ds(pl.multiple_of(i * group * slots + e * slots, slots), slots)
            taken = x_slots[inner, :]
            gate_val = jnp.dot(taken, g_from[(i - skipped) * group + e], preferred_element_type=F32)
            up_val = jnp.dot(taken, u_from[(i - skipped) * group + e], preferred_element_type=F32)
            gate_val = (gate_val + total_in[mine, :hidden]) * scale[inner]
            up_val = (up_val + total_in[mine, hidden:]) * scale[inner]
            value = gate_val * jax.nn.sigmoid(gate_val) * (up_val * weight[mine, :1])
            hidden_out[mine, :] = value.astype(BF16)
        return carry

    lax.fori_loop(0, parts - ready, start, 0)
    for k in range(len(downs)):
        lax.fori_loop(0, parts, functools.partial(start_down, k), 0)
    place_rows(n, distances, pos, pieces, r_all)
    lax.fori_loop(0, ready, functools.partial(step, g_some, u_some, 0), 0)
    lax.fori_loop(ready, parts, functools.partial(step, g_all, u_all, ready), 0)
    for i in range(parts):
        d_copy(0, i).wait()
    for e in range(d_here.shape[0]):
        mine = slice(e * slots, (e + 1) * slots)
        product = jnp.dot(hidden_out[mine, :], d_here[e], preferred_element_type=F32)
        y_slots[mine, :] = product.astype(BF16)
    out[...] = jnp.dot(place[...], y_slots[...], preferred_element_type=F32).astype(BF16)
    for i in range(parts):
        d_copy(1, i).wait()


def self_down_kernel(slots, group, distances, pos, hidden, place, w_down, out, kept, y_slots, sems):
    copies = [
        down_copies(pos, distances, i, group, w_down, (kept,), sems)[0]
        for i in range(kept.shape[0] // group)
    ]
    for copy in copies:
        copy.start()

    def step(i, carry):
        down_copies(pos, distances, i, group, w_down, (kept,), sems)[0].wait()
        for e in range(group):
            mine = pl.ds(pl.multiple_of(i * group * slots + e * slots, slots), slots)
            product = jnp.dot(hidden[mine, :], kept[i * group + e], preferred_element_type=F32)
            y_slots[mine, :] = product.astype(BF16)
        return carry

    lax.fori_loop(0, len(copies), step, 0)
    out[...] = jnp.dot(place[...], y_slots[...], preferred_element_type=F32).astype(BF16)


def down_kernel(slots, pos, hidden, place, *refs):
    count = len(refs) // 2
    for kept, out in zip(refs[:count], refs[count:]):
        y_slots = refs[-1]
        for e in range(kept.shape[0]):
            mine = slice(e * slots, (e + 1) * slots)
            product = jnp.dot(hidden[mine, :], kept[e], preferred_element_type=F32)
            y_slots[mine, :] = product.astype(BF16)
        out[...] = jnp.dot(place[...], y_slots[...], preferred_element_type=F32).astype(BF16)


def add_kernel(distances, pos, base, part, *refs):
    cores, outs = refs[: len(distances)], refs[len(distances) :]
    rows = outs[0].shape[0]
    in_half = part.shape[0] // rows
    for d, core, out in zip(distances, cores, outs):
        block = pos[1] ^ d
        value = base[span(block, rows), :].astype(F32) + core[...].astype(F32)
        out[...] = (value + part[span(block % in_half, rows), :].astype(F32)).astype(out.dtype)


def down_blocks_kernel(slots, pos, hidden, place, kept, *refs):
    outs, (y_slots, whole) = refs[:-2], refs[-2:]
    rows = outs[0].shape[0]
    for e in range(kept.shape[0]):
        mine = slice(e * slots, (e + 1) * slots)
        product = jnp.dot(hidden[mine, :], kept[e], preferred_element_type=F32)
        y_slots[mine, :] = product.astype(BF16)
    whole[...] = jnp.dot(place[...], y_slots[...], preferred_element_type=F32).astype(BF16)
    for d, out in enumerate(outs):
        out[...] = whole[span(pos[1] ^ d, rows), :]


def cores_kernel(shares, pos, base, core, *outs):
    rows = outs[0].shape[0] // len(shares[0])
    for distances, out in zip(shares, outs):
        for d in distances:
            block = pos[1] ^ d
            inside = block % len(distances)
            value = base[span(block, rows), :].astype(F32) + core[span(block, rows), :].astype(F32)
            out[span(inside, rows), :] = value.astype(out.dtype)


def square_body(
    n, tokens, attn_weight, attn_gain, moe_gain, routes, gates, expert_gate, expert_up, expert_down
):
    g, s, h = (lax.axis_index(axis) for axis in ("grp", "seq", "head"))
    pos = jnp.stack([g, s, h]).astype(jnp.int32)
    rows, width = tokens.shape
    cols = width // n
    depth = attn_weight.shape[1]
    half = depth // 2
    experts, _, hidden = expert_gate.shape
    total = n * rows
    slots = -(-n * CAP // 16) * 16
    pairs = experts * slots
    sds = jax.ShapeDtypeStruct
    dma = pltpu.SemaphoreType.DMA

    def room(mib):
        return pltpu.CompilerParams(vmem_limit_bytes=mib * MIB)

    def cost(macs, size):
        return pl.CostEstimate(flops=2 * macs, bytes_accessed=size, transcendentals=0)

    def plus(*terms):
        total_value = terms[0].astype(F32)
        for term in terms[1:]:
            total_value = total_value + term.astype(F32)
        return total_value

    lines = 2 * TOPK
    with jax.named_scope("cut_pieces"):
        x_send, *w_sends = pl.pallas_call(
            cut_kernel,
            out_shape=[sds((rows + lines, cols), BF16)]
            + [sds((half, 3 * HEAD_DIM), BF16)] * (n - 1),
            in_specs=[SMEM] + [ANY] * 4,
            out_specs=[VMEM] * n,
            scratch_shapes=[
                pltpu.VMEM((TOPK, rows), jnp.int32),
                pltpu.VMEM((TOPK, rows), F32),
                dma((3 + 3 * (n - 1),)),
            ],
            compiler_params=room(8),
        )(pos, *map(held, (routes.T, gates.T, tokens, attn_weight)))
    group = experts // 4
    w_gate, w_up, w_down = map(held, (expert_gate, expert_up, expert_down))

    early, late = tuple(range(n // 2)), tuple(range(n // 2, n))
    wide = n // 2 * cols
    ahead = experts // 2
    hidden_cost = cost(pairs * wide * (total + 2 * hidden), 4 * experts * wide * hidden)

    def load(distances, amount, *earlier):
        return pl.pallas_call(
            functools.partial(load_kernel, group, distances),
            out_shape=[pltpu.VMEM((amount, wide, hidden), BF16)] * 2,
            in_specs=[SMEM] + [ANY] * 2,
            out_specs=[VMEM] * 2,
            scratch_shapes=[dma((amount // group, 2 * len(distances)))],
            compiler_params=room(2),
            cost_estimate=cost(0, 4 * amount * wide * hidden),
        )(after(pos, *earlier), w_gate, w_up)

    def load_down(distances, *earlier):
        count = len(distances)
        return pl.pallas_call(
            functools.partial(load_down_kernel, group, distances),
            out_shape=[pltpu.VMEM((experts, hidden, cols), BF16)] * count,
            in_specs=[SMEM, ANY],
            out_specs=[VMEM] * count,
            scratch_shapes=[dma((experts // group, count))],
            compiler_params=room(2),
            cost_estimate=cost(0, 2 * count * experts * cols * hidden),
        )(after(pos, *earlier), w_down)

    with jax.named_scope("gather_tokens_and_weights"):
        x_far = [swap(x_send, "seq", d) for d in range(1, n)]
        w_near = [swap(w_sends[d - 1], "seq", d) for d in range(1, n - 1)]
        step = in_step(*x_far, *w_near, w_sends[-1])
        x_far, w_near, w_last = step[: n - 1], list(step[n - 1 : -1]), step[-1]
        x_pieces = {0: jnp.stack([x[:rows] for x in x_far])}
        x_pieces[2] = swap(x_pieces[0], "head", 2)
        w_far = [swap(w, "grp", 1) for w in w_near]
        w_near.append(swap(w_last, "seq", n - 1))
        late_weights = list(load(late, ahead, w_near[0]))
        late_weights[0], x_pieces[2], w_near[-1], *w_far = in_step(
            late_weights[0], x_pieces[2], w_near[-1], *w_far
        )
        w_far.append(swap(w_near[-1], "grp", 1))
        for e in (0, 2):
            x_pieces[e ^ 1] = swap(x_pieces[e], "head", 1)
    with jax.named_scope("routing"):
        pick, place, weight = pl.pallas_call(
            functools.partial(route_kernel, n, experts, slots),
            out_shape=[sds((pairs, total), BF16), sds((total, pairs), BF16), sds((pairs, 128), F32)],
            in_specs=[SMEM] + [VMEM] * n,
            out_specs=[VMEM] * 3,
            scratch_shapes=[pltpu.VMEM((2 * TOPK, total), F32)],
            compiler_params=room(16),
        )(pos, x_send, *x_far)
    with jax.named_scope("gather_out_weights"):
        w_near[-1] = after(w_near[-1], pick)
        o_own = after(attn_weight, pick)[3]
        o_pieces = {0: o_own, 2: swap(o_own, "head", 2)}

    with jax.named_scope("projected_tokens"):
        partial, x_last, x_share = pl.pallas_call(
            functools.partial(project_tokens_kernel, n),
            out_shape=[
                sds((total, 3 * HEAD_DIM), F32),
                sds((total, half), BF16),
                sds((rows, cols), BF16),
            ],
            in_specs=[SMEM, VMEM] + [ANY] * (2 + n + 2 * (n - 1) - 1),
            out_specs=[VMEM] * 3,
            scratch_shapes=[
                pltpu.VMEM((total, width), BF16),
                pltpu.VMEM((width, 3 * HEAD_DIM), BF16),
                dma((1 + n * (n - 1),)),
                dma((3 + 2 * (n - 1) - 1,)),
            ],
            compiler_params=room(9),
            cost_estimate=cost(total * width * 3 * HEAD_DIM, 4 * total * width),
        )(
            pos, attn_gain.reshape(1, width), held(tokens), held(attn_weight),
            *[held(x_pieces[e]) for e in range(n)], *map(held, w_near), *map(held, w_far[:-1]),
        )
    with jax.named_scope("attention"):
        attended = pl.pallas_call(
            functools.partial(attend_kernel, n),
            out_shape=[sds((rows, HEAD_DIM), BF16)] * n,
            in_specs=[SMEM] + [VMEM] * 3,
            out_specs=[VMEM] * n,
            scratch_shapes=[pltpu.VMEM((total, 3 * HEAD_DIM), BF16)],
            compiler_params=room(6),
        )(pos, partial, x_last, w_far[-1])

    gain_row = moe_gain.reshape(1, width)

    def first_hidden(pieces, weights):
        return pl.pallas_call(
            functools.partial(first_hidden_kernel, n, slots, group, early),
            out_shape=[sds((pairs, 2 * hidden), F32), sds((pairs, 128), F32)],
            in_specs=[SMEM] + [VMEM] * (4 + n * len(early)),
            out_specs=[VMEM] * 2,
            scratch_shapes=[pltpu.VMEM((total, wide), BF16), pltpu.VMEM((pairs, wide), BF16)],
            compiler_params=room(12),
            cost_estimate=hidden_cost,
        )(pos, gain_row, pick, *map(here, weights), *pieces)

    def last_hidden(pieces, weights, state, downs):
        return pl.pallas_call(
            functools.partial(last_hidden_kernel, n, slots, group, late, downs),
            out_shape=[
                sds((pairs, hidden), BF16),
                sds((total, cols), BF16),
                pltpu.VMEM((experts, hidden, cols), BF16),
            ],
            in_specs=[SMEM] + [VMEM] * 2 + [ANY] * 3 + [VMEM] * (6 + n * len(late)),
            out_specs=[VMEM] * 3,
            scratch_shapes=[pltpu.VMEM((total, wide), BF16), pltpu.VMEM((group * slots, wide), BF16)]
            + [pltpu.VMEM((experts - ahead, wide, hidden), BF16)] * 2
            + [pltpu.VMEM((experts, hidden, cols), BF16), pltpu.VMEM((pairs, cols), BF16)]
            + [dma(((experts - ahead) // group, 2 * len(late)))]
            + [dma((experts // group, len(downs)))],
            compiler_params=room(21),
            cost_estimate=hidden_cost,
        )(
            pos, gain_row, pick, w_gate, w_up, w_down, *map(here, weights), *state,
            weight, place, *pieces,
        )

    with jax.named_scope("heads_to_tokens"):
        for e in (0, 2):
            o_pieces[e ^ 1] = swap(after(o_pieces[e], attended[0]), "head", 1)
        arrived = [attended[0]] + [swap(attended[e], "head", e) for e in range(1, n)]
        arrived = jnp.stack(arrived)
        a_pieces = [arrived, swap(arrived, "seq", 1), swap(arrived, "seq", 2)]
        with jax.named_scope("expert_weights"):
            early_weights = load(early, experts, arrived)
        a_pieces[2] = after(a_pieces[2], early_weights[0])
        a_pieces.append(swap(a_pieces[2], "seq", 1))
        with jax.named_scope("expert_weights"):
            (d_2,) = load_down((2,), a_pieces[2])
        x_share = after(x_share, d_2)

    with jax.named_scope("bring_out_weights"):
        o_here = pl.pallas_call(
            bring_kernel,
            out_shape=[pltpu.VMEM((depth, cols), BF16)] * n,
            in_specs=[ANY] * n,
            out_specs=[VMEM] * n,
            scratch_shapes=[dma((n,))],
            compiler_params=room(2),
            cost_estimate=cost(0, 2 * n * depth * cols),
        )(*[o_pieces[e] for e in range(n)])
    with jax.named_scope("output_projection"):
        residual = pl.pallas_call(
            functools.partial(project_kernel, n),
            out_shape=sds((rows, cols), BF16),
            in_specs=[SMEM] + [VMEM] * (1 + 2 * n),
            out_specs=VMEM,
            scratch_shapes=[pltpu.VMEM((n, rows, n * HEAD_DIM), BF16)],
            compiler_params=room(12),
        )(pos, x_share, *map(here, o_here), *a_pieces)

    with jax.named_scope("gather_residual"):
        r_pieces = {0: {0: residual}}
        for d in (1, 2):
            r_pieces[d] = {0: swap(residual, "seq", d)}
        r_pieces[3] = {0: swap(r_pieces[2][0], "seq", 1)}
        for d in range(n):
            r_pieces[d][2] = swap(r_pieces[d][0], "head", 2)
            r_pieces[d][1] = swap(r_pieces[d][0], "head", 1)
        for d in early:
            r_pieces[d][3] = swap(r_pieces[d][2], "head", 1)
        r_pieces[0][0] = after(residual, r_pieces[3][0])
        pieces = [r_pieces[d][e] for d in early for e in range(n)]
        with jax.named_scope("first_hidden_units"):
            state = first_hidden(pieces, early_weights)
        for d in late:
            r_pieces[d][3] = swap(after(r_pieces[d][2], state[1]), "head", 1)
        pieces = [r_pieces[d][e] for d in late for e in range(n)]
        with jax.named_scope("last_hidden_units"):
            units, out_3, d_1 = last_hidden(pieces, late_weights, state, (3, 1))
        r_choices = [r_pieces[d][d] for d in range(n)]
    def down(units, *weights):
        count = len(weights)
        with jax.named_scope("down_products"):
            return pl.pallas_call(
                functools.partial(down_kernel, slots),
                out_shape=[sds((total, cols), BF16)] * count,
                in_specs=[SMEM] + [VMEM] * (2 + count),
                out_specs=[VMEM] * count,
                scratch_shapes=[pltpu.VMEM((pairs, cols), BF16)],
                compiler_params=room(6),
                cost_estimate=cost(
                    count * pairs * cols * (total + hidden), 2 * count * experts * cols * hidden
                ),
            )(pos, units, place, *map(here, weights))

    def self_down(units, distance):
        with jax.named_scope("down_products_alone"):
            return pl.pallas_call(
                functools.partial(self_down_kernel, slots, group, (distance,)),
                out_shape=sds((total, cols), BF16),
                in_specs=[SMEM] + [VMEM] * 2 + [ANY],
                out_specs=VMEM,
                scratch_shapes=[
                    pltpu.VMEM((experts, hidden, cols), BF16),
                    pltpu.VMEM((pairs, cols), BF16),
                    dma((experts // group, 1)),
                ],
                compiler_params=room(9),
                cost_estimate=cost(0, 0),
            )(pos, units, place, w_down)

    with jax.named_scope("sum_over_devices"):
        core_2 = swap(out_3, "head", 1)
        (out_2,) = down(after(units, out_3), d_2)
        halves = (tuple(range(n // 2, n)), tuple(range(n // 2)))
        with jax.named_scope("sums_over_cores"):
            near = pl.pallas_call(
                functools.partial(cores_kernel, halves),
                out_shape=[sds((len(d) * rows, cols), BF16) for d in halves],
                in_specs=[SMEM] + [VMEM] * 2,
                out_specs=[VMEM] * len(halves),
                compiler_params=room(4),
                cost_estimate=cost(0, 4 * total * cols),
            )(pos, out_2, core_2)
        far = [swap(part, "head", 2) for part in near]
        with jax.named_scope("down_products_by_block"):
            out_1 = pl.pallas_call(
                functools.partial(down_blocks_kernel, slots),
                out_shape=[pltpu.VMEM((rows, cols), BF16)] * n,
                in_specs=[SMEM] + [VMEM] * 3,
                out_specs=[VMEM] * n,
                scratch_shapes=[pltpu.VMEM((pairs, cols), BF16), pltpu.VMEM((total, cols), BF16)],
                compiler_params=room(6),
                cost_estimate=cost(SLOW, 2 * experts * cols * hidden),
            )(pos, after(units, *near), place, here(d_1))
        core_0 = [swap(part, "head", 1) for part in out_1]
        out_0 = self_down(after(units, out_1[0]), 0)

        def add_parts(distances, part, macs):
            with jax.named_scope("rows_" + "_".join(map(str, distances))):
                return pl.pallas_call(
                    functools.partial(add_kernel, distances),
                    out_shape=[sds((rows, cols), BF16 if d else F32) for d in distances],
                    in_specs=[SMEM] + [VMEM] * (2 + len(distances)),
                    out_specs=[VMEM] * len(distances),
                    compiler_params=room(4),
                    cost_estimate=cost(macs, 4 * part.size),
                )(pos, out_0, part, *[core_0[d] for d in distances])

        far_line, near_line = halves
        far_sums = add_parts(far_line, far[0], 0)
        from_far = [swap(part, "seq", d) for d, part in zip(far_line, far_sums)]
        own_sum, *near_sums = add_parts(near_line, far[1], SLOW)
        from_near = [swap(part, "seq", d) for d, part in zip(near_line[1:], near_sums)]
        mixed = plus(lax.select_n(s ^ h, *in_step(*r_choices, own_sum)[:n]), own_sum, *from_far)
        mixed = plus(*in_step(mixed, *from_near))
        mixed = mixed.astype(BF16)
    with jax.named_scope("gather_columns"):
        return lax.all_gather(mixed, "head", axis=1, tiled=True)


def solution(mesh):
    sizes = dict(mesh.shape)
    n = sizes["seq"]

    def body(tokens, attn_weight, *rest):
        width = tokens.shape[1]
        square = (
            n == sizes["head"]
            and n == 4
            and sizes["grp"] == 2
            and width == n * attn_weight.shape[1] == n * attn_weight.shape[2]
            and width == n * n * HEAD_DIM
            and n * tokens.shape[0] <= width // n
        )
        if square:
            return square_body(n, tokens, attn_weight, *rest)
        return general_body(tokens, attn_weight, *rest)

    return jax.shard_map(
        body,
        mesh=mesh,
        in_specs=(
            P(("grp", "seq"), None),
            P(None, "seq", "head"),
            P(),
            P(),
            P(("grp", "seq"), None),
            P(("grp", "seq"), None),
            P("seq", None, "head"),
            P("seq", None, "head"),
            P("seq", "head", None),
        ),
        out_specs=P(("grp", "seq"), None),
        check_vma=False,
    )
```
